128 devices in a mesh: gx: 8 (over z, core), gy: 16 (over y, x).
Axes of the slice: x: 4, y: 4, z: 4, core: 2. Of those that a mesh axis runs over, the one named last changes fastest.
Arguments:
- fields: bfloat16 [2, 20, 256, 240, 128], P(None, None, 'gx', 'gy'), may hold values from -6 to 6
- cotangents: bfloat16 [2, 20, 256, 240, 128], P(None, None, 'gx', 'gy'), may hold values from -6 to 6
- w_point: bfloat16 [20, 20], replicated, may hold values from -1.25 to 1.25
- bias_vector: float32 [20], replicated, may hold values from -0.5 to 0.5
- spectral: float32 [2, 20, 20, 55296], P(None, None, None, ('gx', 'gy')), may hold values from -3 to 3
Outputs:
- activation: bfloat16 [20, 256, 240, 128], P(None, 'gx', 'gy')
- trained: float32 [2, 20, 20, 55296], P(None, None, None, ('gx', 'gy'))
The draws below stay inside these ranges and needn't reach their ends.
All inputs are finite; a program needn't handle non-finite values.
Results may differ from the reference program's by a relative error of at most 0.008.
Values may be sent and summed in bfloat16 or wider, within the bound.
A program may use at most 128 MiB of HBM per device.

```python
import math
import jax
import jax.numpy as jnp
from jax import lax

C = 20
NX = 256
NY = 240
NZ = 128
KX = 48
KY = 48
KZ = 24
STEPS = 2
MODES = 55296


def levels(rng, dims, cuts, least, largest):
    loudness = 1.0
    for dim, parts in cuts:
        steps = jax.random.uniform(jax.random.fold_in(jax.random.fold_in(rng, 6), dim), (parts,), jnp.float32, least / len(cuts), largest / len(cuts))
        loudness = loudness * jnp.repeat(jnp.exp(steps), dims[dim] // parts).reshape((-1,) + (1,) * (len(dims) - 1 - dim))
    return loudness


def centred(own_key, shape, width, bound, split=(), kind=jnp.bfloat16):
    drawn = width * jax.random.normal(own_key, shape, jnp.float32)
    if split:
        drawn = drawn * levels(own_key, shape, split, -0.22, 0.18)
    return jnp.clip(drawn, -bound, bound).astype(kind)


def setup_inputs(seed: int = 0) -> dict:
    key_list = jax.random.split(jax.random.key(seed), 6)
    return {
        "fields": centred(key_list[0], (STEPS, C, NX, NY, NZ), 1.0, 6.0, ((2, 8), (3, 16))),
        "cotangents": centred(key_list[1], (STEPS, C, NX, NY, NZ), 1.0, 6.0, ((2, 8), (3, 16))),
        "w_point": centred(key_list[2], (C, C), C ** -0.5, 1.25),
        "bias_vector": jnp.clip(jax.random.uniform(key_list[3], (C,), jnp.float32, -0.5, 0.5), -0.5, 0.5),
        "spectral": centred(key_list[4], (2, C, C, MODES), 0.5, 3.0, ((3, 128),), jnp.float32),
    }


learn_rate = 0.1

def angle_pair(positions, frequencies, length):
    product = positions[:, None] * frequencies[None, :] % length
    phase_angle = product.astype(jnp.float32) * (2.0 * math.pi / length)
    return (jnp.cos(phase_angle), jnp.sin(phase_angle))

def kept_waves(length, kept_count):
    wave_index = jnp.arange(kept_count, dtype=jnp.int32)
    return jnp.where(wave_index < kept_count // 2, wave_index, wave_index - kept_count + length)

def complex_table(positions, length, kept_count):
    cosine, sine_part = angle_pair(positions, kept_waves(length, kept_count), length)
    upper_rows = jnp.stack([cosine, -sine_part], axis=1)
    lower_rows = jnp.stack([sine_part, cosine], axis=1)
    return jnp.stack([upper_rows, lower_rows], axis=1)

def make_tables():
    cosine, sine_part = angle_pair(jnp.arange(NZ, dtype=jnp.int32), jnp.arange(KZ, dtype=jnp.int32), NZ)
    factor = jnp.where(jnp.arange(KZ) == 0, jnp.float32(1.0), jnp.float32(2.0))
    depth_forward = jnp.concatenate([cosine, -sine_part], axis=1).astype(jnp.bfloat16)
    depth_inverse = jnp.concatenate([cosine.T * factor[:, None], -sine_part.T * factor[:, None]], axis=0).astype(jnp.bfloat16)
    column_forward = complex_table(jnp.arange(NY, dtype=jnp.int32), NY, KY).astype(jnp.bfloat16)
    column_inverse = jnp.transpose(column_forward, (3, 2, 1, 0))
    row_float = complex_table(jnp.arange(NX, dtype=jnp.int32), NX, KX)
    row_forward = row_float.astype(jnp.bfloat16)
    row_inverse = jnp.transpose(row_float, (3, 2, 1, 0))
    return (depth_forward, depth_inverse, column_forward, column_inverse, row_forward, row_inverse)

def spectrum(field_cells, tables):
    depth_modes = jnp.dot(field_cells.reshape(-1, NZ), tables[0], preferred_element_type=jnp.float32).astype(jnp.bfloat16)
    depth_modes = depth_modes.reshape(C, NX, NY, 2, KZ)
    column_modes = jnp.einsum('cxypk,ypqj->qcxjk', depth_modes.astype(jnp.float32), tables[2].astype(jnp.float32)).astype(jnp.bfloat16)
    column_modes = column_modes.reshape(2, C, NX, KY * KZ)
    spectra = jnp.einsum('pcxm,xpqj->qcmj', column_modes.astype(jnp.float32), tables[4].astype(jnp.float32))
    return spectra.reshape(2, C, MODES)

def field_from(mixed_modes, tables):
    inverse_total = 1.0 / (NX * NY * NZ)
    blocks = mixed_modes.reshape(2, C, KY * KZ, KX)
    rows_back = jnp.einsum('pcmj,jpqx->qcxm', blocks, tables[5], precision=lax.Precision.HIGHEST)
    rows_back = (rows_back * inverse_total).astype(jnp.bfloat16)
    line_modes = jnp.einsum('pcxjk,jpqy->cxyqk', rows_back.reshape(2, C, NX, KY, KZ).astype(jnp.float32), tables[3].astype(jnp.float32)).astype(jnp.bfloat16)
    cell_values = jnp.dot(line_modes.reshape(-1, 2 * KZ), tables[1], preferred_element_type=jnp.float32).astype(jnp.bfloat16)
    return cell_values.reshape(C, NX, NY, NZ)

def mix_modes(weights, spectra):
    real_in = spectra[0][:, None, :]
    imag_in = spectra[1][:, None, :]
    real_part = lax.optimization_barrier(jnp.sum(weights[0] * real_in - weights[1] * imag_in, axis=0))
    imag_part = lax.optimization_barrier(jnp.sum(weights[0] * imag_in + weights[1] * real_in, axis=0))
    return jnp.stack([real_part, imag_part])

def mode_grad(grad_spectra, spectra, weight_scale):
    grad_real = (grad_spectra[0] * weight_scale)[None]
    grad_imag = (grad_spectra[1] * weight_scale)[None]
    real_in = spectra[0][:, None, :]
    imag_in = spectra[1][:, None, :]
    return jnp.stack([real_in * grad_real + imag_in * grad_imag, real_in * grad_imag - imag_in * grad_real])

def reference(fields, cotangents, w_point, bias_vector, spectral):
    tables = make_tables()
    mode_ids = jnp.arange(MODES, dtype=jnp.int32) // KX
    weight_scale = jnp.where(mode_ids % KZ == 0, jnp.float32(1.0), jnp.float32(2.0)) * (1.0 / (NX * NY * NZ))
    weights = spectral
    activation = None
    for step_index in range(STEPS):
        field_cells = fields[step_index]
        spectra = spectrum(field_cells, tables)
        branch = field_from(mix_modes(weights, spectra), tables)
        pre_gelu = jnp.einsum('oi,ixyz->oxyz', w_point.astype(jnp.float32), field_cells.astype(jnp.float32))
        pre_gelu = pre_gelu + branch.astype(jnp.float32) + bias_vector[:, None, None, None]
        output_value, pullback = jax.vjp(jax.nn.gelu, pre_gelu)
        grad_pre = pullback(cotangents[step_index].astype(jnp.float32))[0].astype(jnp.bfloat16)
        grad_spectra = spectrum(grad_pre, tables)
        weights = weights - learn_rate * mode_grad(grad_spectra, spectra, weight_scale)
        activation = output_value.astype(jnp.bfloat16)
    return (activation, weights)
```

```python
import math

import jax
import jax.numpy as jnp
from jax import lax
from jax.sharding import PartitionSpec as P

NX = 256
NY = 240
NZ = 128
KX = 48
KY = 48
KZ = 24


learn_rate = 0.1


def angle_pair(positions, frequencies, length):
    product = positions[:, None] * frequencies[None, :] % length
    phase_angle = product.astype(jnp.float32) * (2.0 * math.pi / length)
    return (jnp.cos(phase_angle), jnp.sin(phase_angle))


def kept_waves(length, kept_count):
    wave_index = jnp.arange(kept_count, dtype=jnp.int32)
    return jnp.where(wave_index < kept_count // 2, wave_index, wave_index - kept_count + length)


def complex_table(positions, length, kept_count):
    cosine, sine_part = angle_pair(positions, kept_waves(length, kept_count), length)
    upper_rows = jnp.stack([cosine, -sine_part], axis=1)
    lower_rows = jnp.stack([sine_part, cosine], axis=1)
    return jnp.stack([upper_rows, lower_rows], axis=1)


def build_tables():
    cosine, sine_part = angle_pair(
        jnp.arange(NZ, dtype=jnp.int32), jnp.arange(KZ, dtype=jnp.int32), NZ
    )
    factor = jnp.where(jnp.arange(KZ) == 0, jnp.float32(1.0), jnp.float32(2.0))
    depth_forward = jnp.concatenate([cosine, -sine_part], axis=1).astype(jnp.bfloat16)
    depth_inverse = jnp.concatenate(
        [cosine.T * factor[:, None], -sine_part.T * factor[:, None]], axis=0
    ).astype(jnp.bfloat16)
    column_forward = complex_table(jnp.arange(NY, dtype=jnp.int32), NY, KY).astype(jnp.bfloat16)
    column_inverse = jnp.transpose(column_forward, (3, 2, 1, 0))
    natural_rows = jnp.arange(NX, dtype=jnp.int32)
    row_forward = complex_table(natural_rows, NX, KX).astype(jnp.bfloat16)
    row_inverse = jnp.transpose(complex_table(natural_rows, NX, KX), (3, 2, 1, 0))
    return (depth_forward, depth_inverse, column_forward, column_inverse, row_forward, row_inverse)


def spectrum(field_cells, tables):
    channels, slab_rows, slab_cols, depth_count = field_cells.shape
    depth_modes = jnp.dot(
        field_cells.reshape(-1, depth_count), tables[0], preferred_element_type=jnp.float32
    ).astype(jnp.bfloat16)
    depth_modes = depth_modes.reshape(channels, slab_rows, slab_cols, 2 * KZ)
    line_modes = lax.all_to_all(depth_modes, "gy", split_axis=1, concat_axis=2, tiled=True)
    line_rows = line_modes.shape[1]
    column_modes = jnp.einsum(
        "cxypk,ypqj->qcxjk",
        line_modes.reshape(channels, line_rows, NY, 2, KZ),
        tables[2],
        preferred_element_type=jnp.float32,
    ).astype(jnp.bfloat16)
    column_modes = column_modes.reshape(2, channels, line_rows, KY * KZ)
    gathered = lax.all_to_all(column_modes, ("gx", "gy"), split_axis=3, concat_axis=2, tiled=True)
    local_modes = gathered.shape[3]
    spectra = jnp.einsum("pcxm,xpqj->qcmj", gathered, tables[4], preferred_element_type=jnp.float32)
    return spectra.reshape(2, channels, local_modes * KX)


def field_from(mixed_modes, tables):
    inverse_total = 1.0 / (NX * NY * NZ)
    channels = mixed_modes.shape[1]
    local_modes = mixed_modes.shape[2] // KX
    blocks = mixed_modes.reshape(2, channels, local_modes, KX)
    rows_back = jnp.einsum(
        "pcmj,jpqx->qcxm",
        blocks,
        tables[5],
        precision=lax.Precision.HIGHEST,
        preferred_element_type=jnp.float32,
    )
    rows_back = (rows_back * inverse_total).astype(jnp.bfloat16)
    returned = lax.all_to_all(rows_back, ("gx", "gy"), split_axis=2, concat_axis=3, tiled=True)
    line_rows = returned.shape[2]
    line_modes = jnp.einsum(
        "pcxjk,jpqy->cxyqk",
        returned.reshape(2, channels, line_rows, KY, KZ),
        tables[3],
        preferred_element_type=jnp.float32,
    ).astype(jnp.bfloat16)
    line_modes = line_modes.reshape(channels, line_rows, NY, 2 * KZ)
    slab_modes = lax.all_to_all(line_modes, "gy", split_axis=2, concat_axis=1, tiled=True)
    cell_values = jnp.dot(
        slab_modes.reshape(-1, 2 * KZ), tables[1], preferred_element_type=jnp.float32
    ).astype(jnp.bfloat16)
    return cell_values.reshape(channels, slab_modes.shape[1], slab_modes.shape[2], NZ)


def mix_modes(weights, spectra):
    real_in = spectra[0][:, None, :]
    imag_in = spectra[1][:, None, :]
    real_part = jnp.sum(weights[0] * real_in - weights[1] * imag_in, axis=0)
    imag_part = jnp.sum(weights[0] * imag_in + weights[1] * real_in, axis=0)
    return jnp.stack([real_part, imag_part])


def mode_grad(grad_spectra, spectra, weight_scale):
    grad_real = (grad_spectra[0] * weight_scale)[None]
    grad_imag = (grad_spectra[1] * weight_scale)[None]
    real_in = spectra[0][:, None, :]
    imag_in = spectra[1][:, None, :]
    return jnp.stack(
        [real_in * grad_real + imag_in * grad_imag, real_in * grad_imag - imag_in * grad_real]
    )


def shards(fields, cotangents, w_point, bias_vector, spectral):
    tables = build_tables()
    local_modes = spectral.shape[3] // KX
    owner_index = lax.axis_index("gx") * lax.axis_size("gy") + lax.axis_index("gy")
    mode_ids = owner_index * local_modes + jnp.arange(local_modes, dtype=jnp.int32)
    weight_scale = jnp.where(mode_ids % KZ == 0, jnp.float32(1.0), jnp.float32(2.0)) * (
        1.0 / (NX * NY * NZ)
    )
    weight_scale = jnp.repeat(weight_scale, KX)
    weights = spectral
    activation = None
    for step_index in range(fields.shape[0]):
        field_cells = fields[step_index]
        spectra = spectrum(field_cells, tables)
        branch = field_from(mix_modes(weights, spectra), tables)
        pre_gelu = jnp.einsum(
            "oi,ixyz->oxyz", w_point, field_cells, preferred_element_type=jnp.float32
        )
        pre_gelu = pre_gelu + branch.astype(jnp.float32) + bias_vector[:, None, None, None]
        output_value, pullback = jax.vjp(jax.nn.gelu, pre_gelu)
        grad_pre = pullback(cotangents[step_index].astype(jnp.float32))[0].astype(jnp.bfloat16)
        grad_spectra = spectrum(grad_pre, tables)
        weights = weights - learn_rate * mode_grad(grad_spectra, spectra, weight_scale)
        activation = output_value.astype(jnp.bfloat16)
    return (activation, weights)


def solution(mesh):
    return jax.shard_map(
        shards,
        mesh=mesh,
        in_specs=(
            P(None, None, "gx", "gy", None),
            P(None, None, "gx", "gy", None),
            P(),
            P(),
            P(None, None, None, ("gx", "gy")),
        ),
        out_specs=(P(None, "gx", "gy", None), P(None, None, None, ("gx", "gy"))),
        check_vma=False,
    )
```

```python
import functools
import math

import jax
import jax.numpy as jnp
import ml_dtypes
import numpy as np
from jax import lax
from jax.experimental import pallas as pl
from jax.experimental.pallas import tpu as pltpu
from jax.sharding import PartitionSpec as P

C = 20
NX, NY, NZ = 256, 240, 128
KX, KY, KZ = 48, 48, 24
GX, GY = 8, 16
LEARN_RATE = 0.1
INVERSE_TOTAL = 1.0 / (NX * NY * NZ)
BF = jnp.bfloat16
F32 = jnp.float32
MESH = pl.DeviceIdType.MESH
GELU_K = math.sqrt(2.0 / math.pi)
GELU_C = 0.044715


def waves(length, kept):
    index = np.arange(kept)
    return np.where(index < kept // 2, index, index - kept + length)


def angle_tables(length, freqs):
    product = (np.arange(length)[:, None] * freqs[None, :]) % length
    angle = product.astype(np.float32) * np.float32(2.0 * math.pi / length)
    return np.cos(angle), np.sin(angle)


def rounded(table):
    return table.astype(ml_dtypes.bfloat16)


def make_tables():
    cos_z, sin_z = angle_tables(NZ, np.arange(KZ))
    both = np.stack([cos_z, -sin_z]).transpose(0, 2, 1)
    both = both.reshape(2, 8, 3, NZ).transpose(1, 0, 2, 3)
    deep0 = np.einsum("gpkz,nm->gpnkmz", both, np.eye(8, dtype=np.float32)).reshape(384, 1024)
    deep1 = np.zeros((8, 2, 16, 4, NZ), np.float32)
    deep1[:, :, :12] = np.einsum("gpkz,nm->gpnkmz", both, np.eye(4, dtype=np.float32)).reshape(
        8, 2, 12, 4, NZ
    )
    deep1 = deep1.reshape(256, 512)
    factor = np.where(np.arange(KZ) == 0, 1.0, 2.0).astype(np.float32)
    back = np.stack([cos_z * factor, -sin_z * factor]).transpose(0, 2, 1)
    back = back.reshape(2, 8, 3, NZ).transpose(1, 0, 2, 3)
    rise0 = np.einsum("gpkz,nm->gpnkmz", back, np.eye(16, dtype=np.float32))
    rise0 = rise0.reshape(768, 8, 256).transpose(1, 0, 2)
    rise1 = np.zeros((8, 2, 16, 4, NZ), np.float32)
    rise1[:, :, :12] = np.einsum("gpkz,nm->gpnkmz", back, np.eye(4, dtype=np.float32)).reshape(
        8, 2, 12, 4, NZ
    )
    rise1 = rise1.reshape(256, 2, 256).transpose(1, 0, 2)
    cos_y, sin_y = angle_tables(NY, waves(NY, KY))
    padded = np.zeros((2, GY, 16, KY), np.float32)
    padded[:, :, :15] = np.stack([cos_y, sin_y]).reshape(2, GY, 15, KY)
    eye8 = np.eye(8, dtype=np.float32)
    column = np.einsum("asyk,xw->akxswy", padded, eye8)
    column = column.reshape(2, 2, 24 * 8, 2048).transpose(1, 0, 2, 3).reshape(2, 384, 2048)
    signed = np.stack([padded[0], -padded[1]])
    column_back = np.einsum("asyk,wx->kawsxy", signed, eye8)
    column_back = column_back.reshape(768, 8, 256).transpose(1, 0, 2)
    cos_x, sin_x = angle_tables(NX, waves(NX, KX))
    shape = (GX, 2, 2, 8, KX)
    cos_x = cos_x.reshape(shape).transpose(1, 0, 2, 3, 4)
    sin_x = sin_x.reshape(shape).transpose(1, 0, 2, 3, 4)
    row = np.zeros((2, GX, 2, 8, 2, 2, 64), np.float32)
    row_back = np.zeros_like(row)
    for xb in range(2):
        c, s = cos_x[:, :, xb], sin_x[:, :, xb]
        row[:, :, 0, :, xb, 0, :KX] = c
        row[:, :, 1, :, xb, 0, :KX] = s
        row[:, :, 0, :, xb, 1, :KX] = -s
        row[:, :, 1, :, xb, 1, :KX] = c
        row_back[:, :, 0, :, xb, 0, :KX] = c
        row_back[:, :, 0, :, xb, 1, :KX] = -s
        row_back[:, :, 1, :, xb, 0, :KX] = s
        row_back[:, :, 1, :, xb, 1, :KX] = c
    row = row.reshape(256, 256)
    row_back = row_back.reshape(256, 256)
    row_high = rounded(row_back)
    row_low = rounded(row_back - row_high.astype(np.float32))
    return (
        rounded(deep0),
        rounded(deep1),
        rounded(column),
        rounded(row),
        np.stack([row_high, row_low]),
        rounded(column_back),
        rounded(rise0),
        rounded(rise1),
    )


def dot_nt(a, b):
    return lax.dot_general(a, b, (((1,), (1,)), ((), ())), preferred_element_type=F32)


def dot_nn(a, b):
    return lax.dot_general(a, b, (((1,), (0,)), ((), ())), preferred_element_type=F32)


def kernel(
    fields_hbm, cots_hbm, w_ref, bias_ref, spectral_hbm,
    deep0_hbm, deep1_hbm, column_hbm, row_hbm, row_back_hbm, column_back_hbm, rise0_hbm, rise1_hbm,
    act_hbm, trained_hbm,
    fields, cots, cells, weights, act,
    deep0, deep1, column, row, row_back, column_back, rise0, rise1,
    send_a, recv_a, send_b, recv_b, back_b, got_b, back_a, got_a,
    xs, spectra, xi, turned, lifted, branch, kron,
    load_sems, out_sems,
    a_send, a_recv, b_send, b_recv, bb_send, bb_recv, ba_send, ba_recv,
):
    gx = lax.axis_index("gx")
    gy = lax.axis_index("gy")
    me = gx * GY + gy
    my_half = gy // 8
    my_group = gy % 8

    loads = [
        (fields_hbm.at[0], fields.at[0]),
        (deep0_hbm, deep0),
        (deep1_hbm, deep1),
        (column_hbm, column),
        (fields_hbm.at[1], fields.at[1]),
        (row_hbm, row),
        (spectral_hbm, weights),
        (row_back_hbm, row_back),
        (column_back_hbm, column_back),
        (rise0_hbm, rise0),
        (rise1_hbm, rise1),
        (cots_hbm, cots),
    ]
    copies = [
        pltpu.make_async_copy(src, dst, load_sems.at[n]) for n, (src, dst) in enumerate(loads)
    ]
    for copy in copies:
        copy.start()

    barrier = pltpu.get_barrier_semaphore()

    def greet(d, _):
        other = lax.rem(me + d, GX * GY)
        pl.semaphore_signal(
            barrier, inc=1, device_id=(other // GY, lax.rem(other, GY)), device_id_type=MESH
        )
        return 0

    lax.fori_loop(1, GX * GY, greet, 0)

    wide = lax.broadcasted_iota(jnp.int32, (C * 16, C), 0) // 16
    spread = (wide == lax.broadcasted_iota(jnp.int32, (C * 16, C), 1)).astype(BF)
    grown = dot_nt(dot_nn(spread, w_ref[...]).astype(BF), spread)
    same = lax.rem(lax.broadcasted_iota(jnp.int32, (C * 16, C * 16), 0), 16) == lax.rem(
        lax.broadcasted_iota(jnp.int32, (C * 16, C * 16), 1), 16
    )
    kron[...] = jnp.where(same, grown, 0.0).astype(BF)
    xi[...] = jnp.zeros_like(xi)

    def pad_cells(step):
        cells[step] = jnp.zeros((C, 32, 16, 128), BF)

        def one(c, _):
            cells[step, c, :, 0:15, :] = fields[step, c]
            return 0

        lax.fori_loop(0, C, one, 0)

    def deep_half(f, step, xh):
        for xb in range(2):
            rows = pl.ds((xh * 2 + xb) * 8, 8)

            def block(c):
                return cells[step, c, rows].reshape(128, 128)

            o0 = dot_nt(deep0[...], jnp.concatenate([block(c) for c in range(8)], axis=1))
            o1 = dot_nt(deep0[...], jnp.concatenate([block(c) for c in range(8, 16)], axis=1))
            o2 = dot_nt(deep1[...], jnp.concatenate([block(c) for c in range(16, 20)], axis=1))
            for group in range(8):
                for part in range(2):
                    a = group * 48 + part * 24
                    b = group * 32 + part * 16
                    send_a[f, xh * 8 + group, part, xb] = jnp.concatenate(
                        [o0[a : a + 24], o1[a : a + 24], o2[b : b + 16]], axis=0
                    ).astype(BF)

    def a_copy(f, target):
        return pltpu.make_async_remote_copy(
            src_ref=send_a.at[f, target],
            dst_ref=recv_a.at[f, gy],
            send_sem=a_send.at[f],
            recv_sem=a_recv.at[f],
            device_id=(gx, target),
            device_id_type=MESH,
        )

    def send_a_half(f, xh):
        def one(k, _):
            target = xh * 8 + lax.rem(my_group + 1 + k, 8)

            @pl.when(target == gy)
            def _():
                pltpu.make_async_copy(send_a.at[f, target], recv_a.at[f, gy], a_recv.at[f]).start()

            @pl.when(target != gy)
            def _():
                a_copy(f, target).start()

            return 0

        lax.fori_loop(0, 8, one, 0)

    def wait_all(ref, sem):
        pltpu.make_async_copy(ref, ref, sem).wait()

    def b_target(ky):
        group = lax.rem(ky, 6) * 8 + my_group
        return ky // 6, group // 3, lax.rem(group, 3)

    def b_copy(f, ky):
        other_x, other_y, slot = b_target(ky)
        return pltpu.make_async_remote_copy(
            src_ref=send_b.at[f, ky],
            dst_ref=recv_b.at[f, slot, my_half, gx],
            send_sem=b_send.at[f],
            recv_sem=b_recv.at[f],
            device_id=(other_x, other_y),
            device_id_type=MESH,
        )

    def columns(f):
        data = jnp.concatenate(
            [recv_a[f, s].reshape(256, 128) for s in range(GY)], axis=1
        )
        for part in range(2):
            out = dot_nt(column[part], data)
            real = out[:192, :128] + out[192:, 128:]
            imag = out[:192, 128:] - out[192:, :128]
            send_b[f, pl.ds(part * 24, 24)] = jnp.concatenate(
                [real.reshape(24, 8, 128), imag.reshape(24, 8, 128)], axis=1
            ).astype(BF)

            def one(k, _):
                ky = part * 24 + lax.rem(gx * 6 + gy + k, 24)
                other_x, other_y, slot = b_target(ky)
                mine = jnp.logical_and(other_x == gx, other_y == gy)

                @pl.when(mine)
                def _():
                    pltpu.make_async_copy(
                        send_b.at[f, ky], recv_b.at[f, slot, my_half, gx], b_recv.at[f]
                    ).start()

                @pl.when(jnp.logical_not(mine))
                def _():
                    b_copy(f, ky).start()

                return 0

            lax.fori_loop(0, 24, one, 0)

    def rows_forward(f):
        pieces = []
        for slot in range(3):
            data = recv_b[f, slot].reshape(256, 128)
            out = dot_nn(data.T, row[...])
            xs[slot] = out[0:64, 0:128] + out[64:128, 128:256]
            for kz in range(3):
                pieces.append(xs[slot, pl.ds(kz, C, stride=3), :])
        spectra[f, 0] = jnp.concatenate([piece[:, 0:48] for piece in pieces], axis=1)
        spectra[f, 1] = jnp.concatenate([piece[:, 64:112] for piece in pieces], axis=1)

    pair = lax.broadcasted_iota(jnp.int32, (1, 432), 1) // KX + me * 9
    scale = jnp.where(lax.rem(pair, KZ) == 0, 1.0, 2.0).astype(F32) * INVERSE_TOTAL

    def mix(f, update):
        if update is not None:
            field_f, grad_f = update
            grad_re = spectra[grad_f, 0] * scale * LEARN_RATE
            grad_im = spectra[grad_f, 1] * scale * LEARN_RATE

        def one(i, carry):
            w_re, w_im = weights[0, i], weights[1, i]
            if update is not None:
                in_re = spectra[field_f, 0, pl.ds(i, 1), :]
                in_im = spectra[field_f, 1, pl.ds(i, 1), :]
                w_re = w_re - (in_re * grad_re + in_im * grad_im)
                w_im = w_im - (in_re * grad_im - in_im * grad_re)
                weights[0, i] = w_re
                weights[1, i] = w_im
            if f is None:
                return carry
            re, im = carry
            s_re = spectra[f, 0, pl.ds(i, 1), :]
            s_im = spectra[f, 1, pl.ds(i, 1), :]
            return re + (w_re * s_re - w_im * s_im), im + (w_re * s_im + w_im * s_re)

        zero = jnp.zeros((C, 432), F32)
        return lax.fori_loop(0, C, one, (zero, zero))

    def bb_copy(step, slot, n):
        group = gy * 3 + slot
        return pltpu.make_async_remote_copy(
            src_ref=back_b.at[step, slot, n],
            dst_ref=got_b.at[step, gx * 6 + group // 8],
            send_sem=bb_send.at[step],
            recv_sem=bb_recv.at[step],
            device_id=(lax.rem(n, 8), (n // 8) * 8 + lax.rem(group, 8)),
            device_id_type=MESH,
        )

    def rows_inverse(step, mixed):
        re, im = mixed
        gap = jnp.zeros((C, 16), F32)
        for slot in range(3):
            for kz in range(3):
                a = (slot * 3 + kz) * 48
                xi[slot, pl.ds(kz, C, stride=3), :] = jnp.concatenate(
                    [re[:, a : a + 48], gap, im[:, a : a + 48], gap], axis=1
                )
            value = xi[slot]
            high = value.astype(BF)
            low = (value - high.astype(F32)).astype(BF)
            none = jnp.zeros((64, 128), BF)

            def both(v):
                return jnp.concatenate(
                    [jnp.concatenate([v, none], axis=1), jnp.concatenate([none, v], axis=1)],
                    axis=0,
                )

            high, low = both(high), both(low)
            out = dot_nt(row_back[0], high) + (dot_nt(row_back[0], low) + dot_nt(row_back[1], high))
            back_b[step, slot] = (out * INVERSE_TOTAL).astype(BF).reshape(16, 16, 128)
            group = gy * 3 + slot

            def one(k, _):
                n = lax.rem(gx + gy + k, 16)
                mine = jnp.logical_and(
                    lax.rem(n, 8) == gx, (n // 8) * 8 + lax.rem(group, 8) == gy
                )

                @pl.when(mine)
                def _():
                    pltpu.make_async_copy(
                        back_b.at[step, slot, n],
                        got_b.at[step, gx * 6 + group // 8],
                        bb_recv.at[step],
                    ).start()

                @pl.when(jnp.logical_not(mine))
                def _():
                    bb_copy(step, slot, n).start()

                return 0

            lax.fori_loop(0, 16, one, 0)

    def ba_copy(step, target):
        return pltpu.make_async_remote_copy(
            src_ref=back_a.at[step, target],
            dst_ref=got_a.at[step, gy],
            send_sem=ba_send.at[step],
            recv_sem=ba_recv.at[step, my_half],
            device_id=(gx, target),
            device_id_type=MESH,
        )

    def columns_inverse(step):
        data = got_b[step].astype(F32)
        swapped = jnp.concatenate([data[:, 8:16], -data[:, 0:8]], axis=1)
        turned[0:128, :] = data.reshape(768, 128).astype(BF).T
        turned[128:256, :] = swapped.reshape(768, 128).astype(BF).T

        def one(k, _):
            duo = lax.rem(gy // 2 + 1 + k, 8)
            out = dot_nn(turned[...], column_back[duo]).astype(BF)
            for j in range(2):
                target = duo * 2 + j
                back_a[step, target] = out[:, j * 128 : j * 128 + 128].reshape(2, 2, 64, 128)

                @pl.when(target == gy)
                def _():
                    pltpu.make_async_copy(
                        back_a.at[step, target], got_a.at[step, gy], ba_recv.at[step, my_half]
                    ).start()

                @pl.when(target != gy)
                def _():
                    ba_copy(step, target).start()

            return 0

        lax.fori_loop(0, 8, one, 0)

    def deep_inverse(step, xh):
        wait_all(got_a.at[step, pl.ds(xh * 8, 8)], ba_recv.at[step, xh])
        for xb in range(2):
            first = jnp.concatenate(
                [got_a[step, xh * 8 + g, p, xb, 0:48] for g in range(8) for p in range(2)], axis=0
            )
            second = jnp.concatenate(
                [got_a[step, xh * 8 + g, p, xb, 48:64] for g in range(8) for p in range(2)], axis=0
            )
            lifted[xb * 128 : xb * 128 + 128, 0:768] = first.T
            lifted[xb * 128 : xb * 128 + 128, 768:1024] = second.T

        def save(out, c):
            for j in range(2):
                branch[c + j, pl.ds(xh * 16, 16)] = (
                    out[:, j * 128 : j * 128 + 128].astype(BF).reshape(16, 16, 128)
                )

        def one(k, _):
            save(dot_nn(lifted[:, 0:768], rise0[k]), 2 * k)
            return 0

        lax.fori_loop(0, 8, one, 0)
        for k in range(2):
            save(dot_nn(lifted[:, 768:1024], rise1[k]), 16 + 2 * k)

    def pointwise(step, xh, last):
        def one(k, _):
            x = xh * 16 + k
            data = jnp.concatenate([cells[step, c, x] for c in range(C)], axis=0)
            pre = dot_nn(kron[...], data)
            for o in range(C):
                v = pre[o * 16 : o * 16 + 16] + branch[o, x].astype(F32) + bias_ref[o]
                v = v[0:15]
                square = v * v
                t = jnp.tanh(v * (GELU_K + (GELU_K * GELU_C) * square))
                half = 0.5 + 0.5 * t
                slope = half + (0.5 * v) * (1.0 - t * t) * (
                    GELU_K + (3.0 * GELU_K * GELU_C) * square
                )
                cells[step, o, x, 0:15, :] = (cots[step, o, x].astype(F32) * slope).astype(BF)
                if last:
                    act[o, x] = (v * half).astype(BF)
            return 0

        lax.fori_loop(0, 16, one, 0)

    copies[0].wait()
    pad_cells(0)
    copies[1].wait()
    copies[2].wait()
    deep_half(0, 0, 0)
    pl.semaphore_wait(barrier, GX * GY - 1)
    send_a_half(0, 0)
    deep_half(0, 0, 1)
    send_a_half(0, 1)

    copies[4].wait()
    pad_cells(1)
    deep_half(1, 1, 0)
    deep_half(1, 1, 1)

    wait_all(recv_a.at[0], a_recv.at[0])
    send_a_half(1, 0)
    send_a_half(1, 1)
    copies[3].wait()
    columns(0)
    copies[5].wait()
    copies[6].wait()
    copies[7].wait()
    wait_all(recv_b.at[0], b_recv.at[0])
    rows_forward(0)
    rows_inverse(0, mix(0, None))
    copies[8].wait()
    wait_all(got_b.at[0], bb_recv.at[0])
    columns_inverse(0)

    wait_all(recv_a.at[1], a_recv.at[1])
    columns(1)
    copies[9].wait()
    copies[10].wait()
    copies[11].wait()

    for xh in range(2):
        deep_inverse(0, xh)
        pointwise(0, xh, False)
        deep_half(2, 0, xh)
        send_a_half(2, xh)
    wait_all(recv_b.at[1], b_recv.at[1])
    rows_forward(1)
    wait_all(recv_a.at[2], a_recv.at[2])
    columns(2)
    wait_all(recv_b.at[2], b_recv.at[2])
    rows_forward(2)
    rows_inverse(1, mix(1, (0, 2)))
    wait_all(got_b.at[1], bb_recv.at[1])
    columns_inverse(1)
    for xh in range(2):
        deep_inverse(1, xh)
        pointwise(1, xh, True)
        deep_half(3, 1, xh)
        send_a_half(3, xh)
    act_out = pltpu.make_async_copy(act, act_hbm, out_sems.at[0])
    act_out.start()
    wait_all(recv_a.at[3], a_recv.at[3])
    columns(3)
    wait_all(recv_b.at[3], b_recv.at[3])
    rows_forward(3)
    mix(None, (1, 3))
    trained_out = pltpu.make_async_copy(weights, trained_hbm, out_sems.at[1])
    trained_out.start()

    for f in range(4):

        def sent_a(k, _):
            @pl.when(k != gy)
            def _():
                a_copy(f, k).wait_send()

            return 0

        lax.fori_loop(0, GY, sent_a, 0)

        def sent_b(ky, _):
            other_x, other_y, slot = b_target(ky)

            @pl.when(jnp.logical_not(jnp.logical_and(other_x == gx, other_y == gy)))
            def _():
                b_copy(f, ky).wait_send()

            return 0

        lax.fori_loop(0, KY, sent_b, 0)
    for step in range(2):

        def sent_ba(k, _):
            @pl.when(k != gy)
            def _():
                ba_copy(step, k).wait_send()

            return 0

        lax.fori_loop(0, GY, sent_ba, 0)
        for slot in range(3):
            group = gy * 3 + slot

            def sent_bb(n, _):
                mine = jnp.logical_and(
                    lax.rem(n, 8) == gx, (n // 8) * 8 + lax.rem(group, 8) == gy
                )

                @pl.when(jnp.logical_not(mine))
                def _():
                    bb_copy(step, slot, n).wait_send()

                return 0

            lax.fori_loop(0, 16, sent_bb, 0)
    act_out.wait()
    trained_out.wait()


def shards(fields, cotangents, w_point, bias_vector, spectral):
    tables = [jnp.asarray(table) for table in make_tables()]
    anywhere = pl.BlockSpec(memory_space=pl.ANY)
    vmem = pltpu.VMEM
    grid_shape = (C, 32, 15, 128)
    dma = pltpu.SemaphoreType.DMA
    scratch = [
        vmem((2,) + grid_shape, BF),
        vmem((2,) + grid_shape, BF),
        vmem((2, C, 32, 16, 128), BF),
        vmem((2, C, C, 432), F32),
        vmem(grid_shape, BF),
    ]
    scratch += [vmem(table.shape, BF) for table in tables]
    scratch += [
        vmem((4, GY, 2, 2, 64, 128), BF),
        vmem((4, GY, 2, 2, 64, 128), BF),
        vmem((4, KY, 16, 128), BF),
        vmem((4, 3, 2, GX, 16, 128), BF),
        vmem((2, 3, 16, 16, 128), BF),
        vmem((2, KY, 16, 128), BF),
        vmem((2, GY, 2, 2, 64, 128), BF),
        vmem((2, GY, 2, 2, 64, 128), BF),
        vmem((3, 64, 128), F32),
        vmem((4, 2, C, 432), F32),
        vmem((3, 64, 128), F32),
        vmem((256, 768), BF),
        vmem((256, 1024), BF),
        vmem((C, 32, 16, 128), BF),
        vmem((C * 16, C * 16), BF),
        dma((12,)),
        dma((2,)),
        dma((4,)),
        dma((4,)),
        dma((4,)),
        dma((4,)),
        dma((2,)),
        dma((2,)),
        dma((2,)),
        dma((2, 2)),
    ]
    return pl.pallas_call(
        kernel,
        out_shape=(
            jax.ShapeDtypeStruct(grid_shape, BF),
            jax.ShapeDtypeStruct((2, C, C, 432), F32),
        ),
        in_specs=[
            anywhere,
            anywhere,
            pl.BlockSpec(memory_space=pltpu.VMEM),
            pl.BlockSpec(memory_space=pltpu.SMEM),
            anywhere,
        ]
        + [anywhere] * len(tables),
        out_specs=(anywhere, anywhere),
        scratch_shapes=scratch,
        compiler_params=pltpu.CompilerParams(
            collective_id=0, has_side_effects=True, vmem_limit_bytes=62 * 1024 * 1024
        ),
    )(fields, cotangents, w_point, bias_vector, spectral, *tables)


def solution(mesh):
    return jax.shard_map(
        shards,
        mesh=mesh,
        in_specs=(
            P(None, None, "gx", "gy", None),
            P(None, None, "gx", "gy", None),
            P(),
            P(),
            P(None, None, None, ("gx", "gy")),
        ),
        out_specs=(P(None, "gx", "gy", None), P(None, None, None, ("gx", "gy"))),
        check_vma=False,
    )
```

```python
import functools
import math

import jax
import jax.numpy as jnp
import ml_dtypes
import numpy as np
from jax import lax
from jax.experimental import pallas as pl
from jax.experimental.pallas import tpu as pltpu
from jax.sharding import PartitionSpec as P

C = 20
NX, NY, NZ = 256, 240, 128
KX, KY, KZ = 48, 48, 24
GX, GY = 8, 16
LEARN_RATE = 0.1
INVERSE_TOTAL = 1.0 / (NX * NY * NZ)
BF = jnp.bfloat16
F32 = jnp.float32
MESH = pl.DeviceIdType.MESH
GELU_K = math.sqrt(2.0 / math.pi)
GELU_C = 0.044715


def waves(length, kept):
    index = np.arange(kept)
    return np.where(index < kept // 2, index, index - kept + length)


def angle_tables(length, freqs):
    product = (np.arange(length)[:, None] * freqs[None, :]) % length
    angle = product.astype(np.float32) * np.float32(2.0 * math.pi / length)
    return np.cos(angle), np.sin(angle)


def rounded(table):
    return table.astype(ml_dtypes.bfloat16)


def make_tables():
    cos_z, sin_z = angle_tables(NZ, np.arange(KZ))
    both = np.stack([cos_z, -sin_z]).transpose(0, 2, 1)
    both = both.reshape(2, 8, 3, NZ).transpose(1, 0, 2, 3)
    deep0 = np.einsum("gpkz,nm->gpnkmz", both, np.eye(8, dtype=np.float32)).reshape(384, 1024)
    deep1 = np.zeros((8, 2, 16, 4, NZ), np.float32)
    deep1[:, :, :12] = np.einsum("gpkz,nm->gpnkmz", both, np.eye(4, dtype=np.float32)).reshape(
        8, 2, 12, 4, NZ
    )
    deep1 = deep1.reshape(256, 512)
    factor = np.where(np.arange(KZ) == 0, 1.0, 2.0).astype(np.float32)
    back = np.stack([cos_z * factor, -sin_z * factor]).transpose(0, 2, 1)
    back = back.reshape(2, 8, 3, NZ).transpose(1, 0, 2, 3)
    rise0 = np.einsum("gpkz,nm->gpnkmz", back, np.eye(16, dtype=np.float32))
    rise0 = rise0.reshape(768, 8, 256).transpose(1, 0, 2)
    rise1 = np.zeros((8, 2, 16, 4, NZ), np.float32)
    rise1[:, :, :12] = np.einsum("gpkz,nm->gpnkmz", back, np.eye(4, dtype=np.float32)).reshape(
        8, 2, 12, 4, NZ
    )
    rise1 = rise1.reshape(256, 2, 256).transpose(1, 0, 2)
    cos_y, sin_y = angle_tables(NY, waves(NY, KY))
    padded = np.zeros((2, GY, 16, KY), np.float32)
    padded[:, :, :15] = np.stack([cos_y, sin_y]).reshape(2, GY, 15, KY)
    eye8 = np.eye(8, dtype=np.float32)
    column = np.einsum("asyk,xw->akxsyw", padded, eye8)
    column = column.reshape(2, 2, 24 * 8, 2048).transpose(1, 0, 2, 3).reshape(2, 384, 2048)
    signed = np.stack([padded[0], -padded[1]])
    column_back = np.einsum("asyk,wx->kawsyx", signed, eye8)
    column_back = column_back.reshape(768, 8, 256).transpose(1, 0, 2)
    cos_x, sin_x = angle_tables(NX, waves(NX, KX))
    shape = (GX, 2, 2, 8, KX)
    cos_x = cos_x.reshape(shape).transpose(1, 0, 2, 3, 4)
    sin_x = sin_x.reshape(shape).transpose(1, 0, 2, 3, 4)
    row = np.zeros((2, GX, 2, 8, 2, 2, 64), np.float32)
    row_back = np.zeros_like(row)
    for xb in range(2):
        c, s = cos_x[:, :, xb], sin_x[:, :, xb]
        row[:, :, 0, :, xb, 0, :KX] = c
        row[:, :, 1, :, xb, 0, :KX] = s
        row[:, :, 0, :, xb, 1, :KX] = -s
        row[:, :, 1, :, xb, 1, :KX] = c
        row_back[:, :, 0, :, xb, 0, :KX] = c
        row_back[:, :, 0, :, xb, 1, :KX] = -s
        row_back[:, :, 1, :, xb, 0, :KX] = s
        row_back[:, :, 1, :, xb, 1, :KX] = c
    row = row.reshape(256, 256)
    row_back = row_back.reshape(256, 256)
    row_high = rounded(row_back)
    row_low = rounded(row_back - row_high.astype(np.float32))
    return (
        rounded(deep0),
        rounded(deep1),
        rounded(column),
        rounded(row),
        np.stack([row_high, row_low]),
        rounded(column_back),
        rounded(rise0),
        rounded(rise1),
    )


def dot_nt(a, b):
    return lax.dot_general(a, b, (((1,), (1,)), ((), ())), preferred_element_type=F32)


def dot_nn(a, b):
    return lax.dot_general(a, b, (((1,), (0,)), ((), ())), preferred_element_type=F32)


def kernel(
    fields_hbm, cots_hbm, w_ref, bias_ref, spectral_hbm,
    deep0_hbm, deep1_hbm, column_hbm, row_hbm, row_back_hbm, column_back_hbm, rise0_hbm, rise1_hbm,
    act_hbm, trained_hbm,
    fields, cots, cells, packed, weights, act,
    deep0, deep1, column, row, row_back, column_back, rise0, rise1,
    send_a, recv_a, send_b, recv_b, back_b, got_b, back_a, got_a,
    xs, spectra, xi, turned, lifted, branch, kron,
    load_sems, out_sems,
    a_send, a_recv, b_send, b_recv, bb_send, bb_recv, ba_send, ba_recv,
):
    gx = lax.axis_index("gx")
    gy = lax.axis_index("gy")
    me = gx * GY + gy
    my_half = gy // 8
    my_group = gy % 8

    loads = [
        (fields_hbm.at[0], fields.at[0, :, pl.ds(0, 15)]),
        (deep0_hbm, deep0),
        (deep1_hbm, deep1),
        (column_hbm, column),
        (fields_hbm.at[1], fields.at[1, :, pl.ds(0, 15)]),
        (row_hbm, row),
        (spectral_hbm, packed),
        (row_back_hbm, row_back),
        (column_back_hbm, column_back),
        (rise0_hbm, rise0),
        (rise1_hbm, rise1),
        (cots_hbm, cots.at[:, :, pl.ds(0, 15)]),
    ]
    copies = [
        pltpu.make_async_copy(src, dst, load_sems.at[n]) for n, (src, dst) in enumerate(loads)
    ]
    for copy in copies[:3]:
        copy.start()
    for step in range(2):
        fields[step, :, 15] = jnp.zeros((C, 32, 128), BF)
        cots[step, :, 15] = jnp.zeros((C, 32, 128), BF)

    barrier = pltpu.get_barrier_semaphore()

    def greet(d, _):
        other = lax.rem(me + d, GX * GY)
        pl.semaphore_signal(
            barrier, inc=1, device_id=(other // GY, lax.rem(other, GY)), device_id_type=MESH
        )
        return 0

    lax.fori_loop(1, GX * GY, greet, 0)

    wide = lax.broadcasted_iota(jnp.int32, (C * 16, C), 0) // 16
    spread = (wide == lax.broadcasted_iota(jnp.int32, (C * 16, C), 1)).astype(BF)
    grown = dot_nt(dot_nn(spread, w_ref[...]).astype(BF), spread)
    same = lax.rem(lax.broadcasted_iota(jnp.int32, (C * 16, C * 16), 0), 16) == lax.rem(
        lax.broadcasted_iota(jnp.int32, (C * 16, C * 16), 1), 16
    )
    kron[...] = jnp.where(same, grown, 0.0).astype(BF)
    xi[...] = jnp.zeros_like(xi)

    def pad_cells(step):
        def one(c, _):
            value = fields[step, c].astype(F32).reshape(16, 4, 8, 128)
            for block in range(4):
                cells[step, c, block] = value[:, block].reshape(128, 128).astype(BF)
            return 0

        lax.fori_loop(0, C, one, 0)

    def deep_half(f, step, xh):
        for xb in range(2):
            def block(c):
                return cells[step, c, xh * 2 + xb]

            o0 = dot_nt(deep0[...], jnp.concatenate([block(c) for c in range(8)], axis=1))
            o1 = dot_nt(deep0[...], jnp.concatenate([block(c) for c in range(8, 16)], axis=1))
            o2 = dot_nt(deep1[...], jnp.concatenate([block(c) for c in range(16, 20)], axis=1))
            for group in range(8):
                for part in range(2):
                    a = group * 48 + part * 24
                    b = group * 32 + part * 16
                    send_a[f, xh * 8 + group, part, xb] = jnp.concatenate(
                        [o0[a : a + 24], o1[a : a + 24], o2[b : b + 16]], axis=0
                    ).astype(BF)

    def a_copy(f, target):
        return pltpu.make_async_remote_copy(
            src_ref=send_a.at[f, target],
            dst_ref=recv_a.at[f, gy],
            send_sem=a_send.at[f],
            recv_sem=a_recv.at[f],
            device_id=(gx, target),
            device_id_type=MESH,
        )

    def send_a_half(f, xh):
        def one(k, _):
            target = xh * 8 + lax.rem(my_group + 1 + k, 8)

            @pl.when(target == gy)
            def _():
                pltpu.make_async_copy(send_a.at[f, target], recv_a.at[f, gy], a_recv.at[f]).start()

            @pl.when(target != gy)
            def _():
                a_copy(f, target).start()

            return 0

        lax.fori_loop(0, 8, one, 0)

    def wait_all(ref, sem):
        pltpu.make_async_copy(ref, ref, sem).wait()

    def b_target(ky):
        group = lax.rem(ky, 6) * 8 + my_group
        return ky // 6, group // 3, lax.rem(group, 3)

    def b_copy(f, ky):
        other_x, other_y, slot = b_target(ky)
        return pltpu.make_async_remote_copy(
            src_ref=send_b.at[f, ky],
            dst_ref=recv_b.at[f, slot, my_half, gx],
            send_sem=b_send.at[f],
            recv_sem=b_recv.at[f],
            device_id=(other_x, other_y),
            device_id_type=MESH,
        )

    def columns(f):
        data = jnp.concatenate(
            [recv_a[f, s].reshape(256, 128) for s in range(GY)], axis=1
        )
        for part in range(2):
            out = dot_nt(column[part], data)
            real = out[:192, :128] + out[192:, 128:]
            imag = out[:192, 128:] - out[192:, :128]
            send_b[f, pl.ds(part * 24, 24)] = jnp.concatenate(
                [real.reshape(24, 8, 128), imag.reshape(24, 8, 128)], axis=1
            ).astype(BF)

            def one(k, _):
                ky = part * 24 + lax.rem(gx * 6 + gy + k, 24)
                other_x, other_y, slot = b_target(ky)
                mine = jnp.logical_and(other_x == gx, other_y == gy)

                @pl.when(mine)
                def _():
                    pltpu.make_async_copy(
                        send_b.at[f, ky], recv_b.at[f, slot, my_half, gx], b_recv.at[f]
                    ).start()

                @pl.when(jnp.logical_not(mine))
                def _():
                    b_copy(f, ky).start()

                return 0

            lax.fori_loop(0, 24, one, 0)

    def rows_forward(f):
        pieces = []
        for slot in range(3):
            data = recv_b[f, slot].reshape(256, 128)
            out = dot_nn(data.T, row[...])
            xs[slot] = out[0:64, 0:128] + out[64:128, 128:256]
            for kz in range(3):
                pieces.append(xs[slot, pl.ds(kz, C, stride=3), :])
        spectra[f, 0] = jnp.concatenate([piece[:, 0:48] for piece in pieces], axis=1)
        spectra[f, 1] = jnp.concatenate([piece[:, 64:112] for piece in pieces], axis=1)

    pair = lax.broadcasted_iota(jnp.int32, (1, 432), 1) // KX + me * 9
    scale = jnp.where(lax.rem(pair, KZ) == 0, 1.0, 2.0).astype(F32) * INVERSE_TOTAL

    def mix(f, update):
        if update is not None:
            field_f, grad_f = update
            grad_re = spectra[grad_f, 0] * scale * LEARN_RATE
            grad_im = spectra[grad_f, 1] * scale * LEARN_RATE

        def one(i, carry):
            w_re, w_im = weights[0, i], weights[1, i]
            if update is not None:
                in_re = spectra[field_f, 0, pl.ds(i, 1), :]
                in_im = spectra[field_f, 1, pl.ds(i, 1), :]
                w_re = w_re - (in_re * grad_re + in_im * grad_im)
                w_im = w_im - (in_re * grad_im - in_im * grad_re)
                weights[0, i] = w_re
                weights[1, i] = w_im
            if f is None:
                return carry
            re, im = carry
            s_re = spectra[f, 0, pl.ds(i, 1), :]
            s_im = spectra[f, 1, pl.ds(i, 1), :]
            return re + (w_re * s_re - w_im * s_im), im + (w_re * s_im + w_im * s_re)

        zero = jnp.zeros((C, 432), F32)
        return lax.fori_loop(0, C, one, (zero, zero))

    def bb_copy(step, slot, n):
        group = gy * 3 + slot
        return pltpu.make_async_remote_copy(
            src_ref=back_b.at[step, slot, n],
            dst_ref=got_b.at[step, gx * 6 + group // 8],
            send_sem=bb_send.at[step],
            recv_sem=bb_recv.at[step],
            device_id=(lax.rem(n, 8), (n // 8) * 8 + lax.rem(group, 8)),
            device_id_type=MESH,
        )

    def rows_inverse(step, mixed):
        re, im = mixed
        gap = jnp.zeros((C, 16), F32)
        for slot in range(3):
            for kz in range(3):
                a = (slot * 3 + kz) * 48
                xi[slot, pl.ds(kz, C, stride=3), :] = jnp.concatenate(
                    [re[:, a : a + 48], gap, im[:, a : a + 48], gap], axis=1
                )
            value = xi[slot]
            high = value.astype(BF)
            low = (value - high.astype(F32)).astype(BF)
            none = jnp.zeros((64, 128), BF)

            def both(v):
                return jnp.concatenate(
                    [jnp.concatenate([v, none], axis=1), jnp.concatenate([none, v], axis=1)],
                    axis=0,
                )

            high, low = both(high), both(low)
            out = dot_nt(row_back[0], high) + (dot_nt(row_back[0], low) + dot_nt(row_back[1], high))
            back_b[step, slot] = (out * INVERSE_TOTAL).astype(BF).reshape(16, 16, 128)
            group = gy * 3 + slot

            def one(k, _):
                n = lax.rem(gx + gy + k, 16)
                mine = jnp.logical_and(
                    lax.rem(n, 8) == gx, (n // 8) * 8 + lax.rem(group, 8) == gy
                )

                @pl.when(mine)
                def _():
                    pltpu.make_async_copy(
                        back_b.at[step, slot, n],
                        got_b.at[step, gx * 6 + group // 8],
                        bb_recv.at[step],
                    ).start()

                @pl.when(jnp.logical_not(mine))
                def _():
                    bb_copy(step, slot, n).start()

                return 0

            lax.fori_loop(0, 16, one, 0)

    def ba_copy(step, target):
        return pltpu.make_async_remote_copy(
            src_ref=back_a.at[step, target],
            dst_ref=got_a.at[step, gy],
            send_sem=ba_send.at[step],
            recv_sem=ba_recv.at[step, my_half],
            device_id=(gx, target),
            device_id_type=MESH,
        )

    def columns_inverse(step):
        data = got_b[step].astype(F32)
        swapped = jnp.concatenate([data[:, 8:16], -data[:, 0:8]], axis=1)
        turned[0:128, :] = data.reshape(768, 128).astype(BF).T
        turned[128:256, :] = swapped.reshape(768, 128).astype(BF).T

        def one(k, _):
            duo = lax.rem(gy // 2 + 1 + k, 8)
            out = dot_nn(turned[...], column_back[duo]).astype(BF)
            for j in range(2):
                target = duo * 2 + j
                back_a[step, target] = out[:, j * 128 : j * 128 + 128].reshape(2, 2, 64, 128)

                @pl.when(target == gy)
                def _():
                    pltpu.make_async_copy(
                        back_a.at[step, target], got_a.at[step, gy], ba_recv.at[step, my_half]
                    ).start()

                @pl.when(target != gy)
                def _():
                    ba_copy(step, target).start()

            return 0

        lax.fori_loop(0, 8, one, 0)

    def deep_inverse(step, xh):
        wait_all(got_a.at[step, pl.ds(xh * 8, 8)], ba_recv.at[step, xh])
        for xb in range(2):
            first = jnp.concatenate(
                [got_a[step, xh * 8 + g, p, xb, 0:48] for g in range(8) for p in range(2)], axis=0
            )
            second = jnp.concatenate(
                [got_a[step, xh * 8 + g, p, xb, 48:64] for g in range(8) for p in range(2)], axis=0
            )
            lifted[xb * 128 : xb * 128 + 128, 0:768] = first.T
            lifted[xb * 128 : xb * 128 + 128, 768:1024] = second.T

        def save(out, c):
            for j in range(2):
                branch[c + j, pl.ds(xh * 2, 2)] = (
                    out[:, j * 128 : j * 128 + 128].astype(BF).reshape(2, 128, 128)
                )

        def one(k, _):
            save(dot_nn(lifted[:, 0:768], rise0[k]), 2 * k)
            return 0

        lax.fori_loop(0, 8, one, 0)
        for k in range(2):
            save(dot_nn(lifted[:, 768:1024], rise1[k]), 16 + 2 * k)

    def pointwise(step, xh, last):
        def one(k, _):
            rows = pl.ds(k * 16, 16)
            data = jnp.concatenate(
                [
                    jnp.concatenate([cells[step, c, xh * 2 + xb, rows] for c in range(C)], axis=0)
                    for xb in range(2)
                ],
                axis=1,
            )
            pre = dot_nn(kron[...], data)
            for o in range(C):
                cot = cots[step, o, pl.ds(2 * k, 2), xh * 16 : xh * 16 + 16].astype(F32)
                cot = cot.reshape(2, 2, 8, 128)
                outs = []
                for xb in range(2):
                    v = pre[o * 16 : o * 16 + 16, xb * 128 : xb * 128 + 128]
                    v = v + (branch[o, xh * 2 + xb, rows].astype(F32) + bias_ref[o])
                    square = v * v
                    half = 0.5 + 0.5 * jnp.tanh(v * (GELU_K + (GELU_K * GELU_C) * square))
                    slope = half + (half * (1.0 - half)) * (
                        v * (2.0 * GELU_K + (6.0 * GELU_K * GELU_C) * square)
                    )
                    cells[step, o, xh * 2 + xb, rows] = (
                        cot[:, xb].reshape(16, 128) * slope
                    ).astype(BF)
                    outs.append((v * half).reshape(2, 8, 128))
                if last:
                    act[o, pl.ds(2 * k, 2), xh * 16 : xh * 16 + 16] = jnp.concatenate(
                        outs, axis=1
                    ).astype(BF)
            return 0

        lax.fori_loop(0, 8, one, 0)

    def all_a_sent(f):
        def one(k, _):
            @pl.when(k != gy)
            def _():
                a_copy(f, k).wait_send()

            return 0

        lax.fori_loop(0, GY, one, 0)

    def all_b_sent(f):
        def one(ky, _):
            other_x, other_y, slot = b_target(ky)

            @pl.when(jnp.logical_not(jnp.logical_and(other_x == gx, other_y == gy)))
            def _():
                b_copy(f, ky).wait_send()

            return 0

        lax.fori_loop(0, KY, one, 0)

    def all_ba_sent(step):
        def one(k, _):
            @pl.when(k != gy)
            def _():
                ba_copy(step, k).wait_send()

            return 0

        lax.fori_loop(0, GY, one, 0)

    def all_bb_sent(step):
        for slot in range(3):
            group = gy * 3 + slot

            def one(n, _):
                mine = jnp.logical_and(
                    lax.rem(n, 8) == gx, (n // 8) * 8 + lax.rem(group, 8) == gy
                )

                @pl.when(jnp.logical_not(mine))
                def _():
                    bb_copy(step, slot, n).wait_send()

                return 0

            lax.fori_loop(0, 16, one, 0)

    def mix_and_return(step, f, update):
        rows_inverse(step, mix(f, update))

    def wait_a(f):
        wait_all(recv_a.at[f], a_recv.at[f])

    def wait_b(f):
        wait_all(recv_b.at[f], b_recv.at[f])

    def wait_bb(step):
        wait_all(got_b.at[step], bb_recv.at[step])

    def start():
        copies[0].wait()
        for copy in copies[3:]:
            copy.start()
        pad_cells(0)
        copies[1].wait()
        copies[2].wait()

    def unpack_weights():
        def one(i, _):
            for part in range(2):
                weights[part, i] = packed[i, :, part, :]
            return 0

        lax.fori_loop(0, C, one, 0)

    def pack_weights():
        def one(i, _):
            for part in range(2):
                packed[i, :, part, :] = weights[part, i]
            return 0

        lax.fori_loop(0, C, one, 0)

    def meet():
        pl.semaphore_wait(barrier, GX * GY - 1)

    def load_second():
        copies[4].wait()
        pad_cells(1)

    def loaded(*numbers):
        for n in numbers:
            copies[n].wait()

    def act_copy():
        return pltpu.make_async_copy(act.at[:, pl.ds(0, 15)], act_hbm, out_sems.at[0])

    def act_start():
        act_copy().start()

    schedule = [
        (start,),
        (deep_half, 0, 0, 0),
        (meet,),
        (send_a_half, 0, 0),
        (deep_half, 0, 0, 1),
        (send_a_half, 0, 1),
        (load_second,),
        (deep_half, 1, 1, 0),
        (deep_half, 1, 1, 1),
        (loaded, 6),
        (unpack_weights,),
        (wait_a, 0),
        (send_a_half, 1, 0),
        (send_a_half, 1, 1),
        (loaded, 3),
        (columns, 0),
        (loaded, 5, 7),
        (wait_b, 0),
        (rows_forward, 0),
        (mix_and_return, 0, 0, None),
        (loaded, 8),
        (wait_bb, 0),
        (columns_inverse, 0),
        (wait_a, 1),
        (columns, 1),
        (loaded, 9, 10, 11),
        (deep_inverse, 0, 0),
        (pointwise, 0, 0, False),
        (deep_half, 2, 0, 0),
        (send_a_half, 2, 0),
        (deep_inverse, 0, 1),
        (pointwise, 0, 1, False),
        (deep_half, 2, 0, 1),
        (send_a_half, 2, 1),
        (wait_b, 1),
        (rows_forward, 1),
        (wait_a, 2),
        (columns, 2),
        (wait_b, 2),
        (rows_forward, 2),
        (mix_and_return, 1, 1, (0, 2)),
        (wait_bb, 1),
        (columns_inverse, 1),
        (deep_inverse, 1, 0),
        (pointwise, 1, 0, True),
        (deep_half, 3, 1, 0),
        (send_a_half, 3, 0),
        (deep_inverse, 1, 1),
        (pointwise, 1, 1, True),
        (deep_half, 3, 1, 1),
        (send_a_half, 3, 1),
        (act_start,),
        (wait_a, 3),
        (columns, 3),
        (wait_b, 3),
        (rows_forward, 3),
        (mix, None, (1, 3)),
        (pack_weights,),
    ]
    for stage, *numbers in schedule:
        stage(*numbers)
    trained_out = pltpu.make_async_copy(packed, trained_hbm, out_sems.at[1])
    trained_out.start()

    for f in range(4):
        all_a_sent(f)
        all_b_sent(f)
    for step in range(2):
        all_ba_sent(step)
        all_bb_sent(step)
    act_copy().wait()
    trained_out.wait()


def shards(fields, cotangents, w_point, bias_vector, spectral):
    tables = [jnp.asarray(table) for table in make_tables()]
    anywhere = pl.BlockSpec(memory_space=pl.ANY)
    vmem = pltpu.VMEM
    fields = jnp.transpose(fields, (0, 1, 3, 2, 4))
    cotangents = jnp.transpose(cotangents, (0, 1, 3, 2, 4))
    spectral = jnp.transpose(spectral, (1, 2, 0, 3))
    grid_shape = (C, 16, 32, 128)
    dma = pltpu.SemaphoreType.DMA
    scratch = [
        vmem((2,) + grid_shape, BF),
        vmem((2,) + grid_shape, BF),
        vmem((2, C, 4, 128, 128), BF),
        vmem((C, C, 2, 432), F32),
        vmem((2, C, C, 432), F32),
        vmem(grid_shape, BF),
    ]
    scratch += [vmem(table.shape, BF) for table in tables]
    scratch += [
        vmem((4, GY, 2, 2, 64, 128), BF),
        vmem((4, GY, 2, 2, 64, 128), BF),
        vmem((4, KY, 16, 128), BF),
        vmem((4, 3, 2, GX, 16, 128), BF),
        vmem((2, 3, 16, 16, 128), BF),
        vmem((2, KY, 16, 128), BF),
        vmem((2, GY, 2, 2, 64, 128), BF),
        vmem((2, GY, 2, 2, 64, 128), BF),
        vmem((3, 64, 128), F32),
        vmem((4, 2, C, 432), F32),
        vmem((3, 64, 128), F32),
        vmem((256, 768), BF),
        vmem((256, 1024), BF),
        vmem((C, 4, 128, 128), BF),
        vmem((C * 16, C * 16), BF),
        dma((12,)),
        dma((2,)),
        dma((4,)),
        dma((4,)),
        dma((4,)),
        dma((4,)),
        dma((2,)),
        dma((2,)),
        dma((2,)),
        dma((2, 2)),
    ]
    act, trained = pl.pallas_call(
        kernel,
        out_shape=(
            jax.ShapeDtypeStruct((C, 15, 32, 128), BF),
            jax.ShapeDtypeStruct((C, C, 2, 432), F32),
        ),
        in_specs=[
            anywhere,
            anywhere,
            pl.BlockSpec(memory_space=pltpu.VMEM),
            pl.BlockSpec(memory_space=pltpu.SMEM),
            anywhere,
        ]
        + [anywhere] * len(tables),
        out_specs=(anywhere, anywhere),
        scratch_shapes=scratch,
        compiler_params=pltpu.CompilerParams(
            collective_id=0, has_side_effects=True, vmem_limit_bytes=62 * 1024 * 1024
        ),
    )(fields, cotangents, w_point, bias_vector, spectral, *tables)
    return jnp.transpose(act, (0, 2, 1, 3)), jnp.transpose(trained, (2, 0, 1, 3))


def solution(mesh):
    return jax.shard_map(
        shards,
        mesh=mesh,
        in_specs=(
            P(None, None, "gx", "gy", None),
            P(None, None, "gx", "gy", None),
            P(),
            P(),
            P(None, None, None, ("gx", "gy")),
        ),
        out_specs=(P(None, "gx", "gy", None), P(None, None, None, ("gx", "gy"))),
        check_vma=False,
    )
```

```python
import functools
import math

import jax
import jax.numpy as jnp
import ml_dtypes
import numpy as np
from jax import lax
from jax.experimental import pallas as pl
from jax.experimental.pallas import tpu as pltpu
from jax.sharding import PartitionSpec as P

C = 20
NX, NY, NZ = 256, 240, 128
KX, KY, KZ = 48, 48, 24
GX, GY = 8, 16
LEARN_RATE = 0.1
INVERSE_TOTAL = 1.0 / (NX * NY * NZ)
BF = jnp.bfloat16
F32 = jnp.float32
MESH = pl.DeviceIdType.MESH
GELU_K = math.sqrt(2.0 / math.pi)
GELU_C = 0.044715


def waves(length, kept):
    index = np.arange(kept)
    return np.where(index < kept // 2, index, index - kept + length)


def angle_tables(length, freqs):
    product = (np.arange(length)[:, None] * freqs[None, :]) % length
    angle = product.astype(np.float32) * np.float32(2.0 * math.pi / length)
    return np.cos(angle), np.sin(angle)


def rounded(table):
    return table.astype(ml_dtypes.bfloat16)


def make_tables():
    cos_z, sin_z = angle_tables(NZ, np.arange(KZ))
    both = np.stack([cos_z, -sin_z]).transpose(0, 2, 1)
    both = both.reshape(2, 8, 3, NZ).transpose(1, 0, 2, 3)
    deep0 = np.einsum("gpkz,nm->gpnkmz", both, np.eye(8, dtype=np.float32)).reshape(384, 1024)
    deep1 = np.zeros((8, 2, 16, 4, NZ), np.float32)
    deep1[:, :, :12] = np.einsum("gpkz,nm->gpnkmz", both, np.eye(4, dtype=np.float32)).reshape(
        8, 2, 12, 4, NZ
    )
    deep1 = deep1.reshape(256, 512)
    factor = np.where(np.arange(KZ) == 0, 1.0, 2.0).astype(np.float32)
    back = np.stack([cos_z * factor, -sin_z * factor]).transpose(0, 2, 1)
    back = back.reshape(2, 8, 3, NZ).transpose(1, 0, 2, 3)
    rise0 = np.einsum("gpkz,nm->gpnkmz", back, np.eye(16, dtype=np.float32))
    rise0 = rise0.reshape(768, 8, 256).transpose(1, 0, 2)
    rise1 = np.zeros((8, 2, 16, 4, NZ), np.float32)
    rise1[:, :, :12] = np.einsum("gpkz,nm->gpnkmz", back, np.eye(4, dtype=np.float32)).reshape(
        8, 2, 12, 4, NZ
    )
    rise1 = rise1.reshape(256, 2, 256).transpose(1, 0, 2)
    cos_y, sin_y = angle_tables(NY, waves(NY, KY))
    padded = np.zeros((2, GY, 16, KY), np.float32)
    padded[:, :, :15] = np.stack([cos_y, sin_y]).reshape(2, GY, 15, KY)
    eye8 = np.eye(8, dtype=np.float32)
    column = np.einsum("asyk,xw->akxsyw", padded, eye8)
    column = column.reshape(2, 2, 24 * 8, 2048).transpose(1, 0, 2, 3).reshape(2, 384, 2048)
    signed = np.stack([padded[0], -padded[1]])
    column_back = np.einsum("asyk,wx->kawsyx", signed, eye8)
    column_back = column_back.reshape(768, 8, 256).transpose(1, 0, 2)
    cos_x, sin_x = angle_tables(NX, waves(NX, KX))
    shape = (GX, 2, 2, 8, KX)
    cos_x = cos_x.reshape(shape).transpose(2, 0, 1, 3, 4)
    sin_x = sin_x.reshape(shape).transpose(2, 0, 1, 3, 4)
    row = np.zeros((2, GX, 2, 8, 2, 2, 64), np.float32)
    row_back = np.zeros_like(row)
    for xb in range(2):
        c, s = cos_x[:, :, xb], sin_x[:, :, xb]
        row[:, :, 0, :, xb, 0, :KX] = c
        row[:, :, 1, :, xb, 0, :KX] = s
        row[:, :, 0, :, xb, 1, :KX] = -s
        row[:, :, 1, :, xb, 1, :KX] = c
        row_back[:, :, 0, :, xb, 0, :KX] = c
        row_back[:, :, 0, :, xb, 1, :KX] = -s
        row_back[:, :, 1, :, xb, 0, :KX] = s
        row_back[:, :, 1, :, xb, 1, :KX] = c
    row = row.reshape(256, 256)
    row_back = row_back.reshape(256, 256)
    row_high = rounded(row_back)
    row_low = rounded(row_back - row_high.astype(np.float32))
    return (
        rounded(deep0),
        rounded(deep1),
        rounded(column),
        rounded(row),
        np.stack([row_high, row_low]),
        rounded(column_back),
        rounded(rise0),
        rounded(rise1),
    )


def dot_nt(a, b):
    return lax.dot_general(a, b, (((1,), (1,)), ((), ())), preferred_element_type=F32)


def dot_nn(a, b):
    return lax.dot_general(a, b, (((1,), (0,)), ((), ())), preferred_element_type=F32)


def kernel(
    fields_hbm, cots_hbm, w_ref, bias_ref, spectral_hbm,
    deep0_hbm, deep1_hbm, column_hbm, row_hbm, row_back_hbm, column_back_hbm, rise0_hbm, rise1_hbm,
    act_hbm, trained_hbm,
    fields, cots, cells, packed, weights, act,
    deep0, deep1, column, row, row_back, column_back, rise0, rise1,
    send_a, recv_a, send_b, recv_b, back_b, got_b, back_a, got_a,
    xs, spectra, xi, turned, lifted, branch, kron,
    load_sems, out_sems, complete,
    a_send, a_recv, b_send, b_recv, bb_send, bb_recv, ba_send, ba_recv,
):
    gx = lax.axis_index("gx")
    gy = lax.axis_index("gy")
    me = gx * GY + gy
    my_half = gy // 8
    my_group = gy % 8

    loads = [
        (fields_hbm.at[0, :, :, pl.ds(0, 16)], fields.at[0, :, pl.ds(0, 15), pl.ds(0, 16)]),
        (deep0_hbm, deep0),
        (deep1_hbm, deep1),
        (column_hbm, column),
        (fields_hbm.at[1], fields.at[1, :, pl.ds(0, 15)]),
        (row_hbm, row),
        (spectral_hbm, packed),
        (row_back_hbm, row_back),
        (column_back_hbm, column_back),
        (rise0_hbm, rise0),
        (rise1_hbm, rise1),
        (cots_hbm, cots.at[:, :, pl.ds(0, 15)]),
        (fields_hbm.at[0, :, :, pl.ds(16, 16)], fields.at[0, :, pl.ds(0, 15), pl.ds(16, 16)]),
    ]
    copies = [
        pltpu.make_async_copy(src, dst, load_sems.at[n]) for n, (src, dst) in enumerate(loads)
    ]
    for n in (0, 1, 2, 12):
        copies[n].start()
    for step in range(2):
        fields[step, :, 15] = jnp.zeros((C, 32, 128), BF)
        cots[step, :, 15] = jnp.zeros((C, 32, 128), BF)

    barrier = pltpu.get_barrier_semaphore()

    def greet_line(d, _):
        pl.semaphore_signal(
            barrier, inc=1, device_id=(gx, lax.rem(gy + d, GY)), device_id_type=MESH
        )
        return 0

    def greet_plane(d, _):
        pl.semaphore_signal(
            barrier, inc=1, device_id=(lax.rem(gx + d, GX), gy), device_id_type=MESH
        )
        return 0

    lax.fori_loop(1, GY, greet_line, 0)
    lax.fori_loop(1, GX, greet_plane, 0)

    wide = lax.broadcasted_iota(jnp.int32, (C * 16, C), 0) // 16
    spread = (wide == lax.broadcasted_iota(jnp.int32, (C * 16, C), 1)).astype(BF)
    grown = dot_nt(dot_nn(spread, w_ref[...]).astype(BF), spread)
    same = lax.rem(lax.broadcasted_iota(jnp.int32, (C * 16, C * 16), 0), 16) == lax.rem(
        lax.broadcasted_iota(jnp.int32, (C * 16, C * 16), 1), 16
    )
    kron[...] = jnp.where(same, grown, 0.0).astype(BF)
    xi[...] = jnp.zeros_like(xi)

    def pad_cells(step, xb):
        def one(c, _):
            value = fields[step, c, :, xb * 16 : xb * 16 + 16].astype(F32).reshape(16, 2, 8, 128)
            for xh in range(2):
                cells[step, c, xb * 2 + xh] = value[:, xh].reshape(128, 128).astype(BF)
            return 0

        lax.fori_loop(0, C, one, 0)

    def deep_half(f, step, xb):
        for xh in range(2):
            def block(c):
                return cells[step, c, xb * 2 + xh]

            o0 = dot_nt(deep0[...], jnp.concatenate([block(c) for c in range(8)], axis=1))
            o1 = dot_nt(deep0[...], jnp.concatenate([block(c) for c in range(8, 16)], axis=1))
            o2 = dot_nt(deep1[...], jnp.concatenate([block(c) for c in range(16, 20)], axis=1))
            for group in range(8):
                for part in range(2):
                    a = group * 48 + part * 24
                    b = group * 32 + part * 16
                    send_a[f, xb, xh * 8 + group, part] = jnp.concatenate(
                        [o0[a : a + 24], o1[a : a + 24], o2[b : b + 16]], axis=0
                    ).astype(BF)

    def a_copy(f, xb, target):
        return pltpu.make_async_remote_copy(
            src_ref=send_a.at[f, xb, target],
            dst_ref=recv_a.at[f, xb, gy],
            send_sem=a_send.at[f],
            recv_sem=a_recv.at[f],
            device_id=(gx, target),
            device_id_type=MESH,
        )

    def send_a_half(f, xb):
        def one(k, _):
            a_copy(f, xb, lax.rem(gy + k, GY)).start()
            return 0

        lax.fori_loop(1, GY, one, 0)
        pltpu.make_async_copy(send_a.at[f, xb, gy], recv_a.at[f, xb, gy], a_recv.at[f]).start()

    def wait_all(ref, sem):
        pltpu.make_async_copy(ref, ref, sem).wait()

    def b_target(ky):
        group = lax.rem(ky, 6) * 8 + my_group
        return ky // 6, group // 3, lax.rem(group, 3)

    def b_copy(f, ky):
        other_x, other_y, slot = b_target(ky)
        return pltpu.make_async_remote_copy(
            src_ref=send_b.at[f, ky],
            dst_ref=recv_b.at[f, slot, my_half, gx],
            send_sem=b_send.at[f],
            recv_sem=b_recv.at[f],
            device_id=(other_x, other_y),
            device_id_type=MESH,
        )

    def columns(f):
        data = jnp.concatenate(
            [
                jnp.concatenate(
                    [recv_a[f, xb, s, p] for p in range(2) for xb in range(2)], axis=0
                )
                for s in range(GY)
            ],
            axis=1,
        )
        for part in range(2):
            out = dot_nt(column[part], data)
            real = out[:192, :128] + out[192:, 128:]
            imag = out[:192, 128:] - out[192:, :128]
            send_b[f, pl.ds(part * 24, 24)] = jnp.concatenate(
                [real.reshape(24, 8, 128), imag.reshape(24, 8, 128)], axis=1
            ).astype(BF)

            def one(k, _):
                ky = part * 24 + lax.rem(gx * 6 + gy + k, 24)
                other_x, other_y, slot = b_target(ky)
                mine = jnp.logical_and(other_x == gx, other_y == gy)

                @pl.when(mine)
                def _():
                    pltpu.make_async_copy(
                        send_b.at[f, ky], recv_b.at[f, slot, my_half, gx], b_recv.at[f]
                    ).start()

                @pl.when(jnp.logical_not(mine))
                def _():
                    b_copy(f, ky).start()

                return 0

            lax.fori_loop(0, 24, one, 0)

    def rows_forward(f):
        pieces = []
        for slot in range(3):
            data = recv_b[f, slot].reshape(256, 128)
            out = dot_nn(data.T, row[...])
            xs[slot] = out[0:64, 0:128] + out[64:128, 128:256]
            for kz in range(3):
                pieces.append(xs[slot, pl.ds(kz, C, stride=3), :])
        spectra[f, 0] = jnp.concatenate([piece[:, 0:48] for piece in pieces], axis=1)
        spectra[f, 1] = jnp.concatenate([piece[:, 64:112] for piece in pieces], axis=1)

    pair = lax.broadcasted_iota(jnp.int32, (1, 432), 1) // KX + me * 9
    scale = jnp.where(lax.rem(pair, KZ) == 0, 1.0, 2.0).astype(F32) * INVERSE_TOTAL

    def mix(f, update):
        if update is not None:
            field_f, grad_f = update
            grad_re = spectra[grad_f, 0] * scale * LEARN_RATE
            grad_im = spectra[grad_f, 1] * scale * LEARN_RATE

        def one(i, carry):
            w_re, w_im = weights[0, i], weights[1, i]
            if update is not None:
                in_re = spectra[field_f, 0, pl.ds(i, 1), :]
                in_im = spectra[field_f, 1, pl.ds(i, 1), :]
                w_re = w_re - (in_re * grad_re + in_im * grad_im)
                w_im = w_im - (in_re * grad_im - in_im * grad_re)
                weights[0, i] = w_re
                weights[1, i] = w_im
            if f is None:
                return carry
            re, im = carry
            s_re = spectra[f, 0, pl.ds(i, 1), :]
            s_im = spectra[f, 1, pl.ds(i, 1), :]
            return re + (w_re * s_re - w_im * s_im), im + (w_re * s_im + w_im * s_re)

        zero = jnp.zeros((C, 432), F32)
        return lax.fori_loop(0, C, one, (zero, zero))

    def bb_copy(step, slot, n):
        group = gy * 3 + slot
        return pltpu.make_async_remote_copy(
            src_ref=back_b.at[step, slot, n],
            dst_ref=got_b.at[step, gx * 6 + group // 8],
            send_sem=bb_send.at[step],
            recv_sem=bb_recv.at[step],
            device_id=(lax.rem(n, 8), (n // 8) * 8 + lax.rem(group, 8)),
            device_id_type=MESH,
        )

    def rows_inverse(step, mixed):
        re, im = mixed
        gap = jnp.zeros((C, 16), F32)
        for slot in range(3):
            for kz in range(3):
                a = (slot * 3 + kz) * 48
                xi[slot, pl.ds(kz, C, stride=3), :] = jnp.concatenate(
                    [re[:, a : a + 48], gap, im[:, a : a + 48], gap], axis=1
                )
            value = xi[slot]
            high = value.astype(BF)
            low = (value - high.astype(F32)).astype(BF)
            none = jnp.zeros((64, 128), BF)

            def both(v):
                return jnp.concatenate(
                    [jnp.concatenate([v, none], axis=1), jnp.concatenate([none, v], axis=1)],
                    axis=0,
                )

            high, low = both(high), both(low)
            out = dot_nt(row_back[0], high) + (dot_nt(row_back[0], low) + dot_nt(row_back[1], high))
            back_b[step, slot] = (out * INVERSE_TOTAL).astype(BF).reshape(16, 16, 128)
            group = gy * 3 + slot

            def one(k, _):
                n = lax.rem(gx + gy + k, 16)
                mine = jnp.logical_and(
                    lax.rem(n, 8) == gx, (n // 8) * 8 + lax.rem(group, 8) == gy
                )

                @pl.when(mine)
                def _():
                    pltpu.make_async_copy(
                        back_b.at[step, slot, n],
                        got_b.at[step, gx * 6 + group // 8],
                        bb_recv.at[step],
                    ).start()

                @pl.when(jnp.logical_not(mine))
                def _():
                    bb_copy(step, slot, n).start()

                return 0

            lax.fori_loop(0, 16, one, 0)

    def ba_copy(step, xb, target):
        return pltpu.make_async_remote_copy(
            src_ref=back_a.at[step, xb, target],
            dst_ref=got_a.at[step, xb, gy],
            send_sem=ba_send.at[step],
            recv_sem=ba_recv.at[step, xb],
            device_id=(gx, target),
            device_id_type=MESH,
        )

    def send_ba(step, xb, target):
        @pl.when(target == gy)
        def _():
            pltpu.make_async_copy(
                back_a.at[step, xb, target], got_a.at[step, xb, gy], ba_recv.at[step, xb]
            ).start()

        @pl.when(target != gy)
        def _():
            ba_copy(step, xb, target).start()

    def send_ba_half(step, xb):
        def one(k, _):
            send_ba(step, xb, lax.rem(gy + 1 + k, GY))
            return 0

        lax.fori_loop(0, GY, one, 0)

    def columns_inverse(step):
        data = got_b[step].astype(F32)
        swapped = jnp.concatenate([data[:, 8:16], -data[:, 0:8]], axis=1)
        turned[0:128, :] = data.reshape(768, 128).astype(BF).T
        turned[128:256, :] = swapped.reshape(768, 128).astype(BF).T

        def one(k, _):
            duo = lax.rem(gy // 2 + 1 + k, 8)
            out = dot_nn(turned[...], column_back[duo]).astype(BF)
            for j in range(2):
                target = duo * 2 + j
                value = out[:, j * 128 : j * 128 + 128].reshape(2, 2, 64, 128)
                for xb in range(2):
                    back_a[step, xb, target] = value[:, xb]
                send_ba(step, 0, target)
            return 0

        lax.fori_loop(0, 8, one, 0)

    def deep_inverse(step, xb):
        wait_all(got_a.at[step, xb], ba_recv.at[step, xb])
        for xh in range(2):
            sources = [(xh * 8 + g, p) for g in range(8) for p in range(2)]
            first = jnp.concatenate([got_a[step, xb, t, p, 0:48] for t, p in sources], axis=0)
            second = jnp.concatenate([got_a[step, xb, t, p, 48:64] for t, p in sources], axis=0)
            lifted[xh * 128 : xh * 128 + 128, 0:768] = first.T
            lifted[xh * 128 : xh * 128 + 128, 768:1024] = second.T

        def save(out, c):
            for j in range(2):
                branch[c + j, pl.ds(xb * 2, 2)] = (
                    out[:, j * 128 : j * 128 + 128].astype(BF).reshape(2, 128, 128)
                )

        def one(k, _):
            save(dot_nn(lifted[:, 0:768], rise0[k]), 2 * k)
            return 0

        lax.fori_loop(0, 8, one, 0)
        for k in range(2):
            save(dot_nn(lifted[:, 768:1024], rise1[k]), 16 + 2 * k)

    def pointwise(step, part, last):
        def one(k, _):
            rows = pl.ds(k * 16, 16)
            data = jnp.concatenate(
                [
                    jnp.concatenate([cells[step, c, part * 2 + xh, rows] for c in range(C)], axis=0)
                    for xh in range(2)
                ],
                axis=1,
            )
            pre = dot_nn(kron[...], data)
            for o in range(C):
                cot = cots[step, o, pl.ds(2 * k, 2), part * 16 : part * 16 + 16].astype(F32)
                cot = cot.reshape(2, 2, 8, 128)
                outs = []
                for xh in range(2):
                    v = pre[o * 16 : o * 16 + 16, xh * 128 : xh * 128 + 128]
                    v = v + (branch[o, part * 2 + xh, rows].astype(F32) + bias_ref[o])
                    square = v * v
                    half = 0.5 + 0.5 * jnp.tanh(v * (GELU_K + (GELU_K * GELU_C) * square))
                    slope = half + (half * (1.0 - half)) * (
                        v * (2.0 * GELU_K + (6.0 * GELU_K * GELU_C) * square)
                    )
                    cells[step, o, part * 2 + xh, rows] = (
                        cot[:, xh].reshape(16, 128) * slope
                    ).astype(BF)
                    outs.append((v * half).reshape(2, 8, 128))
                if last:
                    act[o, pl.ds(2 * k, 2), part * 16 : part * 16 + 16] = jnp.concatenate(
                        outs, axis=1
                    ).astype(BF)
            return 0

        lax.fori_loop(0, 8, one, 0)

    def all_a_sent(f):
        def one(k, _):
            for xb in range(2):
                a_copy(f, xb, lax.rem(gy + k, GY)).wait_send()
            return 0

        lax.fori_loop(1, GY, one, 0)

    def all_b_sent(f):
        def one(ky, _):
            other_x, other_y, slot = b_target(ky)

            @pl.when(jnp.logical_not(jnp.logical_and(other_x == gx, other_y == gy)))
            def _():
                b_copy(f, ky).wait_send()

            return 0

        lax.fori_loop(0, KY, one, 0)

    def all_ba_sent(step):
        def one(k, _):
            for xb in range(2):
                ba_copy(step, xb, lax.rem(gy + k, GY)).wait_send()
            return 0

        lax.fori_loop(1, GY, one, 0)

    def all_bb_sent(step):
        for slot in range(3):
            group = gy * 3 + slot

            def one(n, _):
                mine = jnp.logical_and(
                    lax.rem(n, 8) == gx, (n // 8) * 8 + lax.rem(group, 8) == gy
                )

                @pl.when(jnp.logical_not(mine))
                def _():
                    bb_copy(step, slot, n).wait_send()

                return 0

            lax.fori_loop(0, 16, one, 0)

    def mix_and_return(step, f, update):
        rows_inverse(step, mix(f, update))

    def wait_a(f):
        wait_all(recv_a.at[f], a_recv.at[f])

    def wait_b(f):
        wait_all(recv_b.at[f], b_recv.at[f])

    def wait_bb(step):
        wait_all(got_b.at[step], bb_recv.at[step])

    def start():
        copies[0].wait()
        pad_cells(0, 0)
        copies[1].wait()
        copies[2].wait()

    def start_rest():
        copies[12].wait()
        for n in range(3, 12):
            copies[n].start()
        pad_cells(0, 1)

    def unpack_weights():
        def one(i, _):
            for part in range(2):
                weights[part, i] = packed[i, :, part, :]
            return 0

        lax.fori_loop(0, C, one, 0)

    def pack_weights():
        def one(i, _):
            for part in range(2):
                packed[i, :, part, :] = weights[part, i]
            return 0

        lax.fori_loop(0, C, one, 0)

    def meet():
        pl.semaphore_wait(barrier, GX + GY - 2)

        def one(d, _):
            pl.semaphore_signal(
                complete, inc=1, device_id=(lax.rem(gx + d, GX), gy), device_id_type=MESH
            )
            return 0

        lax.fori_loop(1, GX, one, 0)

    def meet_all():
        pl.semaphore_wait(complete, GX - 1)

    def load_second():
        copies[4].wait()
        pad_cells(1, 0)
        pad_cells(1, 1)

    def loaded(*numbers):
        for n in numbers:
            copies[n].wait()

    def act_copy():
        return pltpu.make_async_copy(act.at[:, pl.ds(0, 15)], act_hbm, out_sems.at[0])

    def act_start():
        act_copy().start()

    schedule = [
        (start,),
        (deep_half, 0, 0, 0),
        (meet,),
        (send_a_half, 0, 0),
        (start_rest,),
        (deep_half, 0, 0, 1),
        (send_a_half, 0, 1),
        (load_second,),
        (deep_half, 1, 1, 0),
        (deep_half, 1, 1, 1),
        (loaded, 6),
        (unpack_weights,),
        (wait_a, 0),
        (loaded, 3),
        (meet_all,),
        (columns, 0),
        (send_a_half, 1, 0),
        (loaded, 5, 7),
        (wait_b, 0),
        (rows_forward, 0),
        (mix_and_return, 0, 0, None),
        (send_a_half, 1, 1),
        (loaded, 8),
        (wait_bb, 0),
        (columns_inverse, 0),
        (wait_a, 1),
        (columns, 1),
        (send_ba_half, 0, 1),
        (loaded, 9, 10, 11),
        (deep_inverse, 0, 0),
        (pointwise, 0, 0, False),
        (deep_half, 2, 0, 0),
        (send_a_half, 2, 0),
        (deep_inverse, 0, 1),
        (pointwise, 0, 1, False),
        (deep_half, 2, 0, 1),
        (send_a_half, 2, 1),
        (wait_b, 1),
        (rows_forward, 1),
        (wait_a, 2),
        (columns, 2),
        (wait_b, 2),
        (rows_forward, 2),
        (mix_and_return, 1, 1, (0, 2)),
        (wait_bb, 1),
        (columns_inverse, 1),
        (send_ba_half, 1, 1),
        (deep_inverse, 1, 0),
        (pointwise, 1, 0, True),
        (deep_half, 3, 1, 0),
        (send_a_half, 3, 0),
        (deep_inverse, 1, 1),
        (pointwise, 1, 1, True),
        (deep_half, 3, 1, 1),
        (send_a_half, 3, 1),
        (act_start,),
        (wait_a, 3),
        (columns, 3),
        (wait_b, 3),
        (rows_forward, 3),
        (mix, None, (1, 3)),
        (pack_weights,),
    ]
    for stage, *numbers in schedule:
        stage(*numbers)
    trained_out = pltpu.make_async_copy(packed, trained_hbm, out_sems.at[1])
    trained_out.start()

    for f in range(4):
        all_a_sent(f)
        all_b_sent(f)
    for step in range(2):
        all_ba_sent(step)
        all_bb_sent(step)
    act_copy().wait()
    trained_out.wait()


def shards(fields, cotangents, w_point, bias_vector, spectral):
    tables = [jnp.asarray(table) for table in make_tables()]
    anywhere = pl.BlockSpec(memory_space=pl.ANY)
    vmem = pltpu.VMEM
    fields = jnp.transpose(fields, (0, 1, 3, 2, 4))
    cotangents = jnp.transpose(cotangents, (0, 1, 3, 2, 4))
    spectral = jnp.transpose(spectral, (1, 2, 0, 3))
    grid_shape = (C, 16, 32, 128)
    dma = pltpu.SemaphoreType.DMA
    scratch = [
        vmem((2,) + grid_shape, BF),
        vmem((2,) + grid_shape, BF),
        vmem((2, C, 4, 128, 128), BF),
        vmem((C, C, 2, 432), F32),
        vmem((2, C, C, 432), F32),
        vmem(grid_shape, BF),
    ]
    scratch += [vmem(table.shape, BF) for table in tables]
    scratch += [
        vmem((4, 2, GY, 2, 64, 128), BF),
        vmem((4, 2, GY, 2, 64, 128), BF),
        vmem((4, KY, 16, 128), BF),
        vmem((4, 3, 2, GX, 16, 128), BF),
        vmem((2, 3, 16, 16, 128), BF),
        vmem((2, KY, 16, 128), BF),
        vmem((2, 2, GY, 2, 64, 128), BF),
        vmem((2, 2, GY, 2, 64, 128), BF),
        vmem((3, 64, 128), F32),
        vmem((4, 2, C, 432), F32),
        vmem((3, 64, 128), F32),
        vmem((256, 768), BF),
        vmem((256, 1024), BF),
        vmem((C, 4, 128, 128), BF),
        vmem((C * 16, C * 16), BF),
        dma((13,)),
        dma((2,)),
        pltpu.SemaphoreType.REGULAR,
        dma((4,)),
        dma((4,)),
        dma((4,)),
        dma((4,)),
        dma((2,)),
        dma((2,)),
        dma((2,)),
        dma((2, 2)),
    ]
    act, trained = pl.pallas_call(
        kernel,
        out_shape=(
            jax.ShapeDtypeStruct((C, 15, 32, 128), BF),
            jax.ShapeDtypeStruct((C, C, 2, 432), F32),
        ),
        in_specs=[
            anywhere,
            anywhere,
            pl.BlockSpec(memory_space=pltpu.VMEM),
            pl.BlockSpec(memory_space=pltpu.SMEM),
            anywhere,
        ]
        + [anywhere] * len(tables),
        out_specs=(anywhere, anywhere),
        scratch_shapes=scratch,
        compiler_params=pltpu.CompilerParams(
            collective_id=0, has_side_effects=True, vmem_limit_bytes=62 * 1024 * 1024
        ),
    )(fields, cotangents, w_point, bias_vector, spectral, *tables)
    return jnp.transpose(act, (0, 2, 1, 3)), jnp.transpose(trained, (2, 0, 1, 3))


def solution(mesh):
    return jax.shard_map(
        shards,
        mesh=mesh,
        in_specs=(
            P(None, None, "gx", "gy", None),
            P(None, None, "gx", "gy", None),
            P(),
            P(),
            P(None, None, None, ("gx", "gy")),
        ),
        out_specs=(P(None, "gx", "gy", None), P(None, None, None, ("gx", "gy"))),
        check_vma=False,
    )
```

```python
import functools
import math

import jax
import jax.numpy as jnp
import ml_dtypes
import numpy as np
from jax import lax
from jax.experimental import pallas as pl
from jax.experimental.pallas import tpu as pltpu
from jax.sharding import PartitionSpec as P

C = 20
NX, NY, NZ = 256, 240, 128
KX, KY, KZ = 48, 48, 24
GX, GY = 8, 16
LEARN_RATE = 0.1
INVERSE_TOTAL = 1.0 / (NX * NY * NZ)
BF = jnp.bfloat16
F32 = jnp.float32
MESH = pl.DeviceIdType.MESH
GELU_K = math.sqrt(2.0 / math.pi)
GELU_C = 0.044715


def waves(length, kept):
    index = np.arange(kept)
    return np.where(index < kept // 2, index, index - kept + length)


def angle_tables(length, freqs):
    product = (np.arange(length)[:, None] * freqs[None, :]) % length
    angle = product.astype(np.float32) * np.float32(2.0 * math.pi / length)
    return np.cos(angle), np.sin(angle)


def rounded(table):
    return table.astype(ml_dtypes.bfloat16)


def make_tables():
    cos_z, sin_z = angle_tables(NZ, np.arange(KZ))
    both = np.stack([cos_z, -sin_z]).transpose(0, 2, 1)
    both = both.reshape(2, 8, 3, NZ).transpose(1, 0, 2, 3)
    deep0 = np.einsum("gpkz,nm->gpnkmz", both, np.eye(8, dtype=np.float32)).reshape(384, 1024)
    deep1 = np.zeros((8, 2, 16, 4, NZ), np.float32)
    deep1[:, :, :12] = np.einsum("gpkz,nm->gpnkmz", both, np.eye(4, dtype=np.float32)).reshape(
        8, 2, 12, 4, NZ
    )
    deep1 = deep1.reshape(256, 512)
    factor = np.where(np.arange(KZ) == 0, 1.0, 2.0).astype(np.float32)
    back = np.stack([cos_z * factor, -sin_z * factor]).transpose(0, 2, 1)
    back = back.reshape(2, 8, 3, NZ).transpose(1, 0, 2, 3)
    rise0 = np.einsum("gpkz,nm->gpnkmz", back, np.eye(16, dtype=np.float32))
    rise0 = rise0.reshape(768, 8, 256).transpose(1, 0, 2)
    rise1 = np.zeros((8, 2, 16, 4, NZ), np.float32)
    rise1[:, :, :12] = np.einsum("gpkz,nm->gpnkmz", back, np.eye(4, dtype=np.float32)).reshape(
        8, 2, 12, 4, NZ
    )
    rise1 = rise1.reshape(256, 2, 256).transpose(1, 0, 2)
    cos_y, sin_y = angle_tables(NY, waves(NY, KY))
    padded = np.zeros((2, GY, 16, KY), np.float32)
    padded[:, :, :15] = np.stack([cos_y, sin_y]).reshape(2, GY, 15, KY)
    eye8 = np.eye(8, dtype=np.float32)
    column = np.einsum("asyk,xw->akxsyw", padded, eye8)
    column = column.reshape(2, 2, 24 * 8, 2048).transpose(1, 0, 2, 3).reshape(2, 384, 2048)
    signed = np.stack([padded[0], -padded[1]])
    column_back = np.einsum("asyk,wx->kawsyx", signed, eye8)
    column_back = column_back.reshape(768, 8, 256).transpose(1, 0, 2)
    cos_x, sin_x = angle_tables(NX, waves(NX, KX))
    shape = (GX, 2, 2, 8, KX)
    cos_x = cos_x.reshape(shape).transpose(2, 0, 1, 3, 4)
    sin_x = sin_x.reshape(shape).transpose(2, 0, 1, 3, 4)
    row = np.zeros((2, GX, 2, 8, 2, 2, 64), np.float32)
    row_back = np.zeros_like(row)
    for xb in range(2):
        c, s = cos_x[:, :, xb], sin_x[:, :, xb]
        row[:, :, 0, :, xb, 0, :KX] = c
        row[:, :, 1, :, xb, 0, :KX] = s
        row[:, :, 0, :, xb, 1, :KX] = -s
        row[:, :, 1, :, xb, 1, :KX] = c
        row_back[:, :, 0, :, xb, 0, :KX] = c
        row_back[:, :, 0, :, xb, 1, :KX] = -s
        row_back[:, :, 1, :, xb, 0, :KX] = s
        row_back[:, :, 1, :, xb, 1, :KX] = c
    row = row.reshape(256, 256)
    row_back = row_back.reshape(256, 256)
    row_high = rounded(row_back)
    row_low = rounded(row_back - row_high.astype(np.float32))
    return (
        rounded(deep0),
        rounded(deep1),
        rounded(column),
        rounded(row),
        np.stack([row_high, row_low]),
        rounded(column_back),
        rounded(rise0),
        rounded(rise1),
    )


def dot_nt(a, b):
    return lax.dot_general(a, b, (((1,), (1,)), ((), ())), preferred_element_type=F32)


def dot_nn(a, b):
    return lax.dot_general(a, b, (((1,), (0,)), ((), ())), preferred_element_type=F32)


def kernel(
    fields_hbm, cots_hbm, w_ref, bias_ref, spectral_hbm,
    deep0_hbm, deep1_hbm, column_hbm, row_hbm, row_back_hbm, column_back_hbm, rise0_hbm, rise1_hbm,
    act_hbm, trained_hbm,
    fields, cots, cells, packed, weights, act,
    deep0, deep1, column, row, row_back, column_back, rise0, rise1,
    send_a, recv_a, send_b, recv_b, back_b, got_b, back_a, got_a,
    xs, spectra, xi, turned, lifted, branch, kron,
    load_sems, out_sems, complete,
    a_send, a_recv, b_send, b_recv, bb_send, bb_recv, ba_send, ba_recv,
):
    gx = lax.axis_index("gx")
    gy = lax.axis_index("gy")
    me = gx * GY + gy
    my_half = gy // 8
    my_group = gy % 8
    homes = [(ky * 8 + my_group) // 3 for ky in range(6)]
    slots = [lax.rem(ky * 8 + my_group, 3) for ky in range(6)]
    groups = [lax.rem(gy * 3 + slot, 8) for slot in range(3)]
    lines = [gx * 6 + (gy * 3 + slot) // 8 for slot in range(3)]
    own = functools.reduce(jnp.logical_or, [group == my_group for group in groups])

    loads = [
        (fields_hbm.at[0, :, :, pl.ds(0, 16)], fields.at[0, :, pl.ds(0, 15), pl.ds(0, 16)]),
        (deep0_hbm, deep0),
        (deep1_hbm, deep1),
        (column_hbm, column),
        (fields_hbm.at[1], fields.at[1, :, pl.ds(0, 15)]),
        (row_hbm, row),
        (spectral_hbm, packed),
        (row_back_hbm, row_back),
        (column_back_hbm, column_back),
        (rise0_hbm, rise0),
        (rise1_hbm, rise1),
        (cots_hbm, cots.at[:, :, pl.ds(0, 15)]),
        (fields_hbm.at[0, :, :, pl.ds(16, 16)], fields.at[0, :, pl.ds(0, 15), pl.ds(16, 16)]),
    ]
    copies = [
        pltpu.make_async_copy(src, dst, load_sems.at[n]) for n, (src, dst) in enumerate(loads)
    ]
    for n in (0, 1, 2, 12):
        copies[n].start()
    for step in range(2):
        fields[step, :, 15] = jnp.zeros((C, 32, 128), BF)
        cots[step, :, 15] = jnp.zeros((C, 32, 128), BF)

    barrier = pltpu.get_barrier_semaphore()

    def greet_line(d, _):
        pl.semaphore_signal(
            barrier, inc=1, device_id=(gx, lax.rem(gy + d, GY)), device_id_type=MESH
        )
        return 0

    def greet_plane(d, _):
        pl.semaphore_signal(
            barrier, inc=1, device_id=(lax.rem(gx + d, GX), gy), device_id_type=MESH
        )
        return 0

    lax.fori_loop(1, GY, greet_line, 0)
    lax.fori_loop(1, GX, greet_plane, 0)

    wide = lax.broadcasted_iota(jnp.int32, (C * 16, C), 0) // 16
    spread = (wide == lax.broadcasted_iota(jnp.int32, (C * 16, C), 1)).astype(BF)
    grown = dot_nt(dot_nn(spread, w_ref[...]).astype(BF), spread)
    same = lax.rem(lax.broadcasted_iota(jnp.int32, (C * 16, C * 16), 0), 16) == lax.rem(
        lax.broadcasted_iota(jnp.int32, (C * 16, C * 16), 1), 16
    )
    kron[...] = jnp.where(same, grown, 0.0).astype(BF)
    xi[...] = jnp.zeros_like(xi)

    def pad_cells(step, xb):
        def one(c, _):
            value = fields[step, c, :, xb * 16 : xb * 16 + 16].astype(F32).reshape(16, 2, 8, 128)
            for xh in range(2):
                cells[step, c, xb * 2 + xh] = value[:, xh].reshape(128, 128).astype(BF)
            return 0

        lax.fori_loop(0, C, one, 0)

    def deep_half(f, step, xb):
        for xh in range(2):
            def block(c):
                return cells[step, c, xb * 2 + xh]

            o0 = dot_nt(deep0[...], jnp.concatenate([block(c) for c in range(8)], axis=1))
            o1 = dot_nt(deep0[...], jnp.concatenate([block(c) for c in range(8, 16)], axis=1))
            o2 = dot_nt(deep1[...], jnp.concatenate([block(c) for c in range(16, 20)], axis=1))
            for group in range(8):
                for part in range(2):
                    a = group * 48 + part * 24
                    b = group * 32 + part * 16
                    send_a[f, xb, xh * 8 + group, part] = jnp.concatenate(
                        [o0[a : a + 24], o1[a : a + 24], o2[b : b + 16]], axis=0
                    ).astype(BF)

    def a_copy(f, xb, target):
        return pltpu.make_async_remote_copy(
            src_ref=send_a.at[f, xb, target],
            dst_ref=recv_a.at[f, xb, gy],
            send_sem=a_send.at[f],
            recv_sem=a_recv.at[f],
            device_id=(gx, target),
            device_id_type=MESH,
        )

    def send_a_half(f, xb):
        def one(k, _):
            a_copy(f, xb, lax.rem(gy + k, GY)).start()
            return 0

        lax.fori_loop(1, GY, one, 0)
        pltpu.make_async_copy(send_a.at[f, xb, gy], recv_a.at[f, xb, gy], a_recv.at[f]).start()

    def wait_all(ref, sem):
        pltpu.make_async_copy(ref, ref, sem).wait()

    def b_copy(f, other_x, ky):
        return pltpu.make_async_remote_copy(
            src_ref=send_b.at[f, other_x * 6 + ky],
            dst_ref=recv_b.at[f, slots[ky], my_half, gx],
            send_sem=b_send.at[f],
            recv_sem=b_recv.at[f],
            device_id=(other_x, homes[ky]),
            device_id_type=MESH,
        )

    def send_b_all(f):
        def one(d, _):
            other_x = lax.rem(gx + d, GX)
            for ky in range(6):
                b_copy(f, other_x, ky).start()
            return 0

        lax.fori_loop(1, GX, one, 0)
        for ky in range(6):

            @pl.when(homes[ky] != gy)
            def _():
                b_copy(f, gx, ky).start()

            @pl.when(homes[ky] == gy)
            def _():
                pltpu.make_async_copy(
                    send_b.at[f, gx * 6 + ky],
                    recv_b.at[f, slots[ky], my_half, gx],
                    b_recv.at[f],
                ).start()

    def columns(f):
        data = jnp.concatenate(
            [
                jnp.concatenate(
                    [recv_a[f, xb, s, p] for p in range(2) for xb in range(2)], axis=0
                )
                for s in range(GY)
            ],
            axis=1,
        )
        for part in range(2):
            out = dot_nt(column[part], data)
            real = out[:192, :128] + out[192:, 128:]
            imag = out[:192, 128:] - out[192:, :128]
            send_b[f, pl.ds(part * 24, 24)] = jnp.concatenate(
                [real.reshape(24, 8, 128), imag.reshape(24, 8, 128)], axis=1
            ).astype(BF)
        send_b_all(f)

    def rows_forward(f):
        pieces = []
        for slot in range(3):
            data = recv_b[f, slot].reshape(256, 128)
            out = dot_nn(data.T, row[...])
            xs[slot] = out[0:64, 0:128] + out[64:128, 128:256]
            for kz in range(3):
                pieces.append(xs[slot, pl.ds(kz, C, stride=3), :])
        spectra[f, 0] = jnp.concatenate([piece[:, 0:48] for piece in pieces], axis=1)
        spectra[f, 1] = jnp.concatenate([piece[:, 64:112] for piece in pieces], axis=1)

    pair = lax.broadcasted_iota(jnp.int32, (1, 432), 1) // KX + me * 9
    scale = jnp.where(lax.rem(pair, KZ) == 0, 1.0, 2.0).astype(F32) * INVERSE_TOTAL

    def mix(f, update):
        if update is not None:
            field_f, grad_f = update
            grad_re = spectra[grad_f, 0] * scale * LEARN_RATE
            grad_im = spectra[grad_f, 1] * scale * LEARN_RATE

        def one(i, carry):
            w_re, w_im = weights[0, i], weights[1, i]
            if update is not None:
                in_re = spectra[field_f, 0, pl.ds(i, 1), :]
                in_im = spectra[field_f, 1, pl.ds(i, 1), :]
                w_re = w_re - (in_re * grad_re + in_im * grad_im)
                w_im = w_im - (in_re * grad_im - in_im * grad_re)
                weights[0, i] = w_re
                weights[1, i] = w_im
            if f is None:
                return carry
            re, im = carry
            s_re = spectra[f, 0, pl.ds(i, 1), :]
            s_im = spectra[f, 1, pl.ds(i, 1), :]
            return re + (w_re * s_re - w_im * s_im), im + (w_re * s_im + w_im * s_re)

        zero = jnp.zeros((C, 432), F32)
        return lax.fori_loop(0, C, one, (zero, zero))

    def bb_copy(step, slot, other_x, xh):
        return pltpu.make_async_remote_copy(
            src_ref=back_b.at[step, slot, xh * 8 + other_x],
            dst_ref=got_b.at[step, lines[slot]],
            send_sem=bb_send.at[step],
            recv_sem=bb_recv.at[step],
            device_id=(other_x, xh * 8 + groups[slot]),
            device_id_type=MESH,
        )

    def send_bb_slot(step, slot):
        def one(d, _):
            other_x = lax.rem(gx + d, GX)
            for xh in range(2):
                bb_copy(step, slot, other_x, xh).start()
            return 0

        lax.fori_loop(1, GX, one, 0)
        for xh in range(2):

            @pl.when(xh * 8 + groups[slot] != gy)
            def _():
                bb_copy(step, slot, gx, xh).start()

            @pl.when(xh * 8 + groups[slot] == gy)
            def _():
                pltpu.make_async_copy(
                    back_b.at[step, slot, xh * 8 + gx],
                    got_b.at[step, lines[slot]],
                    bb_recv.at[step],
                ).start()

    def rows_inverse(step, mixed):
        re, im = mixed
        gap = jnp.zeros((C, 16), F32)
        for slot in range(3):
            for kz in range(3):
                a = (slot * 3 + kz) * 48
                xi[slot, pl.ds(kz, C, stride=3), :] = jnp.concatenate(
                    [re[:, a : a + 48], gap, im[:, a : a + 48], gap], axis=1
                )
            value = xi[slot]
            high = value.astype(BF)
            low = (value - high.astype(F32)).astype(BF)
            none = jnp.zeros((64, 128), BF)

            def both(v):
                return jnp.concatenate(
                    [jnp.concatenate([v, none], axis=1), jnp.concatenate([none, v], axis=1)],
                    axis=0,
                )

            high, low = both(high), both(low)
            out = dot_nt(row_back[0], high) + (dot_nt(row_back[0], low) + dot_nt(row_back[1], high))
            back_b[step, slot] = (out * INVERSE_TOTAL).astype(BF).reshape(16, 16, 128)
            send_bb_slot(step, slot)

    def ba_copy(step, xb, target):
        return pltpu.make_async_remote_copy(
            src_ref=back_a.at[step, xb, target],
            dst_ref=got_a.at[step, xb, gy],
            send_sem=ba_send.at[step],
            recv_sem=ba_recv.at[step, xb],
            device_id=(gx, target),
            device_id_type=MESH,
        )

    def send_ba(step, xb, target):
        @pl.when(target == gy)
        def _():
            pltpu.make_async_copy(
                back_a.at[step, xb, target], got_a.at[step, xb, gy], ba_recv.at[step, xb]
            ).start()

        @pl.when(target != gy)
        def _():
            ba_copy(step, xb, target).start()

    def send_ba_half(step, xb):
        def one(k, _):
            send_ba(step, xb, lax.rem(gy + 1 + k, GY))
            return 0

        lax.fori_loop(0, GY, one, 0)

    def columns_inverse(step):
        data = got_b[step].astype(F32)
        swapped = jnp.concatenate([data[:, 8:16], -data[:, 0:8]], axis=1)
        turned[0:128, :] = data.reshape(768, 128).astype(BF).T
        turned[128:256, :] = swapped.reshape(768, 128).astype(BF).T

        def one(k, _):
            duo = lax.rem(gy // 2 + 1 + k, 8)
            out = dot_nn(turned[...], column_back[duo]).astype(BF)
            for j in range(2):
                target = duo * 2 + j
                value = out[:, j * 128 : j * 128 + 128].reshape(2, 2, 64, 128)
                for xb in range(2):
                    back_a[step, xb, target] = value[:, xb]
                send_ba(step, 0, target)
            return 0

        lax.fori_loop(0, 8, one, 0)

    def deep_inverse(step, xb):
        wait_all(got_a.at[step, xb], ba_recv.at[step, xb])
        for xh in range(2):
            sources = [(xh * 8 + g, p) for g in range(8) for p in range(2)]
            first = jnp.concatenate([got_a[step, xb, t, p, 0:48] for t, p in sources], axis=0)
            second = jnp.concatenate([got_a[step, xb, t, p, 48:64] for t, p in sources], axis=0)
            lifted[xh * 128 : xh * 128 + 128, 0:768] = first.T
            lifted[xh * 128 : xh * 128 + 128, 768:1024] = second.T

        def save(out, c):
            for j in range(2):
                branch[c + j, pl.ds(xb * 2, 2)] = (
                    out[:, j * 128 : j * 128 + 128].astype(BF).reshape(2, 128, 128)
                )

        def one(k, _):
            save(dot_nn(lifted[:, 0:768], rise0[k]), 2 * k)
            return 0

        lax.fori_loop(0, 8, one, 0)
        for k in range(2):
            save(dot_nn(lifted[:, 768:1024], rise1[k]), 16 + 2 * k)

    def pointwise(step, part, last):
        def one(k, _):
            rows = pl.ds(k * 16, 16)
            data = jnp.concatenate(
                [
                    jnp.concatenate([cells[step, c, part * 2 + xh, rows] for c in range(C)], axis=0)
                    for xh in range(2)
                ],
                axis=1,
            )
            pre = dot_nn(kron[...], data)
            for o in range(C):
                cot = cots[step, o, pl.ds(2 * k, 2), part * 16 : part * 16 + 16].astype(F32)
                cot = cot.reshape(2, 2, 8, 128)
                outs = []
                for xh in range(2):
                    v = pre[o * 16 : o * 16 + 16, xh * 128 : xh * 128 + 128]
                    v = v + (branch[o, part * 2 + xh, rows].astype(F32) + bias_ref[o])
                    square = v * v
                    half = 0.5 + 0.5 * jnp.tanh(v * (GELU_K + (GELU_K * GELU_C) * square))
                    slope = half + (half * (1.0 - half)) * (
                        v * (2.0 * GELU_K + (6.0 * GELU_K * GELU_C) * square)
                    )
                    cells[step, o, part * 2 + xh, rows] = (
                        cot[:, xh].reshape(16, 128) * slope
                    ).astype(BF)
                    outs.append((v * half).reshape(2, 8, 128))
                if last:
                    act[o, pl.ds(2 * k, 2), part * 16 : part * 16 + 16] = jnp.concatenate(
                        outs, axis=1
                    ).astype(BF)
            return 0

        lax.fori_loop(0, 8, one, 0)

    def all_a_sent(f):
        for xb in range(2):
            wait_all(send_a.at[f, xb, pl.ds(0, GY - 1)], a_send.at[f])

    def all_ba_sent(step):
        for xb in range(2):
            wait_all(back_a.at[step, xb, pl.ds(0, GY - 1)], ba_send.at[step])

    def all_small_sent(sem):
        wait_all(send_b.at[0, pl.ds(0, KY - 1)], sem)

        @pl.when(jnp.logical_not(own))
        def _():
            wait_all(send_b.at[0, KY - 1], sem)

    def all_b_sent(f):
        all_small_sent(b_send.at[f])

    def all_bb_sent(step):
        all_small_sent(bb_send.at[step])

    def mix_and_return(step, f, update):
        rows_inverse(step, mix(f, update))

    def wait_a(f):
        wait_all(recv_a.at[f], a_recv.at[f])

    def wait_b(f):
        wait_all(recv_b.at[f], b_recv.at[f])

    def wait_bb(step):
        wait_all(got_b.at[step], bb_recv.at[step])

    def start():
        copies[0].wait()
        pad_cells(0, 0)
        copies[1].wait()
        copies[2].wait()

    def start_rest():
        copies[12].wait()
        for n in range(3, 12):
            copies[n].start()
        pad_cells(0, 1)

    def unpack_weights():
        def one(i, _):
            for part in range(2):
                weights[part, i] = packed[i, :, part, :]
            return 0

        lax.fori_loop(0, C, one, 0)

    def pack_weights():
        def one(i, _):
            for part in range(2):
                packed[i, :, part, :] = weights[part, i]
            return 0

        lax.fori_loop(0, C, one, 0)

    def meet():
        pl.semaphore_wait(barrier, GX + GY - 2)

        def one(d, _):
            pl.semaphore_signal(
                complete, inc=1, device_id=(lax.rem(gx + d, GX), gy), device_id_type=MESH
            )
            return 0

        lax.fori_loop(1, GX, one, 0)

    def meet_all():
        pl.semaphore_wait(complete, GX - 1)

    def load_second():
        copies[4].wait()
        pad_cells(1, 0)
        pad_cells(1, 1)

    def loaded(*numbers):
        for n in numbers:
            copies[n].wait()

    def act_copy():
        return pltpu.make_async_copy(act.at[:, pl.ds(0, 15)], act_hbm, out_sems.at[0])

    def act_start():
        act_copy().start()

    schedule = [
        (start,),
        (deep_half, 0, 0, 0),
        (meet,),
        (send_a_half, 0, 0),
        (start_rest,),
        (deep_half, 0, 0, 1),
        (send_a_half, 0, 1),
        (load_second,),
        (deep_half, 1, 1, 0),
        (deep_half, 1, 1, 1),
        (loaded, 6),
        (unpack_weights,),
        (wait_a, 0),
        (loaded, 3),
        (meet_all,),
        (columns, 0),
        (send_a_half, 1, 0),
        (loaded, 5, 7),
        (wait_b, 0),
        (rows_forward, 0),
        (mix_and_return, 0, 0, None),
        (send_a_half, 1, 1),
        (loaded, 8),
        (wait_bb, 0),
        (columns_inverse, 0),
        (wait_a, 1),
        (columns, 1),
        (send_ba_half, 0, 1),
        (loaded, 9, 10, 11),
        (deep_inverse, 0, 0),
        (pointwise, 0, 0, False),
        (deep_half, 2, 0, 0),
        (send_a_half, 2, 0),
        (deep_inverse, 0, 1),
        (pointwise, 0, 1, False),
        (deep_half, 2, 0, 1),
        (send_a_half, 2, 1),
        (wait_b, 1),
        (rows_forward, 1),
        (wait_a, 2),
        (columns, 2),
        (wait_b, 2),
        (rows_forward, 2),
        (mix_and_return, 1, 1, (0, 2)),
        (wait_bb, 1),
        (columns_inverse, 1),
        (send_ba_half, 1, 1),
        (deep_inverse, 1, 0),
        (pointwise, 1, 0, True),
        (deep_half, 3, 1, 0),
        (send_a_half, 3, 0),
        (deep_inverse, 1, 1),
        (pointwise, 1, 1, True),
        (deep_half, 3, 1, 1),
        (send_a_half, 3, 1),
        (act_start,),
        (wait_a, 3),
        (columns, 3),
        (wait_b, 3),
        (rows_forward, 3),
        (mix, None, (1, 3)),
        (pack_weights,),
    ]
    for stage, *numbers in schedule:
        stage(*numbers)
    trained_out = pltpu.make_async_copy(packed, trained_hbm, out_sems.at[1])
    trained_out.start()

    for f in range(4):
        all_a_sent(f)
        all_b_sent(f)
    for step in range(2):
        all_ba_sent(step)
        all_bb_sent(step)
    act_copy().wait()
    trained_out.wait()


def shards(fields, cotangents, w_point, bias_vector, spectral):
    tables = [jnp.asarray(table) for table in make_tables()]
    anywhere = pl.BlockSpec(memory_space=pl.ANY)
    vmem = pltpu.VMEM
    fields = jnp.transpose(fields, (0, 1, 3, 2, 4))
    cotangents = jnp.transpose(cotangents, (0, 1, 3, 2, 4))
    spectral = jnp.transpose(spectral, (1, 2, 0, 3))
    grid_shape = (C, 16, 32, 128)
    dma = pltpu.SemaphoreType.DMA
    scratch = [
        vmem((2,) + grid_shape, BF),
        vmem((2,) + grid_shape, BF),
        vmem((2, C, 4, 128, 128), BF),
        vmem((C, C, 2, 432), F32),
        vmem((2, C, C, 432), F32),
        vmem(grid_shape, BF),
    ]
    scratch += [vmem(table.shape, BF) for table in tables]
    scratch += [
        vmem((4, 2, GY, 2, 64, 128), BF),
        vmem((4, 2, GY, 2, 64, 128), BF),
        vmem((4, KY, 16, 128), BF),
        vmem((4, 3, 2, GX, 16, 128), BF),
        vmem((2, 3, 16, 16, 128), BF),
        vmem((2, KY, 16, 128), BF),
        vmem((2, 2, GY, 2, 64, 128), BF),
        vmem((2, 2, GY, 2, 64, 128), BF),
        vmem((3, 64, 128), F32),
        vmem((4, 2, C, 432), F32),
        vmem((3, 64, 128), F32),
        vmem((256, 768), BF),
        vmem((256, 1024), BF),
        vmem((C, 4, 128, 128), BF),
        vmem((C * 16, C * 16), BF),
        dma((13,)),
        dma((2,)),
        pltpu.SemaphoreType.REGULAR,
        dma((4,)),
        dma((4,)),
        dma((4,)),
        dma((4,)),
        dma((2,)),
        dma((2,)),
        dma((2,)),
        dma((2, 2)),
    ]
    act, trained = pl.pallas_call(
        kernel,
        out_shape=(
            jax.ShapeDtypeStruct((C, 15, 32, 128), BF),
            jax.ShapeDtypeStruct((C, C, 2, 432), F32),
        ),
        in_specs=[
            anywhere,
            anywhere,
            pl.BlockSpec(memory_space=pltpu.VMEM),
            pl.BlockSpec(memory_space=pltpu.SMEM),
            anywhere,
        ]
        + [anywhere] * len(tables),
        out_specs=(anywhere, anywhere),
        scratch_shapes=scratch,
        compiler_params=pltpu.CompilerParams(
            collective_id=0, has_side_effects=True, vmem_limit_bytes=62 * 1024 * 1024
        ),
    )(fields, cotangents, w_point, bias_vector, spectral, *tables)
    return jnp.transpose(act, (0, 2, 1, 3)), jnp.transpose(trained, (2, 0, 1, 3))


def solution(mesh):
    return jax.shard_map(
        shards,
        mesh=mesh,
        in_specs=(
            P(None, None, "gx", "gy", None),
            P(None, None, "gx", "gy", None),
            P(),
            P(),
            P(None, None, None, ("gx", "gy")),
        ),
        out_specs=(P(None, "gx", "gy", None), P(None, None, None, ("gx", "gy"))),
        check_vma=False,
    )
```

```python
import functools
import math

import jax
import jax.numpy as jnp
import ml_dtypes
import numpy as np
from jax import lax
from jax.experimental import pallas as pl
from jax.experimental.pallas import tpu as pltpu
from jax.sharding import PartitionSpec as P

C = 20
NX, NY, NZ = 256, 240, 128
KX, KY, KZ = 48, 48, 24
GX, GY = 8, 16
LEARN_RATE = 0.1
INVERSE_TOTAL = 1.0 / (NX * NY * NZ)
BF = jnp.bfloat16
F32 = jnp.float32
MESH = pl.DeviceIdType.MESH
GELU_K = math.sqrt(2.0 / math.pi)
GELU_C = 0.044715


def waves(length, kept):
    index = np.arange(kept)
    return np.where(index < kept // 2, index, index - kept + length)


def angle_tables(length, freqs):
    product = (np.arange(length)[:, None] * freqs[None, :]) % length
    angle = product.astype(np.float32) * np.float32(2.0 * math.pi / length)
    return np.cos(angle), np.sin(angle)


def rounded(table):
    return table.astype(ml_dtypes.bfloat16)


def make_tables():
    cos_z, sin_z = angle_tables(NZ, np.arange(KZ))
    both = np.stack([cos_z, -sin_z]).transpose(0, 2, 1)
    both = both.reshape(2, 8, 3, NZ).transpose(1, 0, 2, 3)
    deep0 = np.einsum("gpkz,nm->gpnkmz", both, np.eye(8, dtype=np.float32)).reshape(384, 1024)
    deep1 = np.zeros((8, 2, 16, 4, NZ), np.float32)
    deep1[:, :, :12] = np.einsum("gpkz,nm->gpnkmz", both, np.eye(4, dtype=np.float32)).reshape(
        8, 2, 12, 4, NZ
    )
    deep1 = deep1.reshape(256, 512)
    factor = np.where(np.arange(KZ) == 0, 1.0, 2.0).astype(np.float32)
    back = np.stack([cos_z * factor, -sin_z * factor]).transpose(0, 2, 1)
    back = back.reshape(2, 8, 3, NZ).transpose(1, 0, 2, 3)
    rise0 = np.einsum("gpkz,nm->gpnkmz", back, np.eye(16, dtype=np.float32))
    rise0 = rise0.reshape(768, 8, 256).transpose(1, 0, 2)
    rise1 = np.zeros((8, 2, 16, 4, NZ), np.float32)
    rise1[:, :, :12] = np.einsum("gpkz,nm->gpnkmz", back, np.eye(4, dtype=np.float32)).reshape(
        8, 2, 12, 4, NZ
    )
    rise1 = rise1.reshape(256, 2, 256).transpose(1, 0, 2)
    cos_y, sin_y = angle_tables(NY, waves(NY, KY))
    padded = np.zeros((2, GY, 16, KY), np.float32)
    padded[:, :, :15] = np.stack([cos_y, sin_y]).reshape(2, GY, 15, KY)
    eye8 = np.eye(8, dtype=np.float32)
    column = np.einsum("asyk,xw->akxsyw", padded, eye8)
    column = column.reshape(2, 2, 24 * 8, 2048).transpose(1, 0, 2, 3).reshape(2, 384, 2048)
    signed = np.stack([padded[0], -padded[1]])
    column_back = np.einsum("asyk,wx->kawsyx", signed, eye8)
    column_back = column_back.reshape(768, 8, 256).transpose(1, 0, 2)
    cos_x, sin_x = angle_tables(NX, waves(NX, KX))
    shape = (GX, 2, 2, 8, KX)
    cos_x = cos_x.reshape(shape).transpose(2, 0, 1, 3, 4)
    sin_x = sin_x.reshape(shape).transpose(2, 0, 1, 3, 4)
    row = np.zeros((2, GX, 2, 8, 2, 2, 64), np.float32)
    row_back = np.zeros_like(row)
    for xb in range(2):
        c, s = cos_x[:, :, xb], sin_x[:, :, xb]
        row[:, :, 0, :, xb, 0, :KX] = c
        row[:, :, 1, :, xb, 0, :KX] = s
        row[:, :, 0, :, xb, 1, :KX] = -s
        row[:, :, 1, :, xb, 1, :KX] = c
        row_back[:, :, 0, :, xb, 0, :KX] = c
        row_back[:, :, 0, :, xb, 1, :KX] = -s
        row_back[:, :, 1, :, xb, 0, :KX] = s
        row_back[:, :, 1, :, xb, 1, :KX] = c
    row = row.reshape(256, 256)
    row_back = row_back.reshape(256, 256)
    row_high = rounded(row_back)
    row_low = rounded(row_back - row_high.astype(np.float32))
    return (
        rounded(deep0),
        rounded(deep1),
        rounded(column),
        rounded(row),
        np.stack([row_high, row_low]),
        rounded(column_back),
        rounded(rise0),
        rounded(rise1),
    )


def dot_nt(a, b):
    return lax.dot_general(a, b, (((1,), (1,)), ((), ())), preferred_element_type=F32)


def dot_nn(a, b):
    return lax.dot_general(a, b, (((1,), (0,)), ((), ())), preferred_element_type=F32)


def kernel(
    fields_hbm, cots_hbm, w_ref, bias_ref, spectral_hbm,
    deep0_hbm, deep1_hbm, column_hbm, row_hbm, row_back_hbm, column_back_hbm, rise0_hbm, rise1_hbm,
    act_hbm, trained_hbm,
    fields, cots, cells, packed, weights, act,
    deep0, deep1, column, row, row_back, column_back, rise0, rise1,
    send_a, recv_a, send_b, recv_b, back_b, got_b, back_a, got_a,
    xs, spectra, xi, turned, lifted, branch, pre, kron,
    load_sems, out_sems, complete,
    a_send, a_recv, b_send, b_recv, bb_send, bb_recv, ba_send, ba_recv,
):
    gx = lax.axis_index("gx")
    gy = lax.axis_index("gy")
    me = gx * GY + gy
    my_half = gy // 8
    my_group = gy % 8
    homes = [(ky * 8 + my_group) // 3 for ky in range(6)]
    slots = [lax.rem(ky * 8 + my_group, 3) for ky in range(6)]
    groups = [lax.rem(gy * 3 + slot, 8) for slot in range(3)]
    lines = [gx * 6 + (gy * 3 + slot) // 8 for slot in range(3)]
    mates = [
        lax.rem(gy // 4 + dy, 4) * 4 + lax.rem(gy + dx, 4)
        for dy, dx in [
            (2, 2), (0, 2), (2, 0), (1, 2), (2, 1), (3, 2), (2, 3), (1, 1),
            (3, 3), (1, 3), (3, 1), (0, 1), (1, 0), (0, 3), (3, 0),
        ]
    ]
    own = functools.reduce(jnp.logical_or, [group == my_group for group in groups])

    loads = [
        (fields_hbm.at[0, :, :, pl.ds(0, 16)], fields.at[0, :, pl.ds(0, 15), pl.ds(0, 16)]),
        (deep0_hbm, deep0),
        (deep1_hbm, deep1),
        (column_hbm, column),
        (fields_hbm.at[1], fields.at[1, :, pl.ds(0, 15)]),
        (row_hbm, row),
        (spectral_hbm, packed),
        (row_back_hbm, row_back),
        (column_back_hbm, column_back),
        (rise0_hbm, rise0),
        (rise1_hbm, rise1),
        (cots_hbm, cots.at[:, :, pl.ds(0, 15)]),
        (fields_hbm.at[0, :, :, pl.ds(16, 16)], fields.at[0, :, pl.ds(0, 15), pl.ds(16, 16)]),
    ]
    copies = [
        pltpu.make_async_copy(src, dst, load_sems.at[n]) for n, (src, dst) in enumerate(loads)
    ]
    for n in (0, 1, 2, 12):
        copies[n].start()
    for step in range(2):
        fields[step, :, 15] = jnp.zeros((C, 32, 128), BF)
        cots[step, :, 15] = jnp.zeros((C, 32, 128), BF)

    barrier = pltpu.get_barrier_semaphore()

    def greet_line(d, _):
        pl.semaphore_signal(
            barrier, inc=1, device_id=(gx, lax.rem(gy + d, GY)), device_id_type=MESH
        )
        return 0

    def greet_plane(d, _):
        pl.semaphore_signal(
            barrier, inc=1, device_id=(lax.rem(gx + d, GX), gy), device_id_type=MESH
        )
        return 0

    lax.fori_loop(1, GY, greet_line, 0)
    lax.fori_loop(1, GX, greet_plane, 0)

    wide = lax.broadcasted_iota(jnp.int32, (C * 16, C), 0) // 16
    spread = (wide == lax.broadcasted_iota(jnp.int32, (C * 16, C), 1)).astype(BF)
    grown = dot_nt(dot_nn(spread, w_ref[...]).astype(BF), spread)
    same = lax.rem(lax.broadcasted_iota(jnp.int32, (C * 16, C * 16), 0), 16) == lax.rem(
        lax.broadcasted_iota(jnp.int32, (C * 16, C * 16), 1), 16
    )
    kron[...] = jnp.where(same, grown, 0.0).astype(BF)
    xi[...] = jnp.zeros_like(xi)

    def pad_cells(step, xb):
        def one(c, _):
            value = fields[step, c, :, xb * 16 : xb * 16 + 16].astype(F32).reshape(16, 2, 8, 128)
            for xh in range(2):
                cells[step, c, xb * 2 + xh] = value[:, xh].reshape(128, 128).astype(BF)
            return 0

        lax.fori_loop(0, C, one, 0)

    def deep_half(f, step, xb):
        for xh in range(2):
            def block(c):
                return cells[step, c, xb * 2 + xh]

            o0 = dot_nt(deep0[...], jnp.concatenate([block(c) for c in range(8)], axis=1))
            o1 = dot_nt(deep0[...], jnp.concatenate([block(c) for c in range(8, 16)], axis=1))
            o2 = dot_nt(deep1[...], jnp.concatenate([block(c) for c in range(16, 20)], axis=1))
            for group in range(8):
                for part in range(2):
                    a = group * 48 + part * 24
                    b = group * 32 + part * 16
                    send_a[f, xb, xh * 8 + group, part] = jnp.concatenate(
                        [o0[a : a + 24], o1[a : a + 24], o2[b : b + 16]], axis=0
                    ).astype(BF)

    def a_copy(f, xb, target):
        return pltpu.make_async_remote_copy(
            src_ref=send_a.at[f, xb, target],
            dst_ref=recv_a.at[f, xb, gy],
            send_sem=a_send.at[f],
            recv_sem=a_recv.at[f],
            device_id=(gx, target),
            device_id_type=MESH,
        )

    def send_a_half(f, xb):
        for mate in mates:
            a_copy(f, xb, mate).start()
        pltpu.make_async_copy(send_a.at[f, xb, gy], recv_a.at[f, xb, gy], a_recv.at[f]).start()

    def wait_all(ref, sem):
        pltpu.make_async_copy(ref, ref, sem).wait()

    def b_copy(f, other_x, ky):
        return pltpu.make_async_remote_copy(
            src_ref=send_b.at[f, other_x * 6 + ky],
            dst_ref=recv_b.at[f, slots[ky], my_half, gx],
            send_sem=b_send.at[f],
            recv_sem=b_recv.at[f],
            device_id=(other_x, homes[ky]),
            device_id_type=MESH,
        )

    def send_b_all(f):
        def one(d, _):
            other_x = lax.rem(gx + d, GX)
            for ky in range(6):
                b_copy(f, other_x, ky).start()
            return 0

        lax.fori_loop(1, GX, one, 0)
        for ky in range(6):

            @pl.when(homes[ky] != gy)
            def _():
                b_copy(f, gx, ky).start()

            @pl.when(homes[ky] == gy)
            def _():
                pltpu.make_async_copy(
                    send_b.at[f, gx * 6 + ky],
                    recv_b.at[f, slots[ky], my_half, gx],
                    b_recv.at[f],
                ).start()

    def columns(f):
        data = jnp.concatenate(
            [
                jnp.concatenate(
                    [recv_a[f, xb, s, p] for p in range(2) for xb in range(2)], axis=0
                )
                for s in range(GY)
            ],
            axis=1,
        )
        for part in range(2):
            out = dot_nt(column[part], data)
            real = out[:192, :128] + out[192:, 128:]
            imag = out[:192, 128:] - out[192:, :128]
            send_b[f, pl.ds(part * 24, 24)] = jnp.concatenate(
                [real.reshape(24, 8, 128), imag.reshape(24, 8, 128)], axis=1
            ).astype(BF)
        send_b_all(f)

    def rows_forward(f):
        pieces = []
        for slot in range(3):
            data = recv_b[f, slot].reshape(256, 128)
            out = dot_nn(data.T, row[...])
            xs[slot] = out[0:64, 0:128] + out[64:128, 128:256]
            for kz in range(3):
                pieces.append(xs[slot, pl.ds(kz, C, stride=3), :])
        spectra[f, 0] = jnp.concatenate([piece[:, 0:48] for piece in pieces], axis=1)
        spectra[f, 1] = jnp.concatenate([piece[:, 64:112] for piece in pieces], axis=1)

    pair = lax.broadcasted_iota(jnp.int32, (1, 432), 1) // KX + me * 9
    scale = jnp.where(lax.rem(pair, KZ) == 0, 1.0, 2.0).astype(F32) * INVERSE_TOTAL

    def mix(f, update):
        if update is not None:
            field_f, grad_f = update
            grad_re = spectra[grad_f, 0] * scale * LEARN_RATE
            grad_im = spectra[grad_f, 1] * scale * LEARN_RATE

        def one(i, carry):
            w_re, w_im = weights[0, i], weights[1, i]
            if update is not None:
                in_re = spectra[field_f, 0, pl.ds(i, 1), :]
                in_im = spectra[field_f, 1, pl.ds(i, 1), :]
                w_re = w_re - (in_re * grad_re + in_im * grad_im)
                w_im = w_im - (in_re * grad_im - in_im * grad_re)
                weights[0, i] = w_re
                weights[1, i] = w_im
            if f is None:
                return carry
            re, im = carry
            s_re = spectra[f, 0, pl.ds(i, 1), :]
            s_im = spectra[f, 1, pl.ds(i, 1), :]
            return re + (w_re * s_re - w_im * s_im), im + (w_re * s_im + w_im * s_re)

        zero = jnp.zeros((C, 432), F32)
        return lax.fori_loop(0, C, one, (zero, zero))

    def bb_copy(step, slot, other_x, xh):
        return pltpu.make_async_remote_copy(
            src_ref=back_b.at[step, slot, xh * 8 + other_x],
            dst_ref=got_b.at[step, lines[slot]],
            send_sem=bb_send.at[step],
            recv_sem=bb_recv.at[step],
            device_id=(other_x, xh * 8 + groups[slot]),
            device_id_type=MESH,
        )

    def send_bb_slot(step, slot):
        def one(d, _):
            other_x = lax.rem(gx + d, GX)
            for xh in range(2):
                bb_copy(step, slot, other_x, xh).start()
            return 0

        lax.fori_loop(1, GX, one, 0)
        for xh in range(2):

            @pl.when(xh * 8 + groups[slot] != gy)
            def _():
                bb_copy(step, slot, gx, xh).start()

            @pl.when(xh * 8 + groups[slot] == gy)
            def _():
                pltpu.make_async_copy(
                    back_b.at[step, slot, xh * 8 + gx],
                    got_b.at[step, lines[slot]],
                    bb_recv.at[step],
                ).start()

    def rows_inverse(step, mixed):
        re, im = mixed
        gap = jnp.zeros((C, 16), F32)
        for slot in range(3):
            for kz in range(3):
                a = (slot * 3 + kz) * 48
                xi[slot, pl.ds(kz, C, stride=3), :] = jnp.concatenate(
                    [re[:, a : a + 48], gap, im[:, a : a + 48], gap], axis=1
                )
            value = xi[slot]
            high = value.astype(BF)
            low = (value - high.astype(F32)).astype(BF)
            none = jnp.zeros((64, 128), BF)

            def both(v):
                return jnp.concatenate(
                    [jnp.concatenate([v, none], axis=1), jnp.concatenate([none, v], axis=1)],
                    axis=0,
                )

            high, low = both(high), both(low)
            out = dot_nt(row_back[0], high) + (dot_nt(row_back[0], low) + dot_nt(row_back[1], high))
            back_b[step, slot] = (out * INVERSE_TOTAL).astype(BF).reshape(16, 16, 128)
            send_bb_slot(step, slot)

    def ba_copy(step, xb, target):
        return pltpu.make_async_remote_copy(
            src_ref=back_a.at[step, xb, target],
            dst_ref=got_a.at[step, xb, gy],
            send_sem=ba_send.at[step],
            recv_sem=ba_recv.at[step, xb],
            device_id=(gx, target),
            device_id_type=MESH,
        )

    def send_ba(step, xb, target):
        @pl.when(target == gy)
        def _():
            pltpu.make_async_copy(
                back_a.at[step, xb, target], got_a.at[step, xb, gy], ba_recv.at[step, xb]
            ).start()

        @pl.when(target != gy)
        def _():
            ba_copy(step, xb, target).start()

    def send_ba_half(step, xb):
        for mate in mates:
            ba_copy(step, xb, mate).start()
        pltpu.make_async_copy(
            back_a.at[step, xb, gy], got_a.at[step, xb, gy], ba_recv.at[step, xb]
        ).start()

    def columns_inverse(step):
        data = got_b[step].astype(F32)
        swapped = jnp.concatenate([data[:, 8:16], -data[:, 0:8]], axis=1)
        turned[0:128, :] = data.reshape(768, 128).astype(BF).T
        turned[128:256, :] = swapped.reshape(768, 128).astype(BF).T

        def one(k, _):
            duo = lax.rem(gy // 2 + 1 + k, 8)
            out = dot_nn(turned[...], column_back[duo]).astype(BF)
            for j in range(2):
                target = duo * 2 + j
                value = out[:, j * 128 : j * 128 + 128].reshape(2, 2, 64, 128)
                for xb in range(2):
                    back_a[step, xb, target] = value[:, xb]
                send_ba(step, 0, target)
            return 0

        lax.fori_loop(0, 8, one, 0)

    def deep_inverse(step, xb):
        wait_all(got_a.at[step, xb], ba_recv.at[step, xb])
        for xh in range(2):
            sources = [(xh * 8 + g, p) for g in range(8) for p in range(2)]
            first = jnp.concatenate([got_a[step, xb, t, p, 0:48] for t, p in sources], axis=0)
            second = jnp.concatenate([got_a[step, xb, t, p, 48:64] for t, p in sources], axis=0)
            lifted[xh * 128 : xh * 128 + 128, 0:768] = first.T
            lifted[xh * 128 : xh * 128 + 128, 768:1024] = second.T

        def save(out, c):
            for j in range(2):
                branch[c + j, pl.ds(xb * 2, 2)] = (
                    out[:, j * 128 : j * 128 + 128].astype(BF).reshape(2, 128, 128)
                )

        def one(k, _):
            save(dot_nn(lifted[:, 0:768], rise0[k]), 2 * k)
            return 0

        lax.fori_loop(0, 8, one, 0)
        for k in range(2):
            save(dot_nn(lifted[:, 768:1024], rise1[k]), 16 + 2 * k)

    def channel_map(step):
        for part in range(2):

            def one(k, _):
                rows = pl.ds(k * 16, 16)
                data = jnp.concatenate(
                    [
                        jnp.concatenate(
                            [cells[step, c, part * 2 + xh, rows] for c in range(C)], axis=0
                        )
                        for xh in range(2)
                    ],
                    axis=1,
                )
                out = dot_nn(kron[...], data)
                for o in range(C):
                    for xh in range(2):
                        pre[o, part * 2 + xh, rows] = (
                            out[o * 16 : o * 16 + 16, xh * 128 : xh * 128 + 128] + bias_ref[o]
                        )
                return 0

            lax.fori_loop(0, 8, one, 0)

    def pointwise(step, part, last):
        def one(o, _):
            cot = cots[step, o, :, part * 16 : part * 16 + 16].astype(F32)
            cot = cot.reshape(16, 2, 8, 128)
            outs = []
            for xh in range(2):
                block = part * 2 + xh
                v = pre[o, block] + branch[o, block].astype(F32)
                square = v * v
                half = 0.5 + 0.5 * jnp.tanh(v * (GELU_K + (GELU_K * GELU_C) * square))
                slope = half + (half * (1.0 - half)) * (
                    v * (2.0 * GELU_K + (6.0 * GELU_K * GELU_C) * square)
                )
                cells[step, o, block] = (cot[:, xh].reshape(128, 128) * slope).astype(BF)
                outs.append((v * half).reshape(16, 8, 128))
            if last:
                act[o, :, part * 16 : part * 16 + 16] = jnp.concatenate(outs, axis=1).astype(BF)
            return 0

        lax.fori_loop(0, C, one, 0)

    def all_a_sent(f):
        for xb in range(2):
            wait_all(send_a.at[f, xb, pl.ds(0, GY - 1)], a_send.at[f])

    def all_ba_sent(step):
        for xb in range(2):
            wait_all(back_a.at[step, xb, pl.ds(0, GY - 1)], ba_send.at[step])

    def all_small_sent(sem):
        wait_all(send_b.at[0, pl.ds(0, KY - 1)], sem)

        @pl.when(jnp.logical_not(own))
        def _():
            wait_all(send_b.at[0, KY - 1], sem)

    def all_b_sent(f):
        all_small_sent(b_send.at[f])

    def all_bb_sent(step):
        all_small_sent(bb_send.at[step])

    def mix_and_return(step, f, update):
        rows_inverse(step, mix(f, update))

    def wait_a(f):
        wait_all(recv_a.at[f], a_recv.at[f])

    def wait_b(f):
        wait_all(recv_b.at[f], b_recv.at[f])

    def wait_bb(step):
        wait_all(got_b.at[step], bb_recv.at[step])

    def start():
        copies[0].wait()
        pad_cells(0, 0)
        copies[1].wait()
        copies[2].wait()

    def start_rest():
        copies[12].wait()
        for n in range(3, 12):
            copies[n].start()
        pad_cells(0, 1)

    def unpack_weights():
        def one(i, _):
            for part in range(2):
                weights[part, i] = packed[i, :, part, :]
            return 0

        lax.fori_loop(0, C, one, 0)

    def pack_weights():
        def one(i, _):
            for part in range(2):
                packed[i, :, part, :] = weights[part, i]
            return 0

        lax.fori_loop(0, C, one, 0)

    def meet():
        pl.semaphore_wait(barrier, GX + GY - 2)

        def one(d, _):
            pl.semaphore_signal(
                complete, inc=1, device_id=(lax.rem(gx + d, GX), gy), device_id_type=MESH
            )
            return 0

        lax.fori_loop(1, GX, one, 0)

    def meet_all():
        pl.semaphore_wait(complete, GX - 1)

    def load_second():
        copies[4].wait()
        pad_cells(1, 0)
        pad_cells(1, 1)

    def loaded(*numbers):
        for n in numbers:
            copies[n].wait()

    def act_copy():
        return pltpu.make_async_copy(act.at[:, pl.ds(0, 15)], act_hbm, out_sems.at[0])

    def act_start():
        act_copy().start()

    schedule = [
        (start,),
        (deep_half, 0, 0, 0),
        (meet,),
        (send_a_half, 0, 0),
        (start_rest,),
        (deep_half, 0, 0, 1),
        (send_a_half, 0, 1),
        (load_second,),
        (deep_half, 1, 1, 0),
        (deep_half, 1, 1, 1),
        (loaded, 6),
        (unpack_weights,),
        (channel_map, 0),
        (wait_a, 0),
        (loaded, 3),
        (meet_all,),
        (columns, 0),
        (send_a_half, 1, 0),
        (loaded, 5, 7),
        (wait_b, 0),
        (rows_forward, 0),
        (mix_and_return, 0, 0, None),
        (send_a_half, 1, 1),
        (loaded, 8),
        (wait_bb, 0),
        (columns_inverse, 0),
        (wait_a, 1),
        (columns, 1),
        (send_ba_half, 0, 1),
        (loaded, 9, 10, 11),
        (deep_inverse, 0, 0),
        (pointwise, 0, 0, False),
        (deep_half, 2, 0, 0),
        (send_a_half, 2, 0),
        (deep_inverse, 0, 1),
        (pointwise, 0, 1, False),
        (deep_half, 2, 0, 1),
        (send_a_half, 2, 1),
        (channel_map, 1),
        (wait_b, 1),
        (rows_forward, 1),
        (wait_a, 2),
        (columns, 2),
        (wait_b, 2),
        (rows_forward, 2),
        (mix_and_return, 1, 1, (0, 2)),
        (wait_bb, 1),
        (columns_inverse, 1),
        (send_ba_half, 1, 1),
        (deep_inverse, 1, 0),
        (pointwise, 1, 0, True),
        (deep_half, 3, 1, 0),
        (send_a_half, 3, 0),
        (deep_inverse, 1, 1),
        (pointwise, 1, 1, True),
        (deep_half, 3, 1, 1),
        (send_a_half, 3, 1),
        (act_start,),
        (wait_a, 3),
        (columns, 3),
        (wait_b, 3),
        (rows_forward, 3),
        (mix, None, (1, 3)),
        (pack_weights,),
    ]
    for stage, *numbers in schedule:
        stage(*numbers)
    trained_out = pltpu.make_async_copy(packed, trained_hbm, out_sems.at[1])
    trained_out.start()

    for f in range(4):
        all_a_sent(f)
        all_b_sent(f)
    for step in range(2):
        all_ba_sent(step)
        all_bb_sent(step)
    act_copy().wait()
    trained_out.wait()


def shards(fields, cotangents, w_point, bias_vector, spectral):
    tables = [jnp.asarray(table) for table in make_tables()]
    anywhere = pl.BlockSpec(memory_space=pl.ANY)
    vmem = pltpu.VMEM
    fields = jnp.transpose(fields, (0, 1, 3, 2, 4))
    cotangents = jnp.transpose(cotangents, (0, 1, 3, 2, 4))
    spectral = jnp.transpose(spectral, (1, 2, 0, 3))
    grid_shape = (C, 16, 32, 128)
    dma = pltpu.SemaphoreType.DMA
    scratch = [
        vmem((2,) + grid_shape, BF),
        vmem((2,) + grid_shape, BF),
        vmem((2, C, 4, 128, 128), BF),
        vmem((C, C, 2, 432), F32),
        vmem((2, C, C, 432), F32),
        vmem(grid_shape, BF),
    ]
    scratch += [vmem(table.shape, BF) for table in tables]
    scratch += [
        vmem((4, 2, GY, 2, 64, 128), BF),
        vmem((4, 2, GY, 2, 64, 128), BF),
        vmem((4, KY, 16, 128), BF),
        vmem((4, 3, 2, GX, 16, 128), BF),
        vmem((2, 3, 16, 16, 128), BF),
        vmem((2, KY, 16, 128), BF),
        vmem((2, 2, GY, 2, 64, 128), BF),
        vmem((2, 2, GY, 2, 64, 128), BF),
        vmem((3, 64, 128), F32),
        vmem((4, 2, C, 432), F32),
        vmem((3, 64, 128), F32),
        vmem((256, 768), BF),
        vmem((256, 1024), BF),
        vmem((C, 4, 128, 128), BF),
        vmem((C, 4, 128, 128), F32),
        vmem((C * 16, C * 16), BF),
        dma((13,)),
        dma((2,)),
        pltpu.SemaphoreType.REGULAR,
        dma((4,)),
        dma((4,)),
        dma((4,)),
        dma((4,)),
        dma((2,)),
        dma((2,)),
        dma((2,)),
        dma((2, 2)),
    ]
    act, trained = pl.pallas_call(
        kernel,
        out_shape=(
            jax.ShapeDtypeStruct((C, 15, 32, 128), BF),
            jax.ShapeDtypeStruct((C, C, 2, 432), F32),
        ),
        in_specs=[
            anywhere,
            anywhere,
            pl.BlockSpec(memory_space=pltpu.VMEM),
            pl.BlockSpec(memory_space=pltpu.SMEM),
            anywhere,
        ]
        + [anywhere] * len(tables),
        out_specs=(anywhere, anywhere),
        scratch_shapes=scratch,
        compiler_params=pltpu.CompilerParams(
            collective_id=0, has_side_effects=True, vmem_limit_bytes=62 * 1024 * 1024
        ),
    )(fields, cotangents, w_point, bias_vector, spectral, *tables)
    return jnp.transpose(act, (0, 2, 1, 3)), jnp.transpose(trained, (2, 0, 1, 3))


def solution(mesh):
    return jax.shard_map(
        shards,
        mesh=mesh,
        in_specs=(
            P(None, None, "gx", "gy", None),
            P(None, None, "gx", "gy", None),
            P(),
            P(),
            P(None, None, None, ("gx", "gy")),
        ),
        out_specs=(P(None, "gx", "gy", None), P(None, None, None, ("gx", "gy"))),
        check_vma=False,
    )
```

```python
import functools
import math

import jax
import jax.numpy as jnp
import ml_dtypes
import numpy as np
from jax import lax
from jax.experimental import pallas as pl
from jax.experimental.pallas import tpu as pltpu
from jax.sharding import PartitionSpec as P

C = 20
NX, NY, NZ = 256, 240, 128
KX, KY, KZ = 48, 48, 24
GX, GY = 8, 16
LEARN_RATE = 0.1
INVERSE_TOTAL = 1.0 / (NX * NY * NZ)
BF = jnp.bfloat16
F32 = jnp.float32
MESH = pl.DeviceIdType.MESH
GELU_K = math.sqrt(2.0 / math.pi)
GELU_C = 0.044715


def waves(length, kept):
    index = np.arange(kept)
    return np.where(index < kept // 2, index, index - kept + length)


def angle_tables(length, freqs):
    product = (np.arange(length)[:, None] * freqs[None, :]) % length
    angle = product.astype(np.float32) * np.float32(2.0 * math.pi / length)
    return np.cos(angle), np.sin(angle)


def rounded(table):
    return table.astype(ml_dtypes.bfloat16)


def make_tables():
    cos_z, sin_z = angle_tables(NZ, np.arange(KZ))
    both = np.stack([cos_z, -sin_z]).transpose(0, 2, 1)
    both = both.reshape(2, 8, 3, NZ).transpose(1, 0, 2, 3)
    deep0 = np.einsum("gpkz,nm->gpnkmz", both, np.eye(8, dtype=np.float32)).reshape(384, 1024)
    deep1 = np.zeros((8, 2, 16, 4, NZ), np.float32)
    deep1[:, :, :12] = np.einsum("gpkz,nm->gpnkmz", both, np.eye(4, dtype=np.float32)).reshape(
        8, 2, 12, 4, NZ
    )
    deep1 = deep1.reshape(256, 512)
    factor = np.where(np.arange(KZ) == 0, 1.0, 2.0).astype(np.float32)
    back = np.stack([cos_z * factor, -sin_z * factor]).transpose(0, 2, 1)
    back = back.reshape(2, 8, 3, NZ).transpose(1, 0, 2, 3)
    rise0 = np.einsum("gpkz,nm->gpnkmz", back, np.eye(16, dtype=np.float32))
    rise0 = rise0.reshape(768, 8, 256).transpose(1, 0, 2)
    rise1 = np.zeros((8, 2, 16, 4, NZ), np.float32)
    rise1[:, :, :12] = np.einsum("gpkz,nm->gpnkmz", back, np.eye(4, dtype=np.float32)).reshape(
        8, 2, 12, 4, NZ
    )
    rise1 = rise1.reshape(256, 2, 256).transpose(1, 0, 2)
    cos_y, sin_y = angle_tables(NY, waves(NY, KY))
    padded = np.zeros((2, GY, 16, KY), np.float32)
    padded[:, :, :15] = np.stack([cos_y, sin_y]).reshape(2, GY, 15, KY)
    eye8 = np.eye(8, dtype=np.float32)
    column = np.einsum("asyk,xw->akxsyw", padded, eye8)
    column = column.reshape(2, 2, 24 * 8, 2048).transpose(1, 0, 2, 3).reshape(2, 384, 2048)
    signed = np.stack([padded[0], -padded[1]])
    column_back = np.einsum("asyk,wx->kawsyx", signed, eye8)
    column_back = column_back.reshape(768, 8, 256).transpose(1, 0, 2)
    cos_x, sin_x = angle_tables(NX, waves(NX, KX))
    shape = (GX, 2, 2, 8, KX)
    cos_x = cos_x.reshape(shape).transpose(2, 0, 1, 3, 4)
    sin_x = sin_x.reshape(shape).transpose(2, 0, 1, 3, 4)
    row = np.zeros((2, GX, 2, 8, 2, 2, 64), np.float32)
    row_back = np.zeros_like(row)
    for xb in range(2):
        c, s = cos_x[:, :, xb], sin_x[:, :, xb]
        row[:, :, 0, :, xb, 0, :KX] = c
        row[:, :, 1, :, xb, 0, :KX] = s
        row[:, :, 0, :, xb, 1, :KX] = -s
        row[:, :, 1, :, xb, 1, :KX] = c
        row_back[:, :, 0, :, xb, 0, :KX] = c
        row_back[:, :, 0, :, xb, 1, :KX] = -s
        row_back[:, :, 1, :, xb, 0, :KX] = s
        row_back[:, :, 1, :, xb, 1, :KX] = c
    row = row.reshape(256, 256)
    row_back = row_back.reshape(256, 256)
    row_high = rounded(row_back)
    row_low = rounded(row_back - row_high.astype(np.float32))
    return (
        rounded(deep0),
        rounded(deep1),
        rounded(column),
        rounded(row),
        np.stack([row_high, row_low]),
        rounded(column_back),
        rounded(rise0),
        rounded(rise1),
    )


def dot_nt(a, b):
    return lax.dot_general(a, b, (((1,), (1,)), ((), ())), preferred_element_type=F32)


def dot_nn(a, b):
    return lax.dot_general(a, b, (((1,), (0,)), ((), ())), preferred_element_type=F32)


def kernel(
    fields_hbm, cots_hbm, w_ref, bias_ref, spectral_hbm,
    deep0_hbm, deep1_hbm, column_hbm, row_hbm, row_back_hbm, column_back_hbm, rise0_hbm, rise1_hbm,
    act_hbm, trained_hbm,
    fields, cots, cells, packed, weights, act,
    deep0, deep1, column, row, row_back, column_back, rise0, rise1,
    send_a, recv_a, send_b, recv_b, back_b, got_b, back_a, got_a,
    xs, spectra, xi, turned, lifted, branch, pre, kron,
    load_sems, out_sems, complete,
    a_send, a_recv, b_send, b_recv, bb_send, bb_recv, ba_send, ba_recv,
):
    gx = lax.axis_index("gx")
    gy = lax.axis_index("gy")
    me = gx * GY + gy
    my_half = gy // 8
    my_group = gy % 8
    homes = [(ky * 8 + my_group) // 3 for ky in range(6)]
    slots = [lax.rem(ky * 8 + my_group, 3) for ky in range(6)]
    groups = [lax.rem(gy * 3 + slot, 8) for slot in range(3)]
    lines = [gx * 6 + (gy * 3 + slot) // 8 for slot in range(3)]
    mates = [
        lax.rem(gy // 4 + dy, 4) * 4 + lax.rem(gy + dx, 4)
        for dy, dx in [
            (2, 2), (0, 2), (2, 0), (1, 2), (2, 1), (3, 2), (2, 3), (1, 1),
            (3, 3), (1, 3), (3, 1), (0, 1), (1, 0), (0, 3), (3, 0),
        ]
    ]
    planes = [lax.rem(gx + d, GX) for d in (4, 5, 3, 2, 6, 7, 1)]
    own = functools.reduce(jnp.logical_or, [group == my_group for group in groups])

    loads = [
        (fields_hbm.at[0, :, :, pl.ds(0, 16)], fields.at[0, :, pl.ds(0, 15), pl.ds(0, 16)]),
        (deep0_hbm, deep0),
        (deep1_hbm, deep1),
        (column_hbm, column),
        (fields_hbm.at[1], fields.at[1, :, pl.ds(0, 15)]),
        (row_hbm, row),
        (spectral_hbm, packed),
        (row_back_hbm, row_back),
        (column_back_hbm, column_back),
        (rise0_hbm, rise0),
        (rise1_hbm, rise1),
        (cots_hbm, cots.at[:, :, pl.ds(0, 15)]),
        (fields_hbm.at[0, :, :, pl.ds(16, 16)], fields.at[0, :, pl.ds(0, 15), pl.ds(16, 16)]),
    ]
    copies = [
        pltpu.make_async_copy(src, dst, load_sems.at[n]) for n, (src, dst) in enumerate(loads)
    ]
    for n in (0, 1, 2, 12):
        copies[n].start()
    for step in range(2):
        fields[step, :, 15] = jnp.zeros((C, 32, 128), BF)
        cots[step, :, 15] = jnp.zeros((C, 32, 128), BF)

    barrier = pltpu.get_barrier_semaphore()

    def greet_line(d, _):
        pl.semaphore_signal(
            barrier, inc=1, device_id=(gx, lax.rem(gy + d, GY)), device_id_type=MESH
        )
        return 0

    def greet_plane(d, _):
        pl.semaphore_signal(
            barrier, inc=1, device_id=(lax.rem(gx + d, GX), gy), device_id_type=MESH
        )
        return 0

    lax.fori_loop(1, GY, greet_line, 0)
    lax.fori_loop(1, GX, greet_plane, 0)

    wide = lax.broadcasted_iota(jnp.int32, (C * 16, C), 0) // 16
    spread = (wide == lax.broadcasted_iota(jnp.int32, (C * 16, C), 1)).astype(BF)
    grown = dot_nt(dot_nn(spread, w_ref[...]).astype(BF), spread)
    same = lax.rem(lax.broadcasted_iota(jnp.int32, (C * 16, C * 16), 0), 16) == lax.rem(
        lax.broadcasted_iota(jnp.int32, (C * 16, C * 16), 1), 16
    )
    kron[...] = jnp.where(same, grown, 0.0).astype(BF)
    xi[...] = jnp.zeros_like(xi)

    def pad_cells(step, xb):
        def one(c, _):
            value = fields[step, c, :, xb * 16 : xb * 16 + 16].astype(F32).reshape(16, 2, 8, 128)
            for xh in range(2):
                cells[step, c, xb * 2 + xh] = value[:, xh].reshape(128, 128).astype(BF)
            return 0

        lax.fori_loop(0, C, one, 0)

    def deep_half(f, step, xb):
        for xh in range(2):
            def block(c):
                return cells[step, c, xb * 2 + xh]

            o0 = dot_nt(deep0[...], jnp.concatenate([block(c) for c in range(8)], axis=1))
            o1 = dot_nt(deep0[...], jnp.concatenate([block(c) for c in range(8, 16)], axis=1))
            o2 = dot_nt(deep1[...], jnp.concatenate([block(c) for c in range(16, 20)], axis=1))
            for group in range(8):
                for part in range(2):
                    a = group * 48 + part * 24
                    b = group * 32 + part * 16
                    send_a[f, xb, xh * 8 + group, part] = jnp.concatenate(
                        [o0[a : a + 24], o1[a : a + 24], o2[b : b + 16]], axis=0
                    ).astype(BF)

    def a_copy(f, xb, target):
        return pltpu.make_async_remote_copy(
            src_ref=send_a.at[f, xb, target],
            dst_ref=recv_a.at[f, xb, gy],
            send_sem=a_send.at[f],
            recv_sem=a_recv.at[f],
            device_id=(gx, target),
            device_id_type=MESH,
        )

    def send_a_half(f, xb):
        for mate in mates:
            a_copy(f, xb, mate).start()
        pltpu.make_async_copy(send_a.at[f, xb, gy], recv_a.at[f, xb, gy], a_recv.at[f]).start()

    def wait_all(ref, sem):
        pltpu.make_async_copy(ref, ref, sem).wait()

    def b_copy(f, other_x, ky):
        return pltpu.make_async_remote_copy(
            src_ref=send_b.at[f, other_x * 6 + ky],
            dst_ref=recv_b.at[f, slots[ky], my_half, gx],
            send_sem=b_send.at[f],
            recv_sem=b_recv.at[f],
            device_id=(other_x, homes[ky]),
            device_id_type=MESH,
        )

    def send_b_all(f):
        for other_x in planes:
            for ky in range(6):
                b_copy(f, other_x, ky).start()
        for ky in range(6):

            @pl.when(homes[ky] != gy)
            def _():
                b_copy(f, gx, ky).start()

            @pl.when(homes[ky] == gy)
            def _():
                pltpu.make_async_copy(
                    send_b.at[f, gx * 6 + ky],
                    recv_b.at[f, slots[ky], my_half, gx],
                    b_recv.at[f],
                ).start()

    def columns(f):
        data = jnp.concatenate(
            [
                jnp.concatenate(
                    [recv_a[f, xb, s, p] for p in range(2) for xb in range(2)], axis=0
                )
                for s in range(GY)
            ],
            axis=1,
        )
        for part in range(2):
            out = dot_nt(column[part], data)
            real = out[:192, :128] + out[192:, 128:]
            imag = out[:192, 128:] - out[192:, :128]
            send_b[f, pl.ds(part * 24, 24)] = jnp.concatenate(
                [real.reshape(24, 8, 128), imag.reshape(24, 8, 128)], axis=1
            ).astype(BF)
        send_b_all(f)

    def rows_forward(f):
        pieces = []
        for slot in range(3):
            data = recv_b[f, slot].reshape(256, 128)
            out = dot_nn(data.T, row[...])
            xs[slot] = out[0:64, 0:128] + out[64:128, 128:256]
            for kz in range(3):
                pieces.append(xs[slot, pl.ds(kz, C, stride=3), :])
        spectra[f, 0] = jnp.concatenate([piece[:, 0:48] for piece in pieces], axis=1)
        spectra[f, 1] = jnp.concatenate([piece[:, 64:112] for piece in pieces], axis=1)

    pair = lax.broadcasted_iota(jnp.int32, (1, 432), 1) // KX + me * 9
    scale = jnp.where(lax.rem(pair, KZ) == 0, 1.0, 2.0).astype(F32) * INVERSE_TOTAL

    def mix(f, update):
        if update is not None:
            field_f, grad_f = update
            grad_re = spectra[grad_f, 0] * scale * LEARN_RATE
            grad_im = spectra[grad_f, 1] * scale * LEARN_RATE

        def one(i, carry):
            w_re, w_im = weights[0, i], weights[1, i]
            if update is not None:
                in_re = spectra[field_f, 0, pl.ds(i, 1), :]
                in_im = spectra[field_f, 1, pl.ds(i, 1), :]
                w_re = w_re - (in_re * grad_re + in_im * grad_im)
                w_im = w_im - (in_re * grad_im - in_im * grad_re)
                weights[0, i] = w_re
                weights[1, i] = w_im
            if f is None:
                return carry
            re, im = carry
            s_re = spectra[f, 0, pl.ds(i, 1), :]
            s_im = spectra[f, 1, pl.ds(i, 1), :]
            return re + (w_re * s_re - w_im * s_im), im + (w_re * s_im + w_im * s_re)

        zero = jnp.zeros((C, 432), F32)
        return lax.fori_loop(0, C, one, (zero, zero))

    def bb_copy(step, slot, other_x, xh):
        return pltpu.make_async_remote_copy(
            src_ref=back_b.at[step, slot, xh * 8 + other_x],
            dst_ref=got_b.at[step, lines[slot]],
            send_sem=bb_send.at[step],
            recv_sem=bb_recv.at[step],
            device_id=(other_x, xh * 8 + groups[slot]),
            device_id_type=MESH,
        )

    def send_bb_slot(step, slot):
        for other_x in planes:
            for xh in range(2):
                bb_copy(step, slot, other_x, xh).start()
        for xh in range(2):

            @pl.when(xh * 8 + groups[slot] != gy)
            def _():
                bb_copy(step, slot, gx, xh).start()

            @pl.when(xh * 8 + groups[slot] == gy)
            def _():
                pltpu.make_async_copy(
                    back_b.at[step, slot, xh * 8 + gx],
                    got_b.at[step, lines[slot]],
                    bb_recv.at[step],
                ).start()

    def rows_inverse(step, mixed):
        re, im = mixed
        gap = jnp.zeros((C, 16), F32)
        for slot in range(3):
            for kz in range(3):
                a = (slot * 3 + kz) * 48
                xi[slot, pl.ds(kz, C, stride=3), :] = jnp.concatenate(
                    [re[:, a : a + 48], gap, im[:, a : a + 48], gap], axis=1
                )
            value = xi[slot]
            high = value.astype(BF)
            low = (value - high.astype(F32)).astype(BF)
            none = jnp.zeros((64, 128), BF)

            def both(v):
                return jnp.concatenate(
                    [jnp.concatenate([v, none], axis=1), jnp.concatenate([none, v], axis=1)],
                    axis=0,
                )

            high, low = both(high), both(low)
            out = dot_nt(row_back[0], high) + (dot_nt(row_back[0], low) + dot_nt(row_back[1], high))
            back_b[step, slot] = (out * INVERSE_TOTAL).astype(BF).reshape(16, 16, 128)
            send_bb_slot(step, slot)

    def ba_copy(step, xb, target):
        return pltpu.make_async_remote_copy(
            src_ref=back_a.at[step, xb, target],
            dst_ref=got_a.at[step, xb, gy],
            send_sem=ba_send.at[step],
            recv_sem=ba_recv.at[step, xb],
            device_id=(gx, target),
            device_id_type=MESH,
        )

    def send_ba(step, xb, target):
        @pl.when(target == gy)
        def _():
            pltpu.make_async_copy(
                back_a.at[step, xb, target], got_a.at[step, xb, gy], ba_recv.at[step, xb]
            ).start()

        @pl.when(target != gy)
        def _():
            ba_copy(step, xb, target).start()

    def send_ba_half(step, xb):
        for mate in mates:
            ba_copy(step, xb, mate).start()
        pltpu.make_async_copy(
            back_a.at[step, xb, gy], got_a.at[step, xb, gy], ba_recv.at[step, xb]
        ).start()

    def columns_inverse(step):
        data = got_b[step].astype(F32)
        swapped = jnp.concatenate([data[:, 8:16], -data[:, 0:8]], axis=1)
        turned[0:128, :] = data.reshape(768, 128).astype(BF).T
        turned[128:256, :] = swapped.reshape(768, 128).astype(BF).T

        def one(k, _):
            duo = lax.rem(gy // 2 + 1 + k, 8)
            out = dot_nn(turned[...], column_back[duo]).astype(BF)
            for j in range(2):
                target = duo * 2 + j
                value = out[:, j * 128 : j * 128 + 128].reshape(2, 2, 64, 128)
                for xb in range(2):
                    back_a[step, xb, target] = value[:, xb]
                send_ba(step, 0, target)
            return 0

        lax.fori_loop(0, 8, one, 0)

    def deep_inverse(step, xb):
        wait_all(got_a.at[step, xb], ba_recv.at[step, xb])
        for xh in range(2):
            sources = [(xh * 8 + g, p) for g in range(8) for p in range(2)]
            first = jnp.concatenate([got_a[step, xb, t, p, 0:48] for t, p in sources], axis=0)
            second = jnp.concatenate([got_a[step, xb, t, p, 48:64] for t, p in sources], axis=0)
            lifted[xh * 128 : xh * 128 + 128, 0:768] = first.T
            lifted[xh * 128 : xh * 128 + 128, 768:1024] = second.T

        def save(out, c):
            for j in range(2):
                branch[c + j, pl.ds(xb * 2, 2)] = (
                    out[:, j * 128 : j * 128 + 128].astype(BF).reshape(2, 128, 128)
                )

        def one(k, _):
            save(dot_nn(lifted[:, 0:768], rise0[k]), 2 * k)
            return 0

        lax.fori_loop(0, 8, one, 0)
        for k in range(2):
            save(dot_nn(lifted[:, 768:1024], rise1[k]), 16 + 2 * k)

    def channel_map(step):
        for part in range(2):

            def one(k, _):
                rows = pl.ds(k * 16, 16)
                data = jnp.concatenate(
                    [
                        jnp.concatenate(
                            [cells[step, c, part * 2 + xh, rows] for c in range(C)], axis=0
                        )
                        for xh in range(2)
                    ],
                    axis=1,
                )
                out = dot_nn(kron[...], data)
                for o in range(C):
                    for xh in range(2):
                        pre[o, part * 2 + xh, rows] = (
                            out[o * 16 : o * 16 + 16, xh * 128 : xh * 128 + 128] + bias_ref[o]
                        )
                return 0

            lax.fori_loop(0, 8, one, 0)

    def pointwise(step, part, last):
        def one(o, _):
            cot = cots[step, o, :, part * 16 : part * 16 + 16].astype(F32)
            cot = cot.reshape(16, 2, 8, 128)
            outs = []
            for xh in range(2):
                block = part * 2 + xh
                v = pre[o, block] + branch[o, block].astype(F32)
                square = v * v
                half = 0.5 + 0.5 * jnp.tanh(v * (GELU_K + (GELU_K * GELU_C) * square))
                slope = half + (half * (1.0 - half)) * (
                    v * (2.0 * GELU_K + (6.0 * GELU_K * GELU_C) * square)
                )
                cells[step, o, block] = (cot[:, xh].reshape(128, 128) * slope).astype(BF)
                outs.append((v * half).reshape(16, 8, 128))
            if last:
                act[o, :, part * 16 : part * 16 + 16] = jnp.concatenate(outs, axis=1).astype(BF)
            return 0

        lax.fori_loop(0, C, one, 0)

    def all_a_sent(f):
        for xb in range(2):
            wait_all(send_a.at[f, xb, pl.ds(0, GY - 1)], a_send.at[f])

    def all_ba_sent(step):
        for xb in range(2):
            wait_all(back_a.at[step, xb, pl.ds(0, GY - 1)], ba_send.at[step])

    def all_small_sent(sem):
        wait_all(send_b.at[0, pl.ds(0, KY - 1)], sem)

        @pl.when(jnp.logical_not(own))
        def _():
            wait_all(send_b.at[0, KY - 1], sem)

    def all_b_sent(f):
        all_small_sent(b_send.at[f])

    def all_bb_sent(step):
        all_small_sent(bb_send.at[step])

    def mix_and_return(step, f, update):
        rows_inverse(step, mix(f, update))

    def wait_a(f):
        wait_all(recv_a.at[f], a_recv.at[f])

    def wait_b(f):
        wait_all(recv_b.at[f], b_recv.at[f])

    def wait_bb(step):
        wait_all(got_b.at[step], bb_recv.at[step])

    def start():
        copies[0].wait()
        pad_cells(0, 0)
        copies[1].wait()
        copies[2].wait()

    def start_rest():
        copies[12].wait()
        for n in range(3, 12):
            copies[n].start()
        pad_cells(0, 1)

    def unpack_weights():
        def one(i, _):
            for part in range(2):
                weights[part, i] = packed[i, :, part, :]
            return 0

        lax.fori_loop(0, C, one, 0)

    def pack_weights():
        def one(i, _):
            for part in range(2):
                packed[i, :, part, :] = weights[part, i]
            return 0

        lax.fori_loop(0, C, one, 0)

    def meet():
        pl.semaphore_wait(barrier, GX + GY - 2)

        def one(d, _):
            pl.semaphore_signal(
                complete, inc=1, device_id=(lax.rem(gx + d, GX), gy), device_id_type=MESH
            )
            return 0

        lax.fori_loop(1, GX, one, 0)

    def meet_all():
        pl.semaphore_wait(complete, GX - 1)

    def load_second():
        copies[4].wait()
        pad_cells(1, 0)
        pad_cells(1, 1)

    def loaded(*numbers):
        for n in numbers:
            copies[n].wait()

    def act_copy():
        return pltpu.make_async_copy(act.at[:, pl.ds(0, 15)], act_hbm, out_sems.at[0])

    def act_start():
        act_copy().start()

    schedule = [
        (start,),
        (deep_half, 0, 0, 0),
        (meet,),
        (send_a_half, 0, 0),
        (start_rest,),
        (deep_half, 0, 0, 1),
        (send_a_half, 0, 1),
        (load_second,),
        (deep_half, 1, 1, 0),
        (deep_half, 1, 1, 1),
        (loaded, 6),
        (unpack_weights,),
        (channel_map, 0),
        (wait_a, 0),
        (loaded, 3),
        (meet_all,),
        (columns, 0),
        (send_a_half, 1, 0),
        (loaded, 5, 7),
        (wait_b, 0),
        (rows_forward, 0),
        (mix_and_return, 0, 0, None),
        (send_a_half, 1, 1),
        (loaded, 8),
        (wait_bb, 0),
        (columns_inverse, 0),
        (wait_a, 1),
        (columns, 1),
        (send_ba_half, 0, 1),
        (loaded, 9, 10, 11),
        (deep_inverse, 0, 0),
        (pointwise, 0, 0, False),
        (deep_half, 2, 0, 0),
        (send_a_half, 2, 0),
        (deep_inverse, 0, 1),
        (pointwise, 0, 1, False),
        (deep_half, 2, 0, 1),
        (send_a_half, 2, 1),
        (channel_map, 1),
        (wait_b, 1),
        (rows_forward, 1),
        (wait_a, 2),
        (columns, 2),
        (wait_b, 2),
        (rows_forward, 2),
        (mix_and_return, 1, 1, (0, 2)),
        (wait_bb, 1),
        (columns_inverse, 1),
        (send_ba_half, 1, 1),
        (deep_inverse, 1, 0),
        (pointwise, 1, 0, True),
        (deep_half, 3, 1, 0),
        (send_a_half, 3, 0),
        (deep_inverse, 1, 1),
        (pointwise, 1, 1, True),
        (deep_half, 3, 1, 1),
        (send_a_half, 3, 1),
        (act_start,),
        (wait_a, 3),
        (columns, 3),
        (wait_b, 3),
        (rows_forward, 3),
        (mix, None, (1, 3)),
        (pack_weights,),
    ]
    for stage, *numbers in schedule:
        stage(*numbers)
    trained_out = pltpu.make_async_copy(packed, trained_hbm, out_sems.at[1])
    trained_out.start()

    for f in range(4):
        all_a_sent(f)
        all_b_sent(f)
    for step in range(2):
        all_ba_sent(step)
        all_bb_sent(step)
    act_copy().wait()
    trained_out.wait()


def shards(fields, cotangents, w_point, bias_vector, spectral):
    tables = [jnp.asarray(table) for table in make_tables()]
    anywhere = pl.BlockSpec(memory_space=pl.ANY)
    vmem = pltpu.VMEM
    fields = jnp.transpose(fields, (0, 1, 3, 2, 4))
    cotangents = jnp.transpose(cotangents, (0, 1, 3, 2, 4))
    spectral = jnp.transpose(spectral, (1, 2, 0, 3))
    grid_shape = (C, 16, 32, 128)
    dma = pltpu.SemaphoreType.DMA
    scratch = [
        vmem((2,) + grid_shape, BF),
        vmem((2,) + grid_shape, BF),
        vmem((2, C, 4, 128, 128), BF),
        vmem((C, C, 2, 432), F32),
        vmem((2, C, C, 432), F32),
        vmem(grid_shape, BF),
    ]
    scratch += [vmem(table.shape, BF) for table in tables]
    scratch += [
        vmem((4, 2, GY, 2, 64, 128), BF),
        vmem((4, 2, GY, 2, 64, 128), BF),
        vmem((4, KY, 16, 128), BF),
        vmem((4, 3, 2, GX, 16, 128), BF),
        vmem((2, 3, 16, 16, 128), BF),
        vmem((2, KY, 16, 128), BF),
        vmem((2, 2, GY, 2, 64, 128), BF),
        vmem((2, 2, GY, 2, 64, 128), BF),
        vmem((3, 64, 128), F32),
        vmem((4, 2, C, 432), F32),
        vmem((3, 64, 128), F32),
        vmem((256, 768), BF),
        vmem((256, 1024), BF),
        vmem((C, 4, 128, 128), BF),
        vmem((C, 4, 128, 128), F32),
        vmem((C * 16, C * 16), BF),
        dma((13,)),
        dma((2,)),
        pltpu.SemaphoreType.REGULAR,
        dma((4,)),
        dma((4,)),
        dma((4,)),
        dma((4,)),
        dma((2,)),
        dma((2,)),
        dma((2,)),
        dma((2, 2)),
    ]
    act, trained = pl.pallas_call(
        kernel,
        out_shape=(
            jax.ShapeDtypeStruct((C, 15, 32, 128), BF),
            jax.ShapeDtypeStruct((C, C, 2, 432), F32),
        ),
        in_specs=[
            anywhere,
            anywhere,
            pl.BlockSpec(memory_space=pltpu.VMEM),
            pl.BlockSpec(memory_space=pltpu.SMEM),
            anywhere,
        ]
        + [anywhere] * len(tables),
        out_specs=(anywhere, anywhere),
        scratch_shapes=scratch,
        compiler_params=pltpu.CompilerParams(
            collective_id=0, has_side_effects=True, vmem_limit_bytes=62 * 1024 * 1024
        ),
    )(fields, cotangents, w_point, bias_vector, spectral, *tables)
    return jnp.transpose(act, (0, 2, 1, 3)), jnp.transpose(trained, (2, 0, 1, 3))


def solution(mesh):
    return jax.shard_map(
        shards,
        mesh=mesh,
        in_specs=(
            P(None, None, "gx", "gy", None),
            P(None, None, "gx", "gy", None),
            P(),
            P(),
            P(None, None, None, ("gx", "gy")),
        ),
        out_specs=(P(None, "gx", "gy", None), P(None, None, None, ("gx", "gy"))),
        check_vma=False,
    )
```

```python
import functools
import math

import jax
import jax.numpy as jnp
import ml_dtypes
import numpy as np
from jax import lax
from jax.experimental import pallas as pl
from jax.experimental.pallas import tpu as pltpu
from jax.sharding import PartitionSpec as P

C = 20
NX, NY, NZ = 256, 240, 128
KX, KY, KZ = 48, 48, 24
GX, GY = 8, 16
LEARN_RATE = 0.1
INVERSE_TOTAL = 1.0 / (NX * NY * NZ)
BF = jnp.bfloat16
F32 = jnp.float32
MESH = pl.DeviceIdType.MESH
GELU_K = math.sqrt(2.0 / math.pi)
GELU_C = 0.044715


def waves(length, kept):
    index = np.arange(kept)
    return np.where(index < kept // 2, index, index - kept + length)


def angle_tables(length, freqs):
    product = (np.arange(length)[:, None] * freqs[None, :]) % length
    angle = product.astype(np.float32) * np.float32(2.0 * math.pi / length)
    return np.cos(angle), np.sin(angle)


def rounded(table):
    return table.astype(ml_dtypes.bfloat16)


def make_tables():
    cos_z, sin_z = angle_tables(NZ, np.arange(KZ))
    both = np.stack([cos_z, -sin_z]).transpose(0, 2, 1)
    both = both.reshape(2, 8, 3, NZ).transpose(1, 0, 2, 3)
    deep0 = np.einsum("gpkz,nm->gpnkmz", both, np.eye(8, dtype=np.float32)).reshape(384, 1024)
    deep1 = np.zeros((8, 2, 16, 4, NZ), np.float32)
    deep1[:, :, :12] = np.einsum("gpkz,nm->gpnkmz", both, np.eye(4, dtype=np.float32)).reshape(
        8, 2, 12, 4, NZ
    )
    deep1 = deep1.reshape(256, 512)
    factor = np.where(np.arange(KZ) == 0, 1.0, 2.0).astype(np.float32)
    back = np.stack([cos_z * factor, -sin_z * factor]).transpose(0, 2, 1)
    back = back.reshape(2, 8, 3, NZ).transpose(1, 0, 2, 3)
    rise0 = np.einsum("gpkz,nm->gpnkmz", back, np.eye(16, dtype=np.float32))
    rise0 = rise0.reshape(768, 8, 256).transpose(1, 0, 2)
    rise1 = np.zeros((8, 2, 16, 4, NZ), np.float32)
    rise1[:, :, :12] = np.einsum("gpkz,nm->gpnkmz", back, np.eye(4, dtype=np.float32)).reshape(
        8, 2, 12, 4, NZ
    )
    rise1 = rise1.reshape(256, 2, 256).transpose(1, 0, 2)
    cos_y, sin_y = angle_tables(NY, waves(NY, KY))
    padded = np.zeros((2, GY, 16, KY), np.float32)
    padded[:, :, :15] = np.stack([cos_y, sin_y]).reshape(2, GY, 15, KY)
    eye8 = np.eye(8, dtype=np.float32)
    column = np.einsum("asyk,xw->akxsyw", padded, eye8)
    column = column.reshape(2, 2, 24 * 8, 2048).transpose(1, 0, 2, 3).reshape(2, 384, 2048)
    signed = np.stack([padded[0], -padded[1]])
    column_back = np.einsum("asyk,wx->kawsyx", signed, eye8)
    column_back = column_back.reshape(768, 8, 256).transpose(1, 0, 2)
    cos_x, sin_x = angle_tables(NX, waves(NX, KX))
    shape = (GX, 2, 2, 8, KX)
    cos_x = cos_x.reshape(shape).transpose(2, 0, 1, 3, 4)
    sin_x = sin_x.reshape(shape).transpose(2, 0, 1, 3, 4)
    row = np.zeros((2, GX, 2, 8, 2, 2, 64), np.float32)
    row_back = np.zeros_like(row)
    for xb in range(2):
        c, s = cos_x[:, :, xb], sin_x[:, :, xb]
        row[:, :, 0, :, xb, 0, :KX] = c
        row[:, :, 1, :, xb, 0, :KX] = s
        row[:, :, 0, :, xb, 1, :KX] = -s
        row[:, :, 1, :, xb, 1, :KX] = c
        row_back[:, :, 0, :, xb, 0, :KX] = c
        row_back[:, :, 0, :, xb, 1, :KX] = -s
        row_back[:, :, 1, :, xb, 0, :KX] = s
        row_back[:, :, 1, :, xb, 1, :KX] = c
    row = row.reshape(256, 256)
    row_back = row_back.reshape(256, 256)
    row_high = rounded(row_back)
    row_low = rounded(row_back - row_high.astype(np.float32))
    return (
        rounded(deep0),
        rounded(deep1),
        rounded(column),
        rounded(row),
        np.stack([row_high, row_low]),
        rounded(column_back),
        rounded(rise0),
        rounded(rise1),
    )


def dot_nt(a, b):
    return lax.dot_general(a, b, (((1,), (1,)), ((), ())), preferred_element_type=F32)


def dot_nn(a, b):
    return lax.dot_general(a, b, (((1,), (0,)), ((), ())), preferred_element_type=F32)


def kernel(
    fields_hbm, cots_hbm, w_ref, bias_ref, spectral_hbm,
    deep0_hbm, deep1_hbm, column_hbm, row_hbm, row_back_hbm, column_back_hbm, rise0_hbm, rise1_hbm,
    act_hbm, trained_hbm,
    fields, cots, cells, packed, weights, act,
    deep0, deep1, column, row, row_back, column_back, rise0, rise1,
    send_a, recv_a, send_b, recv_b, back_b, got_b, back_a, got_a,
    xs, spectra, xi, turned, lifted, branch, pre, kron,
    load_sems, out_sems, complete,
    a_send, a_recv, b_send, b_recv, bb_send, bb_recv, ba_send, ba_recv,
):
    gx = lax.axis_index("gx")
    gy = lax.axis_index("gy")
    me = gx * GY + gy
    my_half = gy // 8
    my_group = gy % 8
    homes = [(ky * 8 + my_group) // 3 for ky in range(6)]
    slots = [lax.rem(ky * 8 + my_group, 3) for ky in range(6)]
    groups = [lax.rem(gy * 3 + slot, 8) for slot in range(3)]
    lines = [gx * 6 + (gy * 3 + slot) // 8 for slot in range(3)]
    mates = [
        lax.rem(gy // 4 + dy, 4) * 4 + lax.rem(gy + dx, 4)
        for dy, dx in [
            (2, 2), (0, 2), (2, 0), (1, 2), (2, 1), (3, 2), (2, 3), (1, 1),
            (3, 3), (1, 3), (3, 1), (0, 1), (1, 0), (0, 3), (3, 0),
        ]
    ]
    planes = [lax.rem(gx + d, GX) for d in (4, 5, 3, 2, 6, 7, 1)]
    near_half = gx // 4
    far_half = 1 - near_half
    own = functools.reduce(jnp.logical_or, [group == my_group for group in groups])

    loads = [
        (fields_hbm.at[0, :, :, pl.ds(0, 16)], fields.at[0, :, pl.ds(0, 15), pl.ds(0, 16)]),
        (deep0_hbm, deep0),
        (deep1_hbm, deep1),
        (column_hbm, column),
        (fields_hbm.at[1], fields.at[1, :, pl.ds(0, 15)]),
        (row_hbm, row),
        (spectral_hbm, packed),
        (row_back_hbm, row_back),
        (column_back_hbm, column_back),
        (rise0_hbm, rise0),
        (rise1_hbm, rise1),
        (cots_hbm, cots.at[:, :, pl.ds(0, 15)]),
        (fields_hbm.at[0, :, :, pl.ds(16, 16)], fields.at[0, :, pl.ds(0, 15), pl.ds(16, 16)]),
    ]
    copies = [
        pltpu.make_async_copy(src, dst, load_sems.at[n]) for n, (src, dst) in enumerate(loads)
    ]
    for n in (0, 1, 2, 12):
        copies[n].start()
    for step in range(2):
        fields[step, :, 15] = jnp.zeros((C, 32, 128), BF)
        cots[step, :, 15] = jnp.zeros((C, 32, 128), BF)

    barrier = pltpu.get_barrier_semaphore()

    def greet_line(d, _):
        pl.semaphore_signal(
            barrier, inc=1, device_id=(gx, lax.rem(gy + d, GY)), device_id_type=MESH
        )
        return 0

    def greet_plane(d, _):
        pl.semaphore_signal(
            barrier, inc=1, device_id=(lax.rem(gx + d, GX), gy), device_id_type=MESH
        )
        return 0

    lax.fori_loop(1, GY, greet_line, 0)
    lax.fori_loop(1, GX, greet_plane, 0)

    wide = lax.broadcasted_iota(jnp.int32, (C * 16, C), 0) // 16
    spread = (wide == lax.broadcasted_iota(jnp.int32, (C * 16, C), 1)).astype(BF)
    grown = dot_nt(dot_nn(spread, w_ref[...]).astype(BF), spread)
    same = lax.rem(lax.broadcasted_iota(jnp.int32, (C * 16, C * 16), 0), 16) == lax.rem(
        lax.broadcasted_iota(jnp.int32, (C * 16, C * 16), 1), 16
    )
    kron[...] = jnp.where(same, grown, 0.0).astype(BF)
    xi[...] = jnp.zeros_like(xi)

    def pad_cells(step, xb):
        def one(c, _):
            value = fields[step, c, :, xb * 16 : xb * 16 + 16].astype(F32).reshape(16, 2, 8, 128)
            for xh in range(2):
                cells[step, c, xb * 2 + xh] = value[:, xh].reshape(128, 128).astype(BF)
            return 0

        lax.fori_loop(0, C, one, 0)

    def deep_half(f, step, xb):
        for xh in range(2):
            def block(c):
                return cells[step, c, xb * 2 + xh]

            o0 = dot_nt(deep0[...], jnp.concatenate([block(c) for c in range(8)], axis=1))
            o1 = dot_nt(deep0[...], jnp.concatenate([block(c) for c in range(8, 16)], axis=1))
            o2 = dot_nt(deep1[...], jnp.concatenate([block(c) for c in range(16, 20)], axis=1))
            for group in range(8):
                for part in range(2):
                    a = group * 48 + part * 24
                    b = group * 32 + part * 16
                    send_a[f, xb, xh * 8 + group, part] = jnp.concatenate(
                        [o0[a : a + 24], o1[a : a + 24], o2[b : b + 16]], axis=0
                    ).astype(BF)

    def a_copy(f, xb, target):
        return pltpu.make_async_remote_copy(
            src_ref=send_a.at[f, xb, target],
            dst_ref=recv_a.at[f, xb, gy],
            send_sem=a_send.at[f],
            recv_sem=a_recv.at[f],
            device_id=(gx, target),
            device_id_type=MESH,
        )

    def send_a_half(f, xb):
        for mate in mates:
            a_copy(f, xb, mate).start()
        pltpu.make_async_copy(send_a.at[f, xb, gy], recv_a.at[f, xb, gy], a_recv.at[f]).start()

    def wait_all(ref, sem):
        pltpu.make_async_copy(ref, ref, sem).wait()

    def b_copy(f, other_x, ky):
        return pltpu.make_async_remote_copy(
            src_ref=send_b.at[f, other_x * 6 + ky],
            dst_ref=recv_b.at[f, slots[ky], my_half, gx],
            send_sem=b_send.at[f],
            recv_sem=b_recv.at[f],
            device_id=(other_x, homes[ky]),
            device_id_type=MESH,
        )

    def send_b_far(f):
        for d in range(4):
            for ky in range(6):
                b_copy(f, far_half * 4 + lax.rem(gx + d, 4), ky).start()

    def send_b_near(f):
        for d in (2, 1, 3):
            for ky in range(6):
                b_copy(f, near_half * 4 + lax.rem(gx + d, 4), ky).start()
        for ky in range(6):

            @pl.when(homes[ky] != gy)
            def _():
                b_copy(f, gx, ky).start()

            @pl.when(homes[ky] == gy)
            def _():
                pltpu.make_async_copy(
                    send_b.at[f, gx * 6 + ky],
                    recv_b.at[f, slots[ky], my_half, gx],
                    b_recv.at[f],
                ).start()

    def columns(f):
        data = jnp.concatenate(
            [
                jnp.concatenate(
                    [recv_a[f, xb, s, p] for p in range(2) for xb in range(2)], axis=0
                )
                for s in range(GY)
            ],
            axis=1,
        )
        for part, send in ((far_half, send_b_far), (near_half, send_b_near)):
            out = dot_nt(column[part], data)
            real = out[:192, :128] + out[192:, 128:]
            imag = out[:192, 128:] - out[192:, :128]
            send_b[f, pl.ds(part * 24, 24)] = jnp.concatenate(
                [real.reshape(24, 8, 128), imag.reshape(24, 8, 128)], axis=1
            ).astype(BF)
            send(f)

    def rows_forward(f):
        pieces = []
        for slot in range(3):
            data = recv_b[f, slot].reshape(256, 128)
            out = dot_nn(data.T, row[...])
            xs[slot] = out[0:64, 0:128] + out[64:128, 128:256]
            for kz in range(3):
                pieces.append(xs[slot, pl.ds(kz, C, stride=3), :])
        spectra[f, 0] = jnp.concatenate([piece[:, 0:48] for piece in pieces], axis=1)
        spectra[f, 1] = jnp.concatenate([piece[:, 64:112] for piece in pieces], axis=1)

    pair = lax.broadcasted_iota(jnp.int32, (1, 432), 1) // KX + me * 9
    scale = jnp.where(lax.rem(pair, KZ) == 0, 1.0, 2.0).astype(F32) * INVERSE_TOTAL

    def mix(f, update):
        if update is not None:
            field_f, grad_f = update
            grad_re = spectra[grad_f, 0] * scale * LEARN_RATE
            grad_im = spectra[grad_f, 1] * scale * LEARN_RATE

        def one(i, carry):
            w_re, w_im = weights[0, i], weights[1, i]
            if update is not None:
                in_re = spectra[field_f, 0, pl.ds(i, 1), :]
                in_im = spectra[field_f, 1, pl.ds(i, 1), :]
                w_re = w_re - (in_re * grad_re + in_im * grad_im)
                w_im = w_im - (in_re * grad_im - in_im * grad_re)
                if f is None:
                    packed[i, :, 0, :] = w_re
                    packed[i, :, 1, :] = w_im
                    return carry
                weights[0, i] = w_re
                weights[1, i] = w_im
            re, im = carry
            s_re = spectra[f, 0, pl.ds(i, 1), :]
            s_im = spectra[f, 1, pl.ds(i, 1), :]
            return re + (w_re * s_re - w_im * s_im), im + (w_re * s_im + w_im * s_re)

        zero = jnp.zeros((C, 432), F32)
        return lax.fori_loop(0, C, one, (zero, zero))

    def bb_copy(step, slot, other_x, xh):
        return pltpu.make_async_remote_copy(
            src_ref=back_b.at[step, slot, xh * 8 + other_x],
            dst_ref=got_b.at[step, lines[slot]],
            send_sem=bb_send.at[step],
            recv_sem=bb_recv.at[step],
            device_id=(other_x, xh * 8 + groups[slot]),
            device_id_type=MESH,
        )

    def send_bb_slot(step, slot):
        for other_x in planes:
            for xh in range(2):
                bb_copy(step, slot, other_x, xh).start()
        for xh in range(2):

            @pl.when(xh * 8 + groups[slot] != gy)
            def _():
                bb_copy(step, slot, gx, xh).start()

            @pl.when(xh * 8 + groups[slot] == gy)
            def _():
                pltpu.make_async_copy(
                    back_b.at[step, slot, xh * 8 + gx],
                    got_b.at[step, lines[slot]],
                    bb_recv.at[step],
                ).start()

    def rows_inverse(step, mixed):
        re, im = mixed
        gap = jnp.zeros((C, 16), F32)
        for slot in range(3):
            for kz in range(3):
                a = (slot * 3 + kz) * 48
                xi[slot, pl.ds(kz, C, stride=3), :] = jnp.concatenate(
                    [re[:, a : a + 48], gap, im[:, a : a + 48], gap], axis=1
                )
            value = xi[slot]
            high = value.astype(BF)
            low = (value - high.astype(F32)).astype(BF)
            none = jnp.zeros((64, 128), BF)

            def both(v):
                return jnp.concatenate(
                    [jnp.concatenate([v, none], axis=1), jnp.concatenate([none, v], axis=1)],
                    axis=0,
                )

            high, low = both(high), both(low)
            out = dot_nt(row_back[0], high) + (dot_nt(row_back[0], low) + dot_nt(row_back[1], high))
            back_b[step, slot] = (out * INVERSE_TOTAL).astype(BF).reshape(16, 16, 128)
            send_bb_slot(step, slot)

    def ba_copy(step, xb, target):
        return pltpu.make_async_remote_copy(
            src_ref=back_a.at[step, xb, target],
            dst_ref=got_a.at[step, xb, gy],
            send_sem=ba_send.at[step],
            recv_sem=ba_recv.at[step, xb],
            device_id=(gx, target),
            device_id_type=MESH,
        )

    def send_ba(step, xb, target):
        @pl.when(target == gy)
        def _():
            pltpu.make_async_copy(
                back_a.at[step, xb, target], got_a.at[step, xb, gy], ba_recv.at[step, xb]
            ).start()

        @pl.when(target != gy)
        def _():
            ba_copy(step, xb, target).start()

    def send_ba_half(step, xb):
        for mate in mates:
            ba_copy(step, xb, mate).start()
        pltpu.make_async_copy(
            back_a.at[step, xb, gy], got_a.at[step, xb, gy], ba_recv.at[step, xb]
        ).start()

    def columns_inverse(step):
        data = got_b[step].astype(F32)
        swapped = jnp.concatenate([data[:, 8:16], -data[:, 0:8]], axis=1)
        turned[0:128, :] = data.reshape(768, 128).astype(BF).T
        turned[128:256, :] = swapped.reshape(768, 128).astype(BF).T

        def one(k, _):
            duo = lax.rem(gy // 2 + 1 + k, 8)
            out = dot_nn(turned[...], column_back[duo]).astype(BF)
            for j in range(2):
                target = duo * 2 + j
                value = out[:, j * 128 : j * 128 + 128].reshape(2, 2, 64, 128)
                for xb in range(2):
                    back_a[step, xb, target] = value[:, xb]
                send_ba(step, 0, target)
            return 0

        lax.fori_loop(0, 8, one, 0)

    def deep_inverse(step, xb):
        wait_all(got_a.at[step, xb], ba_recv.at[step, xb])
        for xh in range(2):
            sources = [(xh * 8 + g, p) for g in range(8) for p in range(2)]
            first = jnp.concatenate([got_a[step, xb, t, p, 0:48] for t, p in sources], axis=0)
            second = jnp.concatenate([got_a[step, xb, t, p, 48:64] for t, p in sources], axis=0)
            lifted[xh * 128 : xh * 128 + 128, 0:768] = first.T
            lifted[xh * 128 : xh * 128 + 128, 768:1024] = second.T

        def save(out, c):
            for j in range(2):
                branch[c + j, pl.ds(xb * 2, 2)] = (
                    out[:, j * 128 : j * 128 + 128].astype(BF).reshape(2, 128, 128)
                )

        def one(k, _):
            save(dot_nn(lifted[:, 0:768], rise0[k]), 2 * k)
            return 0

        lax.fori_loop(0, 8, one, 0)
        for k in range(2):
            save(dot_nn(lifted[:, 768:1024], rise1[k]), 16 + 2 * k)

    def channel_map(step):
        for part in range(2):

            def one(k, _):
                rows = pl.ds(k * 16, 16)
                data = jnp.concatenate(
                    [
                        jnp.concatenate(
                            [cells[step, c, part * 2 + xh, rows] for c in range(C)], axis=0
                        )
                        for xh in range(2)
                    ],
                    axis=1,
                )
                out = dot_nn(kron[...], data)
                for o in range(C):
                    for xh in range(2):
                        pre[o, part * 2 + xh, rows] = (
                            out[o * 16 : o * 16 + 16, xh * 128 : xh * 128 + 128] + bias_ref[o]
                        )
                return 0

            lax.fori_loop(0, 8, one, 0)

    def pointwise(step, part, last):
        def one(o, _):
            cot = cots[step, o, :, part * 16 : part * 16 + 16].astype(F32)
            cot = cot.reshape(16, 2, 8, 128)
            outs = []
            for xh in range(2):
                block = part * 2 + xh
                v = pre[o, block] + branch[o, block].astype(F32)
                square = v * v
                half = 0.5 + 0.5 * jnp.tanh(v * (GELU_K + (GELU_K * GELU_C) * square))
                slope = half + (half * (1.0 - half)) * (
                    v * (2.0 * GELU_K + (6.0 * GELU_K * GELU_C) * square)
                )
                cells[step, o, block] = (cot[:, xh].reshape(128, 128) * slope).astype(BF)
                outs.append((v * half).reshape(16, 8, 128))
            if last:
                act[o, :, part * 16 : part * 16 + 16] = jnp.concatenate(outs, axis=1).astype(BF)
            return 0

        lax.fori_loop(0, C, one, 0)

    def all_a_sent(f):
        for xb in range(2):
            wait_all(send_a.at[f, xb, pl.ds(0, GY - 1)], a_send.at[f])

    def all_ba_sent(step):
        for xb in range(2):
            wait_all(back_a.at[step, xb, pl.ds(0, GY - 1)], ba_send.at[step])

    def all_small_sent(sem):
        wait_all(send_b.at[0, pl.ds(0, KY - 1)], sem)

        @pl.when(jnp.logical_not(own))
        def _():
            wait_all(send_b.at[0, KY - 1], sem)

    def all_b_sent(f):
        all_small_sent(b_send.at[f])

    def all_bb_sent(step):
        all_small_sent(bb_send.at[step])

    def mix_and_return(step, f, update):
        rows_inverse(step, mix(f, update))

    def wait_a(f):
        wait_all(recv_a.at[f], a_recv.at[f])

    def wait_b(f):
        wait_all(recv_b.at[f], b_recv.at[f])

    def wait_bb(step):
        wait_all(got_b.at[step], bb_recv.at[step])

    def start():
        copies[0].wait()
        pad_cells(0, 0)
        copies[1].wait()
        copies[2].wait()

    def start_rest():
        copies[12].wait()
        for n in range(3, 12):
            copies[n].start()
        pad_cells(0, 1)

    def unpack_weights():
        def one(i, _):
            for part in range(2):
                weights[part, i] = packed[i, :, part, :]
            return 0

        lax.fori_loop(0, C, one, 0)

    def meet():
        pl.semaphore_wait(barrier, GX + GY - 2)

        def one(d, _):
            pl.semaphore_signal(
                complete, inc=1, device_id=(lax.rem(gx + d, GX), gy), device_id_type=MESH
            )
            return 0

        lax.fori_loop(1, GX, one, 0)

    def meet_all():
        pl.semaphore_wait(complete, GX - 1)

    def load_second():
        copies[4].wait()
        pad_cells(1, 0)
        pad_cells(1, 1)

    def loaded(*numbers):
        for n in numbers:
            copies[n].wait()

    def act_copy():
        return pltpu.make_async_copy(act.at[:, pl.ds(0, 15)], act_hbm, out_sems.at[0])

    def act_start():
        act_copy().start()

    schedule = [
        (start,),
        (deep_half, 0, 0, 0),
        (meet,),
        (send_a_half, 0, 0),
        (start_rest,),
        (deep_half, 0, 0, 1),
        (send_a_half, 0, 1),
        (load_second,),
        (deep_half, 1, 1, 0),
        (deep_half, 1, 1, 1),
        (loaded, 6),
        (unpack_weights,),
        (channel_map, 0),
        (wait_a, 0),
        (loaded, 3),
        (meet_all,),
        (columns, 0),
        (send_a_half, 1, 0),
        (loaded, 5, 7),
        (wait_b, 0),
        (rows_forward, 0),
        (mix_and_return, 0, 0, None),
        (send_a_half, 1, 1),
        (loaded, 8),
        (wait_bb, 0),
        (columns_inverse, 0),
        (wait_a, 1),
        (columns, 1),
        (send_ba_half, 0, 1),
        (loaded, 9, 10, 11),
        (deep_inverse, 0, 0),
        (pointwise, 0, 0, False),
        (deep_half, 2, 0, 0),
        (send_a_half, 2, 0),
        (deep_inverse, 0, 1),
        (pointwise, 0, 1, False),
        (deep_half, 2, 0, 1),
        (send_a_half, 2, 1),
        (channel_map, 1),
        (wait_b, 1),
        (rows_forward, 1),
        (wait_a, 2),
        (columns, 2),
        (wait_b, 2),
        (rows_forward, 2),
        (mix_and_return, 1, 1, (0, 2)),
        (wait_bb, 1),
        (columns_inverse, 1),
        (send_ba_half, 1, 1),
        (deep_inverse, 1, 0),
        (pointwise, 1, 0, True),
        (deep_half, 3, 1, 0),
        (send_a_half, 3, 0),
        (deep_inverse, 1, 1),
        (pointwise, 1, 1, True),
        (deep_half, 3, 1, 1),
        (send_a_half, 3, 1),
        (act_start,),
        (wait_a, 3),
        (columns, 3),
        (wait_b, 3),
        (rows_forward, 3),
        (mix, None, (1, 3)),
    ]
    for stage, *numbers in schedule:
        stage(*numbers)
    trained_out = pltpu.make_async_copy(packed, trained_hbm, out_sems.at[1])
    trained_out.start()

    for f in range(4):
        all_a_sent(f)
        all_b_sent(f)
    for step in range(2):
        all_ba_sent(step)
        all_bb_sent(step)
    act_copy().wait()
    trained_out.wait()


def shards(fields, cotangents, w_point, bias_vector, spectral):
    tables = [jnp.asarray(table) for table in make_tables()]
    anywhere = pl.BlockSpec(memory_space=pl.ANY)
    vmem = pltpu.VMEM
    fields = jnp.transpose(fields, (0, 1, 3, 2, 4))
    cotangents = jnp.transpose(cotangents, (0, 1, 3, 2, 4))
    spectral = jnp.transpose(spectral, (1, 2, 0, 3))
    grid_shape = (C, 16, 32, 128)
    dma = pltpu.SemaphoreType.DMA
    scratch = [
        vmem((2,) + grid_shape, BF),
        vmem((2,) + grid_shape, BF),
        vmem((2, C, 4, 128, 128), BF),
        vmem((C, C, 2, 432), F32),
        vmem((2, C, C, 432), F32),
        vmem(grid_shape, BF),
    ]
    scratch += [vmem(table.shape, BF) for table in tables]
    scratch += [
        vmem((4, 2, GY, 2, 64, 128), BF),
        vmem((4, 2, GY, 2, 64, 128), BF),
        vmem((4, KY, 16, 128), BF),
        vmem((4, 3, 2, GX, 16, 128), BF),
        vmem((2, 3, 16, 16, 128), BF),
        vmem((2, KY, 16, 128), BF),
        vmem((2, 2, GY, 2, 64, 128), BF),
        vmem((2, 2, GY, 2, 64, 128), BF),
        vmem((3, 64, 128), F32),
        vmem((4, 2, C, 432), F32),
        vmem((3, 64, 128), F32),
        vmem((256, 768), BF),
        vmem((256, 1024), BF),
        vmem((C, 4, 128, 128), BF),
        vmem((C, 4, 128, 128), F32),
        vmem((C * 16, C * 16), BF),
        dma((13,)),
        dma((2,)),
        pltpu.SemaphoreType.REGULAR,
        dma((4,)),
        dma((4,)),
        dma((4,)),
        dma((4,)),
        dma((2,)),
        dma((2,)),
        dma((2,)),
        dma((2, 2)),
    ]
    act, trained = pl.pallas_call(
        kernel,
        out_shape=(
            jax.ShapeDtypeStruct((C, 15, 32, 128), BF),
            jax.ShapeDtypeStruct((C, C, 2, 432), F32),
        ),
        in_specs=[
            anywhere,
            anywhere,
            pl.BlockSpec(memory_space=pltpu.VMEM),
            pl.BlockSpec(memory_space=pltpu.SMEM),
            anywhere,
        ]
        + [anywhere] * len(tables),
        out_specs=(anywhere, anywhere),
        scratch_shapes=scratch,
        compiler_params=pltpu.CompilerParams(
            collective_id=0, has_side_effects=True, vmem_limit_bytes=62 * 1024 * 1024
        ),
    )(fields, cotangents, w_point, bias_vector, spectral, *tables)
    return jnp.transpose(act, (0, 2, 1, 3)), jnp.transpose(trained, (2, 0, 1, 3))


def solution(mesh):
    return jax.shard_map(
        shards,
        mesh=mesh,
        in_specs=(
            P(None, None, "gx", "gy", None),
            P(None, None, "gx", "gy", None),
            P(),
            P(),
            P(None, None, None, ("gx", "gy")),
        ),
        out_specs=(P(None, "gx", "gy", None), P(None, None, None, ("gx", "gy"))),
        check_vma=False,
    )
```
